512 devices in a mesh: seq: 16 (over z), vocab: 8 (over y, core), rep: 4 (over x).
Axes of the slice: x: 4, y: 4, z: 16, core: 2. Of those that a mesh axis runs over, the one named last changes fastest.
Arguments:
- hidden: bfloat16 [4, 1024, 4096], P('rep', 'seq', 'vocab'), may hold values from -128 to 128
- head_weight: bfloat16 [4096, 81920], P('vocab', ('seq', 'rep')), may hold values from -0.25 to 0.25
- positions: int32 [4, 64], replicated, may hold values from 0 to 1023, as said below
- counts: int32 [4], replicated, may hold values from 48 to 64, as said below
- targets: int32 [4, 64], replicated, may hold values from 0 to 81919
- seq_cotangent: float32 [4], replicated, may hold values from 50 to 500
Outputs:
- grad_head: bfloat16 [4096, 81920], P('vocab', ('seq', 'rep'))
- grad_hidden: bfloat16 [4, 1024, 4096], P('rep', 'seq', 'vocab')
- seq_losses: float32 [4], replicated
The draws below stay inside these ranges and needn't reach their ends.
Inputs may be any that keep to these rules, and one draw needn't show every extreme that they name: For each sequence the first counts entries are distinct positions in ascending order and the others are 0; at most 12 of a sequence's masked positions lie in one block of 64 consecutive positions, and in every sequence some block holds exactly 12. `counts`: some sequence has exactly 64 masked positions.
All inputs are finite; a program needn't handle non-finite values.
Results may differ from the reference program's by a relative error of at most 0.0047.
Values may be sent and summed in bfloat16 or wider, within the bound.
A program may use at most 64 MiB of HBM per device.

```python
import math
import jax
import jax.numpy as jnp
import numpy as np

D = 4096
MASK_DEV = 4
TOK_DEV = 64
MASK_CAP = 64
LENGTH = 1024
VOCAB = 81920
N_SEQ = 16
N_REP = 4


def masked_layout(key):
    key = jax.random.fold_in(key, 501)
    subkeys = jax.random.split(key, 5)
    slot_cap = 3 * MASK_DEV
    dropped = jax.random.randint(subkeys[0], (N_REP,), 0, MASK_CAP // 4 + 1)
    full_seq = jax.random.randint(subkeys[1], (), 0, N_REP)
    counts = jnp.where(jnp.arange(N_REP) == full_seq, MASK_CAP, MASK_CAP - dropped).astype(jnp.int32)
    hot_block = jax.random.randint(subkeys[2], (N_REP,), 0, N_SEQ)
    rest_rows = counts - slot_cap
    base_rows = rest_rows // (N_SEQ - 1)
    extra_rows = rest_rows % (N_SEQ - 1)
    cold_ranks = jax.vmap(lambda sub_key: jax.random.permutation(sub_key, N_SEQ - 1))(jax.random.split(subkeys[3], N_REP))
    block_ids = jnp.arange(N_SEQ)
    cold_order = block_ids[None, :] - (block_ids[None, :] > hot_block[:, None]).astype(jnp.int32)
    cold_rank = jnp.take_along_axis(cold_ranks, jnp.clip(cold_order, 0, N_SEQ - 2), axis=1)
    per_block = jnp.where(block_ids[None, :] == hot_block[:, None], slot_cap, base_rows[:, None] + (cold_rank < extra_rows[:, None]).astype(jnp.int32))
    rank_table = jax.vmap(lambda sub_key: jax.random.permutation(sub_key, TOK_DEV))(jax.random.split(subkeys[4], N_REP * N_SEQ))
    rank_table = rank_table.reshape(N_REP, N_SEQ, TOK_DEV)
    selected = (rank_table < per_block[:, :, None]).reshape(N_REP, LENGTH)
    slot_of = jnp.cumsum(selected.astype(jnp.int32), axis=1) - 1
    slot_of = jnp.where(selected, slot_of, MASK_CAP)
    positions = jnp.zeros((N_REP, MASK_CAP), jnp.int32)
    positions = positions.at[jnp.arange(N_REP)[:, None], slot_of].set(jnp.broadcast_to(jnp.arange(LENGTH, dtype=jnp.int32)[None, :], (N_REP, LENGTH)), mode='drop')
    return (positions, counts)


def head_matrix(key):
    head_key = jax.random.fold_in(key, 601)
    values = jax.random.normal(head_key, (D, VOCAB), jnp.float32) * (3.0 / math.sqrt(D))
    return jnp.clip(values, -0.25, 0.25)


def draw_positions(key, part):
    return masked_layout(key)[0]


def draw_counts(key, part):
    return masked_layout(key)[1]


def draw_head_weight(key, part):
    return head_matrix(key).astype(jnp.bfloat16)


def draw_hidden(key, part):
    own_key = jax.random.fold_in(key, 701)
    states = jnp.clip(jax.random.normal(own_key, (N_REP, LENGTH, D), jnp.float32), -6.0, 6.0)
    return states.astype(jnp.bfloat16)


def set_ends(entries, stream_key, least, top_value):
    place = [jax.random.randint(jax.random.fold_in(stream_key, axis), (), 0, length) for axis, length in enumerate(entries.shape)]
    longest = entries.shape.index(max(entries.shape))
    beside = place[:longest] + [(place[longest] + 1) % entries.shape[longest]] + place[longest + 1:]
    return entries.at[tuple(place)].set(least).at[tuple(beside)].set(top_value)


def wide_ids(rng, extent, count, slope):
    portions = [min(1 << octave, count + 1 - (1 << octave)) * (1 << 20) // math.isqrt((1 << octave) ** slope) + 1 for octave in range((count + 1).bit_length()) if 1 << octave <= count]
    deviation = 1 + sum(portions) // (1 << 30)
    listing = np.cumsum(np.array([max(1, weight // deviation) for weight in portions]))
    pick = jax.random.randint(jax.random.fold_in(rng, 1), extent, 0, int(listing[len(portions) - 1]))
    start = jnp.left_shift(1, jnp.searchsorted(jnp.asarray(listing, jnp.int32), pick, side="right").astype(jnp.int32))
    standing = start - 1 + jax.random.randint(jax.random.fold_in(rng, 4), extent, 0, 1 << 30) % jnp.minimum(start, count + 1 - start)
    return jax.random.permutation(jax.random.fold_in(rng, 2), count)[standing].astype(jnp.int32)


def setup_inputs(seed: int = 0) -> dict:
    key_of = jax.random.split(jax.random.key(seed), 7)
    return {
        "hidden": draw_hidden(jax.random.fold_in(key_of[6], 71), 0),
        "head_weight": draw_head_weight(jax.random.fold_in(key_of[6], 71), 0),
        "positions": draw_positions(jax.random.fold_in(key_of[6], 71), 0),
        "counts": draw_counts(jax.random.fold_in(key_of[6], 71), 0),
        "targets": set_ends(wide_ids(key_of[4], (N_REP, MASK_CAP), VOCAB, 2), jax.random.fold_in(key_of[4], 3), 0, VOCAB - 1).astype(jnp.int32),
        "seq_cotangent": jnp.clip(jnp.exp(jax.random.uniform(key_of[5], (N_REP,), jnp.float32, math.log(50.0), math.log(500.0))), 50.0, 500.0),
    }


def take_rows(sequence, places):
    return jnp.take(sequence, places, axis=0)


def put_rows(updates, places):
    return jnp.zeros((LENGTH, D), jnp.bfloat16).at[places].add(updates)


def reference(hidden, head_weight, positions, counts, targets, seq_cotangent):
    total_rows = N_REP * MASK_CAP
    picked = jax.vmap(take_rows)(hidden, positions).reshape(total_rows, D)
    row_live = (jnp.arange(MASK_CAP, dtype=jnp.int32)[None, :] < counts[:, None]).reshape(total_rows)
    count_rows = jnp.repeat(counts, MASK_CAP).astype(jnp.float32)
    row_weight = jnp.where(row_live, jnp.repeat(seq_cotangent, MASK_CAP) / count_rows, 0.0)
    logits = jnp.dot(picked, head_weight, preferred_element_type=jnp.float32)
    row_max = jnp.max(logits, axis=1)
    exponent = jnp.exp(logits - row_max[:, None])
    exp_total = jnp.sum(exponent, axis=1)
    is_target = jnp.arange(VOCAB, dtype=jnp.int32)[None, :] == targets.reshape(total_rows)[:, None]
    target_logit = jnp.sum(jnp.where(is_target, logits, 0.0), axis=1)
    row_loss = jnp.log(exp_total) + row_max - target_logit
    seq_losses = jnp.sum(jnp.where(row_live, row_loss / count_rows, 0.0).reshape(N_REP, MASK_CAP), axis=1)
    grad_logits = (row_weight[:, None] * (exponent / exp_total[:, None] - is_target.astype(jnp.float32))).astype(jnp.bfloat16)
    grad_head = jnp.dot(picked.T, grad_logits, preferred_element_type=jnp.float32).astype(jnp.bfloat16)
    grad_rows = jnp.dot(grad_logits, head_weight.T, preferred_element_type=jnp.float32).astype(jnp.bfloat16)
    grad_hidden = jax.vmap(put_rows)(grad_rows.reshape(N_REP, MASK_CAP, D), positions)
    return grad_head, grad_hidden, seq_losses
```

```python
import jax
import jax.numpy as jnp
from jax import lax
from jax.experimental import pallas as pl
from jax.experimental.pallas import tpu as pltpu
from jax.sharding import PartitionSpec as P

MESH = pl.DeviceIdType.MESH
F32 = jnp.float32
BF16 = jnp.bfloat16

SEQ = 16
REP = 4
SLOTS = 64
TOK = 64
FEAT = 512
COLS = 1280
FOLD = 16
CHUNK = 32
HALF = 16
WIDE = FEAT // 2

PICK_CLASS = 0
PICK_NEAR = 6
PICK_REP = 14
LOGIT_CORE = 20
LOGIT_Y = 24
STAT_SEQ = 30
STAT_REP = 45
GRAD_Y = 48
GRAD_CORE = 54
SCALE = 58
ROW_REP = 65
ROW_NEAR = 71
ROW_CLASS = 79
MESSAGES = 85


def iota(shape, dim):
    return lax.broadcasted_iota(jnp.int32, shape, dim)


def to_column(row, rows, shift=0):
    shape = (rows, row.shape[1])
    at = iota(shape, 1) == iota(shape, 0) + shift
    return jnp.sum(jnp.where(at, row, 0.0), axis=1, keepdims=True)


def to_row(column, shift):
    shape = (CHUNK, 128)
    at = iota(shape, 1) == iota(shape, 0) + shift
    return jnp.sum(jnp.where(at, column, 0.0), axis=0, keepdims=True)


def turn(row, shift):
    return pltpu.roll(row, 128 - shift, 1)


def between(row, first):
    lane = iota((1, 128), 1)
    return jnp.where((lane >= first) & (lane < first + CHUNK), row, 0.0)


def merge_stats(ref, parts):
    rows = [ref[i] for i in range(parts)]
    row_max = rows[0]
    for row in rows[1:]:
        row_max = jnp.maximum(row_max, row)
    row_sum = jnp.zeros((1, 128), F32)
    row_target = jnp.zeros((1, 128), F32)
    for row in rows:
        row_sum = row_sum + turn(row, CHUNK) * jnp.exp(row - row_max)
        row_target = row_target + row
    return row_max, row_sum, turn(row_target, 2 * CHUNK)


def pack_stats(row_max, row_sum, row_target):
    return (
        between(row_max, 0)
        + between(turn(row_sum, 128 - CHUNK), CHUNK)
        + between(turn(row_target, 128 - 2 * CHUNK), 2 * CHUNK)
    )


def fold_rows(rows):
    return (rows[0:16] + rows[16:32]) + (rows[32:48] + rows[48:64])


def unfold_rows(rows):
    return jnp.concatenate([rows, rows, rows, rows], axis=0)


def kernel(
    counts_hbm, cot_hbm, positions_hbm, targets_hbm, hidden_hbm, weight_hbm,
    head_hbm, grad_ref, losses_ref,
    counts_ref, cot_ref, positions_ref, targets_ref, hidden_ref, weight, pick_class, pick_own, pick_near, picked, picked_t, target_cols, target_rows,
    core_out, core_in, part, y_fwd, y_sum, y_direct, y_acc, logits_ref,
    stat_seq, stat_rep, scales, exps, grads,
    row_sums, row_out, row_in, near_out, near_in, class_out, class_in, head_out,
    send_sem, recv_sem, load_sem, head_sem,
):
    z = lax.axis_index("seq")
    v = lax.axis_index("vocab")
    x = lax.axis_index("rep")
    y = lax.div(v, 2)
    c = lax.rem(v, 2)
    cls = lax.rem(z, 4)
    member = lax.div(z, 4)

    def at_z(shift):
        return {"seq": lax.rem(z + shift + SEQ, SEQ)}

    def at_x(shift):
        return {"rep": lax.rem(x + shift, REP)}

    def y_plus(shift):
        return lax.rem(y + shift, 4)

    def at_y(shift):
        return {"vocab": y_plus(shift) * 2 + c}

    def load(number, src, dst):
        copy = pltpu.make_async_copy(src, dst, load_sem.at[number])
        copy.start()
        return copy

    loads = [
        load(0, positions_hbm, positions_ref),
        load(1, counts_hbm, counts_ref),
        load(2, hidden_hbm, hidden_ref),
        load(3, cot_hbm, cot_ref),
        load(4, targets_hbm, targets_ref),
        load(5, weight_hbm, weight),
    ]

    sibling = {"vocab": y * 2 + 1 - c}

    started = []

    def send(number, src, dst, device):
        copy = pltpu.make_async_remote_copy(
            src_ref=src,
            dst_ref=dst,
            send_sem=send_sem.at[number],
            recv_sem=recv_sem.at[number],
            device_id=device,
            device_id_type=MESH,
        )
        copy.start()
        started.append(copy)
        return copy

    barrier = pltpu.get_barrier_semaphore()
    friends = [at_z(s) for s in range(1, SEQ)] + [at_x(s) for s in (1, 2, 3)]
    friends += [{"vocab": lax.rem(v + s, 8)} for s in range(1, 8)]
    for friend in friends:
        pl.semaphore_signal(barrier, inc=1, device_id=friend, device_id_type=MESH)

    loads[0].wait()
    loads[1].wait()
    all_positions = positions_ref[...].astype(F32)
    position_row = jnp.sum(
        jnp.where(iota((REP, SLOTS), 0) == x, all_positions, 0.0), axis=0, keepdims=True
    )
    count = counts_ref[x]
    position_col = to_column(position_row, SLOTS).astype(jnp.int32)
    live_col = iota((SLOTS, 1), 0) < count
    owner_col = jnp.where(live_col, lax.div(position_col, TOK), -1)
    pick_at = (iota((SLOTS, TOK), 1) + z * TOK == position_col) & (iota((SLOTS, TOK), 0) < count)
    put_at = (iota((TOK, SLOTS), 0) + z * TOK == position_row.astype(jnp.int32)) & (
        iota((TOK, SLOTS), 1) < count
    )

    loads[2].wait()
    own_rows = jnp.dot(
        jnp.where(pick_at, 1.0, 0.0).astype(BF16), hidden_ref[0], preferred_element_type=F32
    )
    folded = fold_rows(own_rows).astype(BF16)
    for h in range(2):
        pick_class[h, member] = folded[:, h * WIDE : (h + 1) * WIDE]

    pl.semaphore_wait(barrier, len(friends))

    class_copies = [
        [
            send(
                PICK_CLASS + 3 * h + d - 1, pick_class.at[h, member], pick_class.at[h, member],
                at_z(4 * d),
            )
            for d in (1, 2, 3)
        ]
        for h in range(2)
    ]

    def send_near(number, src, dst):
        low, high = pl.ds(0, 32), pl.ds(32, 32)
        return [
            send(number, src, dst.at[0], at_z(1)),
            send(number + 1, src, dst.at[1], at_z(-1)),
            send(number + 2, src.at[low], dst.at[2, low], at_z(2)),
            send(number + 3, src.at[high], dst.at[2, high], at_z(-2)),
        ]

    loads[4].wait()
    all_targets = targets_ref[...].astype(F32)
    column = iota((CHUNK, COLS), 1) + (z * REP + x) * COLS
    for i in range(8):
        target_cols[i] = to_column(
            all_targets[i // 2 : i // 2 + 1], CHUNK, CHUNK * (i % 2)
        ).astype(jnp.int32)

    def head_at_targets(h):
        hot = [jnp.where(column == target_cols[i], 1.0, 0.0).astype(BF16) for i in range(8)]
        target_rows[h] = lax.dot_general(
            jnp.concatenate(hot, axis=0), weight[h * WIDE : (h + 1) * WIDE],
            (((1,), (1,)), ((), ())), preferred_element_type=F32,
        ).reshape(8, CHUNK, WIDE)

    loads[5].wait()
    head_at_targets(0)

    totals = []
    near_copies = []
    for h in range(2):
        for copy in class_copies[h]:
            copy.wait_recv()
        total = jnp.zeros((SLOTS, WIDE), F32)
        for j in range(4):
            block = unfold_rows(pick_class[h, j].astype(F32))
            total = total + jnp.where(owner_col == cls + 4 * j, block, 0.0)
        pick_own[h] = total.astype(BF16)
        near_copies.append(send_near(PICK_NEAR + 4 * h, pick_own.at[h], pick_near.at[h]))
        totals.append(total)
    head_at_targets(1)
    rep_copies = []
    for h in range(2):
        for copy in near_copies[h]:
            copy.wait_recv()
        total = totals[h]
        for i in range(3):
            total = total + pick_near[h, i].astype(F32)
        picked[h, x] = total.astype(BF16)
        rep_copies.append([
            send(PICK_REP + 3 * h + d - 1, picked.at[h, x], picked.at[h, x], at_x(d))
            for d in (1, 2, 3)
        ])

    def partial_logits(h, core):
        rows = picked[h, pl.ds(2 * core, 2)].reshape(2 * SLOTS, WIDE)
        return jnp.dot(
            rows, weight[h * WIDE : (h + 1) * WIDE], preferred_element_type=F32
        ).reshape(4, CHUNK, COLS)

    for copy in rep_copies[0]:
        copy.wait_recv()
    core_out[...] = partial_logits(0, 1 - c)
    part[...] = partial_logits(0, c)
    for copy in rep_copies[1]:
        copy.wait_recv()
    core_out[...] = core_out[...] + partial_logits(1, 1 - c)
    order = (2, 1, 3, 0)
    core_copies = [
        send(LOGIT_CORE + i, core_out.at[y_plus(s)], core_in.at[y_plus(s)], sibling)
        for i, s in enumerate(order)
    ]
    part[...] = part[...] + partial_logits(1, c)

    low, high = pl.ds(0, HALF), pl.ds(HALF, HALF)
    y_copies = []
    for i, s in enumerate(order):
        core_copies[i].wait_recv()
        at = y_plus(s)
        part[at] = part[at] + core_in[at]
        if s == 2:
            y_copies.append(send(LOGIT_Y, part.at[at, low], y_fwd.at[0], at_y(1)))
            y_copies.append(send(LOGIT_Y + 1, part.at[at, high], y_fwd.at[1], at_y(3)))
        if s == 1:
            y_copies.append(send(LOGIT_Y + 2, part.at[at, high], y_direct.at[1], at_y(1)))
        if s == 3:
            y_copies.append(send(LOGIT_Y + 3, part.at[at, low], y_direct.at[0], at_y(3)))
    for h in range(2):
        picked_t[h * WIDE : (h + 1) * WIDE] = picked[h].reshape(REP * SLOTS, WIDE).T
    y_copies[0].wait_recv()
    y_sum[0] = y_fwd[0] + part[y_plus(1), 0:HALF]
    y_copies.append(send(LOGIT_Y + 4, y_sum.at[0], y_acc.at[0], at_y(1)))
    y_copies[1].wait_recv()
    y_sum[1] = y_fwd[1] + part[y_plus(3), HALF:CHUNK]
    y_copies.append(send(LOGIT_Y + 5, y_sum.at[1], y_acc.at[1], at_y(3)))
    for copy in y_copies[2:]:
        copy.wait_recv()
    logits_ref[0:HALF] = part[y, 0:HALF] + (y_direct[0] + y_acc[0])
    logits_ref[HALF:CHUNK] = part[y, HALF:CHUNK] + (y_direct[1] + y_acc[1])

    loads[3].wait()
    my_seq = 2 * c + lax.div(y, 2)
    first_slot = lax.rem(y, 2) * CHUNK
    my_count = counts_ref[my_seq]
    my_cot = cot_ref[my_seq]
    my_chunk = 4 * c + y
    is_target = column == target_cols[my_chunk]
    logits = logits_ref[...]
    local_max = jnp.max(logits, axis=1, keepdims=True)
    exponent = jnp.exp(logits - local_max)

    exps[my_chunk] = jnp.where(is_target, 0.0, exponent).astype(BF16)
    mine = exps.at[my_chunk]
    before = exps.at[4 * c + y_plus(3)]
    after = exps.at[4 * c + y_plus(1)]
    up_low = send(GRAD_Y, mine.at[low], mine.at[low], at_y(1))
    down_high = send(GRAD_Y + 1, mine.at[high], mine.at[high], at_y(3))
    up_high = send(GRAD_Y + 2, mine.at[high], mine.at[high], at_y(1))
    down_low = send(GRAD_Y + 3, mine.at[low], mine.at[low], at_y(3))
    core_copies = [send(GRAD_CORE, mine, mine, sibling)]

    local_sum = jnp.sum(exponent, axis=1, keepdims=True)
    local_target = jnp.sum(jnp.where(is_target, logits, 0.0), axis=1, keepdims=True)
    max_row = to_row(local_max, 0)
    stat_seq[z] = max_row + to_row(local_sum, CHUNK) + to_row(local_target, 2 * CHUNK)
    seq_copies = [
        send(STAT_SEQ + d - 1, stat_seq.at[z], stat_seq.at[z], at_z(d)) for d in range(1, SEQ)
    ]

    up_low.wait_recv()
    up_again = send(GRAD_Y + 4, before.at[low], before.at[low], at_y(1))
    down_high.wait_recv()
    down_again = send(GRAD_Y + 5, after.at[high], after.at[high], at_y(3))
    up_high.wait_recv()
    core_copies.append(send(GRAD_CORE + 1, before, before, sibling))
    down_low.wait_recv()
    core_copies.append(send(GRAD_CORE + 2, after, after, sibling))

    for copy in seq_copies:
        copy.wait_recv()
    stat_rep[x] = pack_stats(*merge_stats(stat_seq, SEQ))
    copies = [send(STAT_REP + d - 1, stat_rep.at[x], stat_rep.at[x], at_x(d)) for d in (1, 2, 3)]
    up_again.wait_recv()
    down_again.wait_recv()
    across = exps.at[4 * c + y_plus(2)]
    core_copies.append(send(GRAD_CORE + 3, across, across, sibling))
    for copy in copies:
        copy.wait_recv()
    total_max, total_sum, target_logit = merge_stats(stat_rep, REP)

    lane = iota((1, 128), 1)
    live = (lane < CHUNK) & (lane + first_slot < my_count)
    count_row = jnp.full((1, 128), my_count.astype(F32), F32)
    weight_row = jnp.where(live, jnp.full((1, 128), my_cot, F32) / count_row, 0.0)
    factor = jnp.where(live, weight_row * (jnp.exp(max_row - total_max) / total_sum), 0.0)
    at_target = jnp.where(
        live, weight_row * (jnp.exp(target_logit - total_max) / total_sum - 1.0), 0.0
    )
    row_loss = jnp.where(live, (jnp.log(total_sum) + total_max - target_logit) / count_row, 0.0)
    scales[my_chunk] = pack_stats(factor, at_target, row_loss)
    scale_copies = [
        send(SCALE + d - 1, scales.at[my_chunk], scales.at[my_chunk], {"vocab": lax.rem(v + d, 8)})
        for d in range(1, 8)
    ]

    def head_times(core):
        block = exps[pl.ds(4 * core, 4)].reshape(4 * CHUNK, COLS)
        for h in range(2):
            row_sums[h, pl.ds(4 * core, 4)] = lax.dot_general(
                block, weight[h * WIDE : (h + 1) * WIDE], (((1,), (1,)), ((), ())),
                preferred_element_type=F32,
            ).reshape(4, CHUNK, WIDE)

    head_times(c)
    for copy in core_copies:
        copy.wait_recv()
    head_times(1 - c)
    for copy in scale_copies:
        copy.wait_recv()
    factors = [to_column(scales[i], CHUNK) for i in range(8)]
    at_targets = [
        to_column(scales[i], CHUNK, CHUNK).astype(BF16).astype(F32) for i in range(8)
    ]
    rep_copies = []
    for h in range(2):
        for i in range(8):
            rows = factors[i] * row_sums[h, i] + at_targets[i] * target_rows[h, i]
            row_sums[h, i] = rows
            row_out[h, i // 2, CHUNK * (i % 2) : CHUNK * (i % 2 + 1)] = rows.astype(BF16)
        rep_copies.append([
            send(
                ROW_REP + 3 * h + d - 1, row_out.at[h, lax.rem(x + d, REP)], row_in.at[h, d - 1],
                at_x(d),
            )
            for d in (1, 2, 3)
        ])
    for i in range(8):
        values = exps[i].astype(F32) * factors[i]
        grads[i] = jnp.where(column == target_cols[i], at_targets[i], values).astype(BF16)
    owns = [row_sums[h, pl.ds(2 * x, 2)].reshape(SLOTS, WIDE) for h in range(2)]

    def head_part(i):
        columns = pl.ds(i * 256, 256)
        tile = jnp.dot(
            picked_t[...], grads[:, :, columns].reshape(REP * SLOTS, 256), preferred_element_type=F32
        )
        head_out[:, columns] = tile.astype(BF16)
        copy = pltpu.make_async_copy(
            head_out.at[:, columns], head_hbm.at[:, columns], head_sem.at[i]
        )
        copy.start()
        return copy

    near_copies = []
    for h in range(2):
        for copy in rep_copies[h]:
            copy.wait_recv()
        for i in range(3):
            owns[h] = owns[h] + row_in[h, i].astype(F32)
        near_out[h] = owns[h].astype(BF16)
        near_copies.append(send_near(ROW_NEAR + 4 * h, near_out.at[h], near_in.at[h]))
    head_copies = [head_part(0), head_part(1), head_part(2)]
    mine_rows = []
    class_copies = []
    for h in range(2):
        for copy in near_copies[h]:
            copy.wait_recv()
        own = owns[h]
        for i in range(3):
            own = own + near_in[h, i].astype(F32)
        mine = jnp.zeros((FOLD, WIDE), F32)
        for j in range(4):
            block = fold_rows(jnp.where(owner_col == cls + 4 * j, own, 0.0))
            class_out[h, j] = block.astype(BF16)
            mine = jnp.where(member == j, block, mine)
        mine_rows.append(mine)
        class_copies.append([
            send(
                ROW_CLASS + 3 * h + d - 1, class_out.at[h, lax.rem(member + d, 4)],
                class_in.at[h, d - 1], at_z(4 * d),
            )
            for d in (1, 2, 3)
        ])
    head_copies += [head_part(3), head_part(4)]
    for q in range(REP):
        losses_ref[q] = jnp.sum(between(scales[2 * q] + scales[2 * q + 1], 2 * CHUNK))
    put = jnp.where(put_at, 1.0, 0.0).astype(BF16)
    for h in range(2):
        for copy in class_copies[h]:
            copy.wait_recv()
        mine = mine_rows[h]
        for i in range(3):
            mine = mine + class_in[h, i].astype(F32)
        final = unfold_rows(mine.astype(BF16).astype(F32))
        final = jnp.where(owner_col == z, final, 0.0).astype(BF16)
        grad_ref[0, :, h * WIDE : (h + 1) * WIDE] = jnp.dot(
            put, final, preferred_element_type=F32
        ).astype(BF16)

    for copy in started:
        copy.wait_send()
    for copy in head_copies:
        copy.wait()


def hand_over(
    head_in, hidden_in, losses_in, head_ref, hidden_ref, losses_ref,
    head, hidden, losses, in_sem, out_sem,
):
    rows = FEAT // 4
    moves = [(hidden_in, hidden, hidden_ref), (losses_in, losses, losses_ref)]
    for i in range(4):
        at = pl.ds(i * rows, rows)
        moves.append((head_in.at[at], head.at[at], head_ref.at[at]))
    loads = [pltpu.make_async_copy(m[0], m[1], in_sem.at[i]) for i, m in enumerate(moves)]
    stores = [pltpu.make_async_copy(m[1], m[2], out_sem.at[i]) for i, m in enumerate(moves)]
    for load in loads:
        load.start()
    for load, store in zip(loads, stores):
        load.wait()
        store.start()
    for store in stores:
        store.wait()


def shards(hidden, head_weight, positions, counts, targets, seq_cotangent):
    vmem = pl.BlockSpec(memory_space=pltpu.VMEM)
    smem = pl.BlockSpec(memory_space=pltpu.SMEM)
    hbm = pl.BlockSpec(memory_space=pltpu.HBM)
    shapes = (
        jax.ShapeDtypeStruct((FEAT, COLS), BF16),
        jax.ShapeDtypeStruct((1, TOK, FEAT), BF16),
        jax.ShapeDtypeStruct((REP,), F32),
    )
    limit = 60 * 1024 * 1024
    results = pl.pallas_call(
        kernel,
        out_shape=shapes,
        in_specs=[hbm] * 6,
        out_specs=(hbm, vmem, smem),
        scratch_shapes=[
            pltpu.SMEM((REP,), jnp.int32),
            pltpu.SMEM((REP,), F32),
            pltpu.VMEM((REP, SLOTS), jnp.int32),
            pltpu.VMEM((REP, SLOTS), jnp.int32),
            pltpu.VMEM((1, TOK, FEAT), BF16),
            pltpu.VMEM((FEAT, COLS), BF16),
            pltpu.VMEM((2, 4, FOLD, WIDE), BF16),
            pltpu.VMEM((2, SLOTS, WIDE), BF16),
            pltpu.VMEM((2, 3, SLOTS, WIDE), BF16),
            pltpu.VMEM((2, REP, SLOTS, WIDE), BF16),
            pltpu.VMEM((FEAT, REP * SLOTS), BF16),
            pltpu.VMEM((8, CHUNK, 1), jnp.int32),
            pltpu.VMEM((2, 8, CHUNK, WIDE), F32),
            pltpu.VMEM((4, CHUNK, COLS), F32),
            pltpu.VMEM((4, CHUNK, COLS), F32),
            pltpu.VMEM((4, CHUNK, COLS), F32),
            pltpu.VMEM((2, HALF, COLS), F32),
            pltpu.VMEM((2, HALF, COLS), F32),
            pltpu.VMEM((2, HALF, COLS), F32),
            pltpu.VMEM((2, HALF, COLS), F32),
            pltpu.VMEM((CHUNK, COLS), F32),
            pltpu.VMEM((SEQ, 1, 128), F32),
            pltpu.VMEM((REP, 1, 128), F32),
            pltpu.VMEM((2 * REP, 1, 128), F32),
            pltpu.VMEM((2 * REP, CHUNK, COLS), BF16),
            pltpu.VMEM((2 * REP, CHUNK, COLS), BF16),
            pltpu.VMEM((2, 8, CHUNK, WIDE), F32),
            pltpu.VMEM((2, REP, SLOTS, WIDE), BF16),
            pltpu.VMEM((2, 3, SLOTS, WIDE), BF16),
            pltpu.VMEM((2, SLOTS, WIDE), BF16),
            pltpu.VMEM((2, 3, SLOTS, WIDE), BF16),
            pltpu.VMEM((2, 4, FOLD, WIDE), BF16),
            pltpu.VMEM((2, 3, FOLD, WIDE), BF16),
            pltpu.VMEM((FEAT, COLS), BF16),
            pltpu.SemaphoreType.DMA((MESSAGES,)),
            pltpu.SemaphoreType.DMA((MESSAGES,)),
            pltpu.SemaphoreType.DMA((6,)),
            pltpu.SemaphoreType.DMA((5,)),
        ],
        compiler_params=pltpu.CompilerParams(
            collective_id=0, has_side_effects=True, vmem_limit_bytes=limit
        ),
        cost_estimate=pl.CostEstimate(
            flops=6 * 256 * FEAT * COLS, bytes_accessed=4 * FEAT * COLS, transcendentals=64 * COLS
        ),
    )(counts, seq_cotangent, positions, targets, hidden, head_weight)
    return pl.pallas_call(
        hand_over,
        out_shape=shapes,
        in_specs=[hbm] * 3,
        out_specs=(hbm,) * 3,
        scratch_shapes=[
            pltpu.VMEM((FEAT, COLS), BF16),
            pltpu.VMEM((1, TOK, FEAT), BF16),
            pltpu.SMEM((REP,), F32),
            pltpu.SemaphoreType.DMA((6,)),
            pltpu.SemaphoreType.DMA((6,)),
        ],
        compiler_params=pltpu.CompilerParams(vmem_limit_bytes=limit),
    )(*results)


def solution(mesh):
    return jax.shard_map(
        shards,
        mesh=mesh,
        in_specs=(P("rep", "seq", "vocab"), P("vocab", ("seq", "rep")), P(), P(), P(), P()),
        out_specs=(P("vocab", ("seq", "rep")), P("rep", "seq", "vocab"), P()),
        check_vma=False,
    )
```

```python
import jax
import jax.numpy as jnp
from jax import lax
from jax.experimental import pallas as pl
from jax.experimental.pallas import tpu as pltpu
from jax.sharding import PartitionSpec as P

MESH = pl.DeviceIdType.MESH
F32 = jnp.float32
BF16 = jnp.bfloat16

SEQ = 16
REP = 4
SLOTS = 64
TOK = 64
FEAT = 512
COLS = 1280
FOLD = 16
CHUNK = 32
HALF = 16
WIDE = FEAT // 2
SPAN = COLS // 2

PICK_CLASS = 0
PICK_NEAR = 6
PICK_REP = 14
LOGIT_CORE = 20
LOGIT_Y = 28
STAT_SEQ = 40
STAT_REP = 55
GRAD_Y = 58
GRAD_CORE = 64
SCALE = 68
ROW_REP = 75
ROW_NEAR = 81
ROW_CLASS = 89
MESSAGES = 95


def iota(shape, dim):
    return lax.broadcasted_iota(jnp.int32, shape, dim)


def to_column(row, rows, shift=0):
    shape = (rows, row.shape[1])
    at = iota(shape, 1) == iota(shape, 0) + shift
    return jnp.sum(jnp.where(at, row, 0.0), axis=1, keepdims=True)


def to_row(column, shift):
    shape = (CHUNK, 128)
    at = iota(shape, 1) == iota(shape, 0) + shift
    return jnp.sum(jnp.where(at, column, 0.0), axis=0, keepdims=True)


def turn(row, shift):
    return pltpu.roll(row, 128 - shift, 1)


def between(row, first):
    lane = iota((1, 128), 1)
    return jnp.where((lane >= first) & (lane < first + CHUNK), row, 0.0)


def merge_stats(ref, parts):
    rows = [ref[i] for i in range(parts)]
    row_max = rows[0]
    for row in rows[1:]:
        row_max = jnp.maximum(row_max, row)
    row_sum = jnp.zeros((1, 128), F32)
    row_target = jnp.zeros((1, 128), F32)
    for row in rows:
        row_sum = row_sum + turn(row, CHUNK) * jnp.exp(row - row_max)
        row_target = row_target + row
    return row_max, row_sum, turn(row_target, 2 * CHUNK)


def pack_stats(row_max, row_sum, row_target):
    return (
        between(row_max, 0)
        + between(turn(row_sum, 128 - CHUNK), CHUNK)
        + between(turn(row_target, 128 - 2 * CHUNK), 2 * CHUNK)
    )


def fold_rows(rows):
    return (rows[0:16] + rows[16:32]) + (rows[32:48] + rows[48:64])


def unfold_rows(rows):
    return jnp.concatenate([rows, rows, rows, rows], axis=0)


def kernel(
    counts_hbm, cot_hbm, positions_hbm, targets_hbm, hidden_hbm, weight_hbm,
    head_hbm, grad_ref, losses_ref,
    counts_ref, cot_ref, positions_ref, targets_ref, hidden_ref, weight, pick_class, pick_own, pick_near, picked, picked_t, target_cols, target_rows,
    core_out, core_in, part, y_fwd, y_sum, y_direct, y_acc, logits_ref,
    stat_seq, stat_rep, scales, exps, grads,
    row_sums, row_out, row_in, near_out, near_in, class_out, class_in, head_out,
    send_sem, recv_sem, load_sem, head_sem,
):
    z = lax.axis_index("seq")
    v = lax.axis_index("vocab")
    x = lax.axis_index("rep")
    y = lax.div(v, 2)
    c = lax.rem(v, 2)
    cls = lax.rem(z, 4)
    member = lax.div(z, 4)

    def at_z(shift):
        return {"seq": lax.rem(z + shift + SEQ, SEQ)}

    def at_x(shift):
        return {"rep": lax.rem(x + shift, REP)}

    def y_plus(shift):
        return lax.rem(y + shift, 4)

    def at_y(shift):
        return {"vocab": y_plus(shift) * 2 + c}

    def load(number, src, dst):
        copy = pltpu.make_async_copy(src, dst, load_sem.at[number])
        copy.start()
        return copy

    loads = [
        load(0, positions_hbm, positions_ref),
        load(1, counts_hbm, counts_ref),
        load(2, hidden_hbm, hidden_ref),
        load(3, cot_hbm, cot_ref),
        load(4, targets_hbm, targets_ref),
        load(5, weight_hbm, weight),
    ]

    sibling = {"vocab": y * 2 + 1 - c}

    started = []

    def send(number, src, dst, device):
        copy = pltpu.make_async_remote_copy(
            src_ref=src,
            dst_ref=dst,
            send_sem=send_sem.at[number],
            recv_sem=recv_sem.at[number],
            device_id=device,
            device_id_type=MESH,
        )
        copy.start()
        started.append(copy)
        return copy

    barrier = pltpu.get_barrier_semaphore()
    friends = [at_z(s) for s in range(1, SEQ)] + [at_x(s) for s in (1, 2, 3)]
    friends += [{"vocab": lax.rem(v + s, 8)} for s in range(1, 8)]
    for friend in friends:
        pl.semaphore_signal(barrier, inc=1, device_id=friend, device_id_type=MESH)

    loads[0].wait()
    loads[1].wait()
    all_positions = positions_ref[...].astype(F32)
    position_row = jnp.sum(
        jnp.where(iota((REP, SLOTS), 0) == x, all_positions, 0.0), axis=0, keepdims=True
    )
    count = counts_ref[x]
    position_col = to_column(position_row, SLOTS).astype(jnp.int32)
    live_col = iota((SLOTS, 1), 0) < count
    owner_col = jnp.where(live_col, lax.div(position_col, TOK), -1)
    pick_at = (iota((SLOTS, TOK), 1) + z * TOK == position_col) & (iota((SLOTS, TOK), 0) < count)
    put_at = (iota((TOK, SLOTS), 0) + z * TOK == position_row.astype(jnp.int32)) & (
        iota((TOK, SLOTS), 1) < count
    )

    loads[2].wait()
    own_rows = jnp.dot(
        jnp.where(pick_at, 1.0, 0.0).astype(BF16), hidden_ref[0], preferred_element_type=F32
    )
    folded = fold_rows(own_rows).astype(BF16)
    for h in range(2):
        pick_class[h, member] = folded[:, h * WIDE : (h + 1) * WIDE]

    pl.semaphore_wait(barrier, len(friends))

    class_copies = [
        [
            send(
                PICK_CLASS + 3 * h + d - 1, pick_class.at[h, member], pick_class.at[h, member],
                at_z(4 * d),
            )
            for d in (1, 2, 3)
        ]
        for h in range(2)
    ]

    def send_near(number, src, dst):
        low, high = pl.ds(0, 32), pl.ds(32, 32)
        return [
            send(number, src, dst.at[0], at_z(1)),
            send(number + 1, src, dst.at[1], at_z(-1)),
            send(number + 2, src.at[low], dst.at[2, low], at_z(2)),
            send(number + 3, src.at[high], dst.at[2, high], at_z(-2)),
        ]

    loads[4].wait()
    all_targets = targets_ref[...].astype(F32)
    column = iota((CHUNK, COLS), 1) + (z * REP + x) * COLS
    for i in range(8):
        target_cols[i] = to_column(
            all_targets[i // 2 : i // 2 + 1], CHUNK, CHUNK * (i % 2)
        ).astype(jnp.int32)

    def head_at_targets(h):
        hot = [jnp.where(column == target_cols[i], 1.0, 0.0).astype(BF16) for i in range(8)]
        target_rows[h] = lax.dot_general(
            jnp.concatenate(hot, axis=0), weight[h * WIDE : (h + 1) * WIDE],
            (((1,), (1,)), ((), ())), preferred_element_type=F32,
        ).reshape(8, CHUNK, WIDE)

    loads[5].wait()
    head_at_targets(0)

    totals = []
    near_copies = []
    for h in range(2):
        for copy in class_copies[h]:
            copy.wait_recv()
        total = jnp.zeros((SLOTS, WIDE), F32)
        for j in range(4):
            block = unfold_rows(pick_class[h, j].astype(F32))
            total = total + jnp.where(owner_col == cls + 4 * j, block, 0.0)
        pick_own[h] = total.astype(BF16)
        near_copies.append(send_near(PICK_NEAR + 4 * h, pick_own.at[h], pick_near.at[h]))
        totals.append(total)
    head_at_targets(1)
    rep_copies = []
    for h in range(2):
        for copy in near_copies[h]:
            copy.wait_recv()
        total = totals[h]
        for i in range(3):
            total = total + pick_near[h, i].astype(F32)
        picked[h, x] = total.astype(BF16)
        rep_copies.append([
            send(PICK_REP + 3 * h + d - 1, picked.at[h, x], picked.at[h, x], at_x(d))
            for d in (1, 2, 3)
        ])

    def partial_logits(h, core, k):
        rows = picked[h, pl.ds(2 * core, 2)].reshape(2 * SLOTS, WIDE)
        return jnp.dot(
            rows, weight[h * WIDE : (h + 1) * WIDE, k * SPAN : (k + 1) * SPAN],
            preferred_element_type=F32,
        ).reshape(4, CHUNK, SPAN)

    for copy in rep_copies[0]:
        copy.wait_recv()
    for k in range(2):
        core_out[k] = partial_logits(0, 1 - c, k)
        part[k] = partial_logits(0, c, k)
    for copy in rep_copies[1]:
        copy.wait_recv()
    order = (2, 1, 3, 0)
    core_copies = []
    for k in range(2):
        core_out[k] = core_out[k] + partial_logits(1, 1 - c, k)
        core_copies.append({
            s: send(
                LOGIT_CORE + 4 * k + s, core_out.at[k, y_plus(s)], core_in.at[k, y_plus(s)], sibling
            )
            for s in order
        })
    for k in range(2):
        part[k] = part[k] + partial_logits(1, c, k)

    low, high = pl.ds(0, HALF), pl.ds(HALF, HALF)
    fwd_copies = []
    last_copies = []
    for s in order:
        for k in range(2):
            core_copies[k][s].wait_recv()
            at = y_plus(s)
            part[k, at] = part[k, at] + core_in[k, at]
            number = LOGIT_Y + 6 * k
            if s == 2:
                fwd_copies.append((
                    send(number, part.at[k, at, low], y_fwd.at[k, 0], at_y(1)),
                    send(number + 1, part.at[k, at, high], y_fwd.at[k, 1], at_y(3)),
                ))
            if s == 1:
                last_copies.append(
                    send(number + 2, part.at[k, at, high], y_direct.at[k, 1], at_y(1))
                )
            if s == 3:
                last_copies.append(
                    send(number + 3, part.at[k, at, low], y_direct.at[k, 0], at_y(3))
                )
    for k in range(2):
        number = LOGIT_Y + 6 * k
        fwd_copies[k][0].wait_recv()
        y_sum[k, 0] = y_fwd[k, 0] + part[k, y_plus(1), 0:HALF]
        last_copies.append(send(number + 4, y_sum.at[k, 0], y_acc.at[k, 0], at_y(1)))
        fwd_copies[k][1].wait_recv()
        y_sum[k, 1] = y_fwd[k, 1] + part[k, y_plus(3), HALF:CHUNK]
        last_copies.append(send(number + 5, y_sum.at[k, 1], y_acc.at[k, 1], at_y(3)))
    for h in range(2):
        picked_t[h * WIDE : (h + 1) * WIDE] = picked[h].reshape(REP * SLOTS, WIDE).T
    for copy in last_copies:
        copy.wait_recv()
    for k in range(2):
        columns = pl.ds(k * SPAN, SPAN)
        logits_ref[0:HALF, columns] = part[k, y, 0:HALF] + (y_direct[k, 0] + y_acc[k, 0])
        logits_ref[HALF:CHUNK, columns] = part[k, y, HALF:CHUNK] + (y_direct[k, 1] + y_acc[k, 1])

    loads[3].wait()
    my_seq = 2 * c + lax.div(y, 2)
    first_slot = lax.rem(y, 2) * CHUNK
    my_count = counts_ref[my_seq]
    my_cot = cot_ref[my_seq]
    my_chunk = 4 * c + y
    is_target = column == target_cols[my_chunk]
    logits = logits_ref[...]
    local_max = jnp.max(logits, axis=1, keepdims=True)
    exponent = jnp.exp(logits - local_max)

    exps[my_chunk] = jnp.where(is_target, 0.0, exponent).astype(BF16)
    mine = exps.at[my_chunk]
    before = exps.at[4 * c + y_plus(3)]
    after = exps.at[4 * c + y_plus(1)]
    up_low = send(GRAD_Y, mine.at[low], mine.at[low], at_y(1))
    down_high = send(GRAD_Y + 1, mine.at[high], mine.at[high], at_y(3))
    up_high = send(GRAD_Y + 2, mine.at[high], mine.at[high], at_y(1))
    down_low = send(GRAD_Y + 3, mine.at[low], mine.at[low], at_y(3))
    core_copies = [send(GRAD_CORE, mine, mine, sibling)]

    local_sum = jnp.sum(exponent, axis=1, keepdims=True)
    local_target = jnp.sum(jnp.where(is_target, logits, 0.0), axis=1, keepdims=True)
    max_row = to_row(local_max, 0)
    stat_seq[z] = max_row + to_row(local_sum, CHUNK) + to_row(local_target, 2 * CHUNK)
    seq_copies = [
        send(STAT_SEQ + d - 1, stat_seq.at[z], stat_seq.at[z], at_z(d)) for d in range(1, SEQ)
    ]

    up_low.wait_recv()
    up_again = send(GRAD_Y + 4, before.at[low], before.at[low], at_y(1))
    down_high.wait_recv()
    down_again = send(GRAD_Y + 5, after.at[high], after.at[high], at_y(3))
    up_high.wait_recv()
    core_copies.append(send(GRAD_CORE + 1, before, before, sibling))
    down_low.wait_recv()
    core_copies.append(send(GRAD_CORE + 2, after, after, sibling))

    for copy in seq_copies:
        copy.wait_recv()
    stat_rep[x] = pack_stats(*merge_stats(stat_seq, SEQ))
    copies = [send(STAT_REP + d - 1, stat_rep.at[x], stat_rep.at[x], at_x(d)) for d in (1, 2, 3)]
    up_again.wait_recv()
    down_again.wait_recv()
    across = exps.at[4 * c + y_plus(2)]
    core_copies.append(send(GRAD_CORE + 3, across, across, sibling))
    for copy in copies:
        copy.wait_recv()
    total_max, total_sum, target_logit = merge_stats(stat_rep, REP)

    lane = iota((1, 128), 1)
    live = (lane < CHUNK) & (lane + first_slot < my_count)
    count_row = jnp.full((1, 128), my_count.astype(F32), F32)
    weight_row = jnp.where(live, jnp.full((1, 128), my_cot, F32) / count_row, 0.0)
    factor = jnp.where(live, weight_row * (jnp.exp(max_row - total_max) / total_sum), 0.0)
    at_target = jnp.where(
        live, weight_row * (jnp.exp(target_logit - total_max) / total_sum - 1.0), 0.0
    )
    row_loss = jnp.where(live, (jnp.log(total_sum) + total_max - target_logit) / count_row, 0.0)
    scales[my_chunk] = pack_stats(factor, at_target, row_loss)
    scale_copies = [
        send(SCALE + d - 1, scales.at[my_chunk], scales.at[my_chunk], {"vocab": lax.rem(v + d, 8)})
        for d in range(1, 8)
    ]

    def head_times(core):
        block = exps[pl.ds(4 * core, 4)].reshape(4 * CHUNK, COLS)
        for h in range(2):
            row_sums[h, pl.ds(4 * core, 4)] = lax.dot_general(
                block, weight[h * WIDE : (h + 1) * WIDE], (((1,), (1,)), ((), ())),
                preferred_element_type=F32,
            ).reshape(4, CHUNK, WIDE)

    head_times(c)
    for copy in core_copies:
        copy.wait_recv()
    head_times(1 - c)
    for copy in scale_copies:
        copy.wait_recv()
    factors = [to_column(scales[i], CHUNK) for i in range(8)]
    at_targets = [
        to_column(scales[i], CHUNK, CHUNK).astype(BF16).astype(F32) for i in range(8)
    ]
    rep_copies = []
    for h in range(2):
        for i in range(8):
            rows = factors[i] * row_sums[h, i] + at_targets[i] * target_rows[h, i]
            row_sums[h, i] = rows
            row_out[h, i // 2, CHUNK * (i % 2) : CHUNK * (i % 2 + 1)] = rows.astype(BF16)
        rep_copies.append([
            send(
                ROW_REP + 3 * h + d - 1, row_out.at[h, lax.rem(x + d, REP)], row_in.at[h, d - 1],
                at_x(d),
            )
            for d in (1, 2, 3)
        ])
    for i in range(8):
        values = exps[i].astype(F32) * factors[i]
        grads[i] = jnp.where(column == target_cols[i], at_targets[i], values).astype(BF16)
    owns = [row_sums[h, pl.ds(2 * x, 2)].reshape(SLOTS, WIDE) for h in range(2)]

    def head_part(i):
        columns = pl.ds(i * 256, 256)
        tile = jnp.dot(
            picked_t[...], grads[:, :, columns].reshape(REP * SLOTS, 256), preferred_element_type=F32
        )
        head_out[:, columns] = tile.astype(BF16)
        copy = pltpu.make_async_copy(
            head_out.at[:, columns], head_hbm.at[:, columns], head_sem.at[i]
        )
        copy.start()
        return copy

    near_copies = []
    for h in range(2):
        for copy in rep_copies[h]:
            copy.wait_recv()
        for i in range(3):
            owns[h] = owns[h] + row_in[h, i].astype(F32)
        near_out[h] = owns[h].astype(BF16)
        near_copies.append(send_near(ROW_NEAR + 4 * h, near_out.at[h], near_in.at[h]))
    head_copies = [head_part(0), head_part(1), head_part(2)]
    mine_rows = []
    class_copies = []
    for h in range(2):
        for copy in near_copies[h]:
            copy.wait_recv()
        own = owns[h]
        for i in range(3):
            own = own + near_in[h, i].astype(F32)
        mine = jnp.zeros((FOLD, WIDE), F32)
        for j in range(4):
            block = fold_rows(jnp.where(owner_col == cls + 4 * j, own, 0.0))
            class_out[h, j] = block.astype(BF16)
            mine = jnp.where(member == j, block, mine)
        mine_rows.append(mine)
        class_copies.append([
            send(
                ROW_CLASS + 3 * h + d - 1, class_out.at[h, lax.rem(member + d, 4)],
                class_in.at[h, d - 1], at_z(4 * d),
            )
            for d in (1, 2, 3)
        ])
    head_copies += [head_part(3), head_part(4)]
    for copy in started[: -2 * 3]:
        copy.wait_send()
    for q in range(REP):
        losses_ref[q] = jnp.sum(between(scales[2 * q] + scales[2 * q + 1], 2 * CHUNK))
    for copy in head_copies:
        copy.wait()
    put = jnp.where(put_at, 1.0, 0.0).astype(BF16)
    for h in range(2):
        for copy in class_copies[h]:
            copy.wait_recv()
        mine = mine_rows[h]
        for i in range(3):
            mine = mine + class_in[h, i].astype(F32)
        final = unfold_rows(mine.astype(BF16).astype(F32))
        final = jnp.where(owner_col == z, final, 0.0).astype(BF16)
        grad_ref[0, :, h * WIDE : (h + 1) * WIDE] = jnp.dot(
            put, final, preferred_element_type=F32
        ).astype(BF16)

    for copies in class_copies:
        for copy in copies:
            copy.wait_send()


def hand_over(
    head_in, hidden_in, losses_in, head_ref, hidden_ref, losses_ref,
    head, hidden, losses, in_sem, out_sem,
):
    rows = FEAT // 4
    moves = [(hidden_in, hidden, hidden_ref), (losses_in, losses, losses_ref)]
    for i in range(4):
        at = pl.ds(i * rows, rows)
        moves.append((head_in.at[at], head.at[at], head_ref.at[at]))
    loads = [pltpu.make_async_copy(m[0], m[1], in_sem.at[i]) for i, m in enumerate(moves)]
    stores = [pltpu.make_async_copy(m[1], m[2], out_sem.at[i]) for i, m in enumerate(moves)]
    for load in loads:
        load.start()
    for load, store in zip(loads, stores):
        load.wait()
        store.start()
    for store in stores:
        store.wait()


def shards(hidden, head_weight, positions, counts, targets, seq_cotangent):
    vmem = pl.BlockSpec(memory_space=pltpu.VMEM)
    smem = pl.BlockSpec(memory_space=pltpu.SMEM)
    hbm = pl.BlockSpec(memory_space=pltpu.HBM)
    shapes = (
        jax.ShapeDtypeStruct((FEAT, COLS), BF16),
        jax.ShapeDtypeStruct((1, TOK, FEAT), BF16),
        jax.ShapeDtypeStruct((REP,), F32),
    )
    limit = 60 * 1024 * 1024
    results = pl.pallas_call(
        kernel,
        out_shape=shapes,
        in_specs=[hbm] * 6,
        out_specs=(hbm, vmem, smem),
        scratch_shapes=[
            pltpu.SMEM((REP,), jnp.int32),
            pltpu.SMEM((REP,), F32),
            pltpu.VMEM((REP, SLOTS), jnp.int32),
            pltpu.VMEM((REP, SLOTS), jnp.int32),
            pltpu.VMEM((1, TOK, FEAT), BF16),
            pltpu.VMEM((FEAT, COLS), BF16),
            pltpu.VMEM((2, 4, FOLD, WIDE), BF16),
            pltpu.VMEM((2, SLOTS, WIDE), BF16),
            pltpu.VMEM((2, 3, SLOTS, WIDE), BF16),
            pltpu.VMEM((2, REP, SLOTS, WIDE), BF16),
            pltpu.VMEM((FEAT, REP * SLOTS), BF16),
            pltpu.VMEM((8, CHUNK, 1), jnp.int32),
            pltpu.VMEM((2, 8, CHUNK, WIDE), F32),
            pltpu.VMEM((2, 4, CHUNK, SPAN), F32),
            pltpu.VMEM((2, 4, CHUNK, SPAN), F32),
            pltpu.VMEM((2, 4, CHUNK, SPAN), F32),
            pltpu.VMEM((2, 2, HALF, SPAN), F32),
            pltpu.VMEM((2, 2, HALF, SPAN), F32),
            pltpu.VMEM((2, 2, HALF, SPAN), F32),
            pltpu.VMEM((2, 2, HALF, SPAN), F32),
            pltpu.VMEM((CHUNK, COLS), F32),
            pltpu.VMEM((SEQ, 1, 128), F32),
            pltpu.VMEM((REP, 1, 128), F32),
            pltpu.VMEM((2 * REP, 1, 128), F32),
            pltpu.VMEM((2 * REP, CHUNK, COLS), BF16),
            pltpu.VMEM((2 * REP, CHUNK, COLS), BF16),
            pltpu.VMEM((2, 8, CHUNK, WIDE), F32),
            pltpu.VMEM((2, REP, SLOTS, WIDE), BF16),
            pltpu.VMEM((2, 3, SLOTS, WIDE), BF16),
            pltpu.VMEM((2, SLOTS, WIDE), BF16),
            pltpu.VMEM((2, 3, SLOTS, WIDE), BF16),
            pltpu.VMEM((2, 4, FOLD, WIDE), BF16),
            pltpu.VMEM((2, 3, FOLD, WIDE), BF16),
            pltpu.VMEM((FEAT, COLS), BF16),
            pltpu.SemaphoreType.DMA((MESSAGES,)),
            pltpu.SemaphoreType.DMA((MESSAGES,)),
            pltpu.SemaphoreType.DMA((6,)),
            pltpu.SemaphoreType.DMA((5,)),
        ],
        compiler_params=pltpu.CompilerParams(
            collective_id=0, has_side_effects=True, vmem_limit_bytes=limit
        ),
        cost_estimate=pl.CostEstimate(
            flops=6 * 256 * FEAT * COLS, bytes_accessed=4 * FEAT * COLS, transcendentals=64 * COLS
        ),
    )(counts, seq_cotangent, positions, targets, hidden, head_weight)
    return pl.pallas_call(
        hand_over,
        out_shape=shapes,
        in_specs=[hbm] * 3,
        out_specs=(hbm,) * 3,
        scratch_shapes=[
            pltpu.VMEM((FEAT, COLS), BF16),
            pltpu.VMEM((1, TOK, FEAT), BF16),
            pltpu.SMEM((REP,), F32),
            pltpu.SemaphoreType.DMA((6,)),
            pltpu.SemaphoreType.DMA((6,)),
        ],
        compiler_params=pltpu.CompilerParams(vmem_limit_bytes=limit),
    )(*results)


def solution(mesh):
    return jax.shard_map(
        shards,
        mesh=mesh,
        in_specs=(P("rep", "seq", "vocab"), P("vocab", ("seq", "rep")), P(), P(), P(), P()),
        out_specs=(P("vocab", ("seq", "rep")), P("rep", "seq", "vocab"), P()),
        check_vma=False,
    )
```

```python
import jax
import jax.numpy as jnp
from jax import lax
from jax.experimental import pallas as pl
from jax.experimental.pallas import tpu as pltpu
from jax.sharding import PartitionSpec as P

MESH = pl.DeviceIdType.MESH
F32 = jnp.float32
BF16 = jnp.bfloat16

SEQ = 16
REP = 4
SLOTS = 64
TOK = 64
FEAT = 512
COLS = 1280
FOLD = 16
CHUNK = 32
HALF = 16
WIDE = FEAT // 2
SPAN = COLS // 2

PICK_CLASS = 0
PICK_NEAR = 6
PICK_REP = 14
LOGIT_CORE = 20
LOGIT_Y = 28
STAT_SEQ = 40
STAT_REP = 55
GRAD_Y = 58
GRAD_CORE = 64
SCALE = 68
ROW_REP = 75
ROW_NEAR = 81
ROW_CLASS = 89
TARGET_REP = 95
MESSAGES = 98


def iota(shape, dim):
    return lax.broadcasted_iota(jnp.int32, shape, dim)


def to_column(row, rows, shift=0):
    shape = (rows, row.shape[1])
    at = iota(shape, 1) == iota(shape, 0) + shift
    return jnp.sum(jnp.where(at, row, 0.0), axis=1, keepdims=True)


def to_row(column, shift):
    shape = (CHUNK, 128)
    at = iota(shape, 1) == iota(shape, 0) + shift
    return jnp.sum(jnp.where(at, column, 0.0), axis=0, keepdims=True)


def turn(row, shift):
    return pltpu.roll(row, 128 - shift, 1)


def between(row, first):
    lane = iota((1, 128), 1)
    return jnp.where((lane >= first) & (lane < first + CHUNK), row, 0.0)


def merge_stats(ref, parts):
    rows = [ref[i] for i in range(parts)]
    row_max = rows[0]
    for row in rows[1:]:
        row_max = jnp.maximum(row_max, row)
    row_sum = jnp.zeros((1, 128), F32)
    row_target = jnp.zeros((1, 128), F32)
    for row in rows:
        row_sum = row_sum + turn(row, CHUNK) * jnp.exp(row - row_max)
        row_target = row_target + row
    return row_max, row_sum, turn(row_target, 2 * CHUNK)


def pack_stats(row_max, row_sum, row_target):
    return (
        between(row_max, 0)
        + between(turn(row_sum, 128 - CHUNK), CHUNK)
        + between(turn(row_target, 128 - 2 * CHUNK), 2 * CHUNK)
    )


def fold_rows(rows):
    return (rows[0:16] + rows[16:32]) + (rows[32:48] + rows[48:64])


def unfold_rows(rows):
    return jnp.concatenate([rows, rows, rows, rows], axis=0)


def kernel(
    counts_hbm, cot_hbm, positions_hbm, targets_hbm, hidden_hbm, weight_hbm,
    head_hbm, grad_ref, losses_ref,
    counts_ref, cot_ref, positions_ref, targets_ref, hidden_ref,
    weight, pick_class, pick_own, pick_near, picked, picked_t, target_cols, target_out, target_in,
    core_out, core_in, part, y_fwd, y_sum, y_direct, y_acc, logits_ref,
    stat_seq, stat_rep, scales, exps, grads,
    row_sums, row_out, row_in, near_out, near_in, class_out, class_in, head_out,
    send_sem, recv_sem, load_sem, head_sem,
):
    z = lax.axis_index("seq")
    v = lax.axis_index("vocab")
    x = lax.axis_index("rep")
    y = lax.div(v, 2)
    c = lax.rem(v, 2)
    cls = lax.rem(z, 4)
    member = lax.div(z, 4)

    def at_z(shift):
        return {"seq": lax.rem(z + shift + SEQ, SEQ)}

    def at_x(shift):
        return {"rep": lax.rem(x + shift, REP)}

    def y_plus(shift):
        return lax.rem(y + shift, 4)

    def at_y(shift):
        return {"vocab": y_plus(shift) * 2 + c}

    def load(number, src, dst):
        copy = pltpu.make_async_copy(src, dst, load_sem.at[number])
        copy.start()
        return copy

    loads = [
        load(0, positions_hbm, positions_ref),
        load(1, counts_hbm, counts_ref),
        load(2, hidden_hbm, hidden_ref),
        load(3, cot_hbm, cot_ref),
        load(4, targets_hbm, targets_ref),
        load(5, weight_hbm, weight),
    ]

    sibling = {"vocab": y * 2 + 1 - c}

    started = []

    def send(number, src, dst, device):
        copy = pltpu.make_async_remote_copy(
            src_ref=src,
            dst_ref=dst,
            send_sem=send_sem.at[number],
            recv_sem=recv_sem.at[number],
            device_id=device,
            device_id_type=MESH,
        )
        copy.start()
        started.append(copy)
        return copy

    barrier = pltpu.get_barrier_semaphore()
    friends = [at_z(s) for s in range(1, SEQ)] + [at_x(s) for s in (1, 2, 3)]
    friends += [{"vocab": lax.rem(v + s, 8)} for s in range(1, 8)]
    for friend in friends:
        pl.semaphore_signal(barrier, inc=1, device_id=friend, device_id_type=MESH)

    loads[0].wait()
    loads[1].wait()
    all_positions = positions_ref[...].astype(F32)
    position_row = jnp.sum(
        jnp.where(iota((REP, SLOTS), 0) == x, all_positions, 0.0), axis=0, keepdims=True
    )
    count = counts_ref[x]
    position_col = to_column(position_row, SLOTS).astype(jnp.int32)
    live_col = iota((SLOTS, 1), 0) < count
    owner_col = jnp.where(live_col, lax.div(position_col, TOK), -1)
    pick_at = (iota((SLOTS, TOK), 1) + z * TOK == position_col) & (iota((SLOTS, TOK), 0) < count)
    put_at = (iota((TOK, SLOTS), 0) + z * TOK == position_row.astype(jnp.int32)) & (
        iota((TOK, SLOTS), 1) < count
    )

    loads[2].wait()
    own_rows = jnp.dot(
        jnp.where(pick_at, 1.0, 0.0).astype(BF16), hidden_ref[0], preferred_element_type=F32
    )
    folded = fold_rows(own_rows).astype(BF16)
    for h in range(2):
        pick_class[h, member] = folded[:, h * WIDE : (h + 1) * WIDE]

    pl.semaphore_wait(barrier, len(friends))

    class_copies = [
        [
            send(
                PICK_CLASS + 3 * h + d - 1, pick_class.at[h, member], pick_class.at[h, member],
                at_z(4 * d),
            )
            for d in (1, 2, 3)
        ]
        for h in range(2)
    ]

    def send_near(number, src, dst):
        low, high = pl.ds(0, 32), pl.ds(32, 32)
        return [
            send(number, src, dst.at[0], at_z(1)),
            send(number + 1, src, dst.at[1], at_z(-1)),
            send(number + 2, src.at[low], dst.at[2, low], at_z(2)),
            send(number + 3, src.at[high], dst.at[2, high], at_z(-2)),
        ]

    loads[4].wait()
    all_targets = targets_ref[...].astype(F32)
    column = iota((CHUNK, COLS), 1) + (z * REP + x) * COLS
    for i in range(8):
        target_cols[i] = to_column(
            all_targets[i // 2 : i // 2 + 1], CHUNK, CHUNK * (i % 2)
        ).astype(jnp.int32)

    def head_at_targets(h):
        hot = [jnp.where(column == target_cols[i], 1.0, 0.0).astype(BF16) for i in range(8)]
        there = lax.dot_general(
            jnp.concatenate(hot, axis=0), weight[h * WIDE : (h + 1) * WIDE],
            (((1,), (1,)), ((), ())), preferred_element_type=F32,
        ).reshape(REP, SLOTS, WIDE)
        for q in range(REP):
            target_out[q, h] = there[q].astype(BF16)

    loads[5].wait()
    head_at_targets(0)

    totals = []
    near_copies = []
    for h in range(2):
        for copy in class_copies[h]:
            copy.wait_recv()
        total = jnp.zeros((SLOTS, WIDE), F32)
        for j in range(4):
            block = unfold_rows(pick_class[h, j].astype(F32))
            total = total + jnp.where(owner_col == cls + 4 * j, block, 0.0)
        pick_own[h] = total.astype(BF16)
        near_copies.append(send_near(PICK_NEAR + 4 * h, pick_own.at[h], pick_near.at[h]))
        totals.append(total)
    head_at_targets(1)
    rep_copies = []
    for h in range(2):
        for copy in near_copies[h]:
            copy.wait_recv()
        total = totals[h]
        for i in range(3):
            total = total + pick_near[h, i].astype(F32)
        picked[h, x] = total.astype(BF16)
        rep_copies.append([
            send(PICK_REP + 3 * h + d - 1, picked.at[h, x], picked.at[h, x], at_x(d))
            for d in (1, 2, 3)
        ])

    def partial_logits(h, core, k):
        rows = picked[h, pl.ds(2 * core, 2)].reshape(2 * SLOTS, WIDE)
        return jnp.dot(
            rows, weight[h * WIDE : (h + 1) * WIDE, k * SPAN : (k + 1) * SPAN],
            preferred_element_type=F32,
        ).reshape(4, CHUNK, SPAN)

    for copy in rep_copies[0]:
        copy.wait_recv()
    for k in range(2):
        core_out[k] = partial_logits(0, 1 - c, k)
        part[k] = partial_logits(0, c, k)
    for copy in rep_copies[1]:
        copy.wait_recv()
    order = (2, 1, 3, 0)
    core_copies = []
    for k in range(2):
        core_out[k] = core_out[k] + partial_logits(1, 1 - c, k)
        core_copies.append({
            s: send(
                LOGIT_CORE + 4 * k + s, core_out.at[k, y_plus(s)], core_in.at[k, y_plus(s)], sibling
            )
            for s in order
        })
    for k in range(2):
        part[k] = part[k] + partial_logits(1, c, k)
    target_copies = [
        send(
            TARGET_REP + d - 1, target_out.at[lax.rem(x + d, REP)], target_in.at[d - 1], at_x(d)
        )
        for d in (1, 2, 3)
    ]

    low, high = pl.ds(0, HALF), pl.ds(HALF, HALF)
    fwd_copies = []
    last_copies = []
    for s in order:
        for k in range(2):
            core_copies[k][s].wait_recv()
            at = y_plus(s)
            part[k, at] = part[k, at] + core_in[k, at]
            number = LOGIT_Y + 6 * k
            if s == 2:
                fwd_copies.append((
                    send(number, part.at[k, at, low], y_fwd.at[k, 0], at_y(1)),
                    send(number + 1, part.at[k, at, high], y_fwd.at[k, 1], at_y(3)),
                ))
            if s == 1:
                last_copies.append(
                    send(number + 2, part.at[k, at, high], y_direct.at[k, 1], at_y(1))
                )
            if s == 3:
                last_copies.append(
                    send(number + 3, part.at[k, at, low], y_direct.at[k, 0], at_y(3))
                )
    for k in range(2):
        number = LOGIT_Y + 6 * k
        fwd_copies[k][0].wait_recv()
        y_sum[k, 0] = y_fwd[k, 0] + part[k, y_plus(1), 0:HALF]
        last_copies.append(send(number + 4, y_sum.at[k, 0], y_acc.at[k, 0], at_y(1)))
        fwd_copies[k][1].wait_recv()
        y_sum[k, 1] = y_fwd[k, 1] + part[k, y_plus(3), HALF:CHUNK]
        last_copies.append(send(number + 5, y_sum.at[k, 1], y_acc.at[k, 1], at_y(3)))
    for h in range(2):
        picked_t[h * WIDE : (h + 1) * WIDE] = picked[h].reshape(REP * SLOTS, WIDE).T
    for copy in last_copies:
        copy.wait_recv()
    for k in range(2):
        columns = pl.ds(k * SPAN, SPAN)
        logits_ref[0:HALF, columns] = part[k, y, 0:HALF] + (y_direct[k, 0] + y_acc[k, 0])
        logits_ref[HALF:CHUNK, columns] = part[k, y, HALF:CHUNK] + (y_direct[k, 1] + y_acc[k, 1])

    loads[3].wait()
    my_seq = 2 * c + lax.div(y, 2)
    first_slot = lax.rem(y, 2) * CHUNK
    my_count = counts_ref[my_seq]
    my_cot = cot_ref[my_seq]
    my_chunk = 4 * c + y
    is_target = column == target_cols[my_chunk]
    logits = logits_ref[...]
    local_max = jnp.max(logits, axis=1, keepdims=True)
    exponent = jnp.exp(logits - local_max)

    exps[my_chunk] = jnp.where(is_target, 0.0, exponent).astype(BF16)
    mine = exps.at[my_chunk]
    before = exps.at[4 * c + y_plus(3)]
    after = exps.at[4 * c + y_plus(1)]
    up_low = send(GRAD_Y, mine.at[low], mine.at[low], at_y(1))
    down_high = send(GRAD_Y + 1, mine.at[high], mine.at[high], at_y(3))
    up_high = send(GRAD_Y + 2, mine.at[high], mine.at[high], at_y(1))
    down_low = send(GRAD_Y + 3, mine.at[low], mine.at[low], at_y(3))
    core_copies = [send(GRAD_CORE, mine, mine, sibling)]

    local_sum = jnp.sum(exponent, axis=1, keepdims=True)
    local_target = jnp.sum(jnp.where(is_target, logits, 0.0), axis=1, keepdims=True)
    max_row = to_row(local_max, 0)
    stat_seq[z] = max_row + to_row(local_sum, CHUNK) + to_row(local_target, 2 * CHUNK)
    seq_copies = [
        send(STAT_SEQ + d - 1, stat_seq.at[z], stat_seq.at[z], at_z(d))
        for d in (8, 7, 9, 6, 10, 5, 11, 4, 12, 3, 13, 2, 14, 1, 15)
    ]

    up_low.wait_recv()
    up_again = send(GRAD_Y + 4, before.at[low], before.at[low], at_y(1))
    down_high.wait_recv()
    down_again = send(GRAD_Y + 5, after.at[high], after.at[high], at_y(3))
    up_high.wait_recv()
    core_copies.append(send(GRAD_CORE + 1, before, before, sibling))
    down_low.wait_recv()
    core_copies.append(send(GRAD_CORE + 2, after, after, sibling))

    up_again.wait_recv()
    down_again.wait_recv()
    across = exps.at[4 * c + y_plus(2)]
    core_copies.append(send(GRAD_CORE + 3, across, across, sibling))

    for copy in seq_copies:
        copy.wait_recv()
    stat_rep[x] = pack_stats(*merge_stats(stat_seq, SEQ)) + to_row(local_max, 3 * CHUNK)
    stat_copies = [
        send(STAT_REP + d - 1, stat_rep.at[x], stat_rep.at[x], at_x(d)) for d in (1, 2, 3)
    ]

    def head_times(core):
        block = exps[pl.ds(4 * core, 4)].reshape(4 * CHUNK, COLS)
        for h in range(2):
            rows = lax.dot_general(
                block, weight[h * WIDE : (h + 1) * WIDE], (((1,), (1,)), ((), ())),
                preferred_element_type=F32,
            ).reshape(2, SLOTS, WIDE)
            row_sums[h, pl.ds(2 * core, 2)] = rows
            row_out[h, pl.ds(2 * core, 2)] = rows.astype(BF16)

    head_times(c)
    for copy in core_copies:
        copy.wait_recv()
    head_times(1 - c)
    rep_copies = [
        [
            send(
                ROW_REP + 3 * h + d - 1, row_out.at[h, lax.rem(x + d, REP)], row_in.at[h, d - 1],
                at_x(d),
            )
            for d in (1, 2, 3)
        ]
        for h in range(2)
    ]

    for copy in stat_copies:
        copy.wait_recv()
    total_max, total_sum, target_logit = merge_stats(stat_rep, REP)
    lane = iota((1, 128), 1)
    live = (lane < CHUNK) & (lane + first_slot < my_count)
    count_row = jnp.full((1, 128), my_count.astype(F32), F32)
    weight_row = jnp.where(live, jnp.full((1, 128), my_cot, F32) / count_row, 0.0)
    factor_row = jnp.zeros((1, 128), F32)
    for i in range(REP):
        there = jnp.exp(turn(stat_rep[i], 3 * CHUNK) - total_max) / total_sum
        factor = jnp.where(live, weight_row * there, 0.0)
        factor_row = factor_row + (turn(factor, 128 - i * CHUNK) if i else factor)
    at_target = jnp.where(
        live, weight_row * (jnp.exp(target_logit - total_max) / total_sum - 1.0), 0.0
    )
    row_loss = jnp.where(live, (jnp.log(total_sum) + total_max - target_logit) / count_row, 0.0)
    scales[my_chunk, 0:1] = factor_row
    scales[my_chunk, 1:2] = at_target + turn(row_loss, 128 - CHUNK)
    scale_copies = [
        send(SCALE + d - 1, scales.at[my_chunk], scales.at[my_chunk], {"vocab": lax.rem(v + d, 8)})
        for d in range(1, 8)
    ]
    for copy in scale_copies:
        copy.wait_recv()

    def slots_of_mine(part_of, first):
        return jnp.concatenate(
            [to_column(scales[2 * x + i, part_of : part_of + 1], CHUNK, first) for i in range(2)],
            axis=0,
        )

    slot_factors = [
        slots_of_mine(0, CHUNK * lax.rem(x + REP - d, REP)) for d in range(REP)
    ]
    slot_target = slots_of_mine(1, 0).astype(BF16).astype(F32)
    for copy in target_copies:
        copy.wait_recv()
    owns = []
    for h in range(2):
        column_sum = target_out[x, h].astype(F32)
        for i in range(3):
            column_sum = column_sum + target_in[i, h].astype(F32)
        owns.append(slot_target * column_sum + slot_factors[0] * row_sums[h, x])

    def scale_grads():
        for i in range(8):
            factor = to_column(scales[i, 0:1], CHUNK, CHUNK * x)
            at_own = to_column(scales[i, 1:2], CHUNK)
            values = exps[i].astype(F32) * factor
            grads[i] = jnp.where(column == target_cols[i], at_own, values).astype(BF16)

    def head_part(i):
        columns = pl.ds(i * 256, 256)
        tile = jnp.dot(
            picked_t[...], grads[:, :, columns].reshape(REP * SLOTS, 256), preferred_element_type=F32
        )
        head_out[:, columns] = tile.astype(BF16)
        copy = pltpu.make_async_copy(
            head_out.at[:, columns], head_hbm.at[:, columns], head_sem.at[i]
        )
        copy.start()
        return copy

    near_copies = []
    for h in range(2):
        for copy in rep_copies[h]:
            copy.wait_recv()
        for i in range(3):
            owns[h] = owns[h] + slot_factors[i + 1] * row_in[h, i].astype(F32)
        near_out[h] = owns[h].astype(BF16)
        near_copies.append(send_near(ROW_NEAR + 4 * h, near_out.at[h], near_in.at[h]))
    scale_grads()
    head_copies = [head_part(0), head_part(1)]
    mine_rows = []
    class_copies = []
    for h in range(2):
        for copy in near_copies[h]:
            copy.wait_recv()
        own = owns[h]
        for i in range(3):
            own = own + near_in[h, i].astype(F32)
        mine = jnp.zeros((FOLD, WIDE), F32)
        for j in range(4):
            block = fold_rows(jnp.where(owner_col == cls + 4 * j, own, 0.0))
            class_out[h, j] = block.astype(BF16)
            mine = jnp.where(member == j, block, mine)
        mine_rows.append(mine)
        class_copies.append([
            send(
                ROW_CLASS + 3 * h + d - 1, class_out.at[h, lax.rem(member + d, 4)],
                class_in.at[h, d - 1], at_z(4 * d),
            )
            for d in (1, 2, 3)
        ])
    head_copies += [head_part(2), head_part(3), head_part(4)]
    for copy in started[: -2 * 3]:
        copy.wait_send()
    for q in range(REP):
        losses_ref[q] = jnp.sum(between(scales[2 * q, 1:2] + scales[2 * q + 1, 1:2], CHUNK))
    for copy in head_copies:
        copy.wait()
    put = jnp.where(put_at, 1.0, 0.0).astype(BF16)
    for h in range(2):
        for copy in class_copies[h]:
            copy.wait_recv()
        mine = mine_rows[h]
        for i in range(3):
            mine = mine + class_in[h, i].astype(F32)
        final = unfold_rows(mine.astype(BF16).astype(F32))
        final = jnp.where(owner_col == z, final, 0.0).astype(BF16)
        grad_ref[0, :, h * WIDE : (h + 1) * WIDE] = jnp.dot(
            put, final, preferred_element_type=F32
        ).astype(BF16)

    for copies in class_copies:
        for copy in copies:
            copy.wait_send()


def hand_over(
    head_in, hidden_in, losses_in, head_ref, hidden_ref, losses_ref,
    head, hidden, losses, in_sem, out_sem,
):
    rows = FEAT // 4
    moves = [(hidden_in, hidden, hidden_ref), (losses_in, losses, losses_ref)]
    for i in range(4):
        at = pl.ds(i * rows, rows)
        moves.append((head_in.at[at], head.at[at], head_ref.at[at]))
    loads = [pltpu.make_async_copy(m[0], m[1], in_sem.at[i]) for i, m in enumerate(moves)]
    stores = [pltpu.make_async_copy(m[1], m[2], out_sem.at[i]) for i, m in enumerate(moves)]
    for load in loads:
        load.start()
    for load, store in zip(loads, stores):
        load.wait()
        store.start()
    for store in stores:
        store.wait()


def shards(hidden, head_weight, positions, counts, targets, seq_cotangent):
    vmem = pl.BlockSpec(memory_space=pltpu.VMEM)
    smem = pl.BlockSpec(memory_space=pltpu.SMEM)
    hbm = pl.BlockSpec(memory_space=pltpu.HBM)
    shapes = (
        jax.ShapeDtypeStruct((FEAT, COLS), BF16),
        jax.ShapeDtypeStruct((1, TOK, FEAT), BF16),
        jax.ShapeDtypeStruct((REP,), F32),
    )
    limit = 60 * 1024 * 1024
    results = pl.pallas_call(
        kernel,
        out_shape=shapes,
        in_specs=[hbm] * 6,
        out_specs=(hbm, vmem, smem),
        scratch_shapes=[
            pltpu.SMEM((REP,), jnp.int32),
            pltpu.SMEM((REP,), F32),
            pltpu.VMEM((REP, SLOTS), jnp.int32),
            pltpu.VMEM((REP, SLOTS), jnp.int32),
            pltpu.VMEM((1, TOK, FEAT), BF16),
            pltpu.VMEM((FEAT, COLS), BF16),
            pltpu.VMEM((2, 4, FOLD, WIDE), BF16),
            pltpu.VMEM((2, SLOTS, WIDE), BF16),
            pltpu.VMEM((2, 3, SLOTS, WIDE), BF16),
            pltpu.VMEM((2, REP, SLOTS, WIDE), BF16),
            pltpu.VMEM((FEAT, REP * SLOTS), BF16),
            pltpu.VMEM((8, CHUNK, 1), jnp.int32),
            pltpu.VMEM((REP, 2, SLOTS, WIDE), BF16),
            pltpu.VMEM((3, 2, SLOTS, WIDE), BF16),
            pltpu.VMEM((2, 4, CHUNK, SPAN), F32),
            pltpu.VMEM((2, 4, CHUNK, SPAN), F32),
            pltpu.VMEM((2, 4, CHUNK, SPAN), F32),
            pltpu.VMEM((2, 2, HALF, SPAN), F32),
            pltpu.VMEM((2, 2, HALF, SPAN), F32),
            pltpu.VMEM((2, 2, HALF, SPAN), F32),
            pltpu.VMEM((2, 2, HALF, SPAN), F32),
            pltpu.VMEM((CHUNK, COLS), F32),
            pltpu.VMEM((SEQ, 1, 128), F32),
            pltpu.VMEM((REP, 1, 128), F32),
            pltpu.VMEM((2 * REP, 2, 128), F32),
            pltpu.VMEM((2 * REP, CHUNK, COLS), BF16),
            pltpu.VMEM((2 * REP, CHUNK, COLS), BF16),
            pltpu.VMEM((2, REP, SLOTS, WIDE), F32),
            pltpu.VMEM((2, REP, SLOTS, WIDE), BF16),
            pltpu.VMEM((2, 3, SLOTS, WIDE), BF16),
            pltpu.VMEM((2, SLOTS, WIDE), BF16),
            pltpu.VMEM((2, 3, SLOTS, WIDE), BF16),
            pltpu.VMEM((2, 4, FOLD, WIDE), BF16),
            pltpu.VMEM((2, 3, FOLD, WIDE), BF16),
            pltpu.VMEM((FEAT, COLS), BF16),
            pltpu.SemaphoreType.DMA((MESSAGES,)),
            pltpu.SemaphoreType.DMA((MESSAGES,)),
            pltpu.SemaphoreType.DMA((6,)),
            pltpu.SemaphoreType.DMA((5,)),
        ],
        compiler_params=pltpu.CompilerParams(
            collective_id=0, has_side_effects=True, vmem_limit_bytes=limit
        ),
        cost_estimate=pl.CostEstimate(
            flops=6 * 256 * FEAT * COLS, bytes_accessed=4 * FEAT * COLS, transcendentals=64 * COLS
        ),
    )(counts, seq_cotangent, positions, targets, hidden, head_weight)
    return pl.pallas_call(
        hand_over,
        out_shape=shapes,
        in_specs=[hbm] * 3,
        out_specs=(hbm,) * 3,
        scratch_shapes=[
            pltpu.VMEM((FEAT, COLS), BF16),
            pltpu.VMEM((1, TOK, FEAT), BF16),
            pltpu.SMEM((REP,), F32),
            pltpu.SemaphoreType.DMA((6,)),
            pltpu.SemaphoreType.DMA((6,)),
        ],
        compiler_params=pltpu.CompilerParams(vmem_limit_bytes=limit),
    )(*results)


def solution(mesh):
    return jax.shard_map(
        shards,
        mesh=mesh,
        in_specs=(P("rep", "seq", "vocab"), P("vocab", ("seq", "rep")), P(), P(), P(), P()),
        out_specs=(P("vocab", ("seq", "rep")), P("rep", "seq", "vocab"), P()),
        check_vma=False,
    )
```

```python
import jax
import jax.numpy as jnp
from jax import lax
from jax.experimental import pallas as pl
from jax.experimental.pallas import tpu as pltpu
from jax.sharding import PartitionSpec as P

MESH = pl.DeviceIdType.MESH
F32 = jnp.float32
BF16 = jnp.bfloat16

SEQ = 16
REP = 4
SLOTS = 64
TOK = 64
FEAT = 512
COLS = 1280
FOLD = 16
CHUNK = 32
HALF = 16
WIDE = FEAT // 2
SPAN = COLS // 2

PICK_CLASS = 0
PICK_NEAR = 6
PICK_REP = 14
LOGIT_CORE = 20
LOGIT_Y = 28
STAT_SEQ = 40
STAT_REP = 55
GRAD_Y = 58
GRAD_CORE = 66
SCALE = 69
ROW_REP = 76
ROW_NEAR = 82
ROW_CLASS = 90
TARGET_REP = 96
MESSAGES = 99


def iota(shape, dim):
    return lax.broadcasted_iota(jnp.int32, shape, dim)


def to_column(row, rows, shift=0):
    shape = (rows, row.shape[1])
    at = iota(shape, 1) == iota(shape, 0) + shift
    return jnp.sum(jnp.where(at, row, 0.0), axis=1, keepdims=True)


def to_row(column, shift):
    shape = (CHUNK, 128)
    at = iota(shape, 1) == iota(shape, 0) + shift
    return jnp.sum(jnp.where(at, column, 0.0), axis=0, keepdims=True)


def turn(row, shift):
    return pltpu.roll(row, 128 - shift, 1)


def between(row, first):
    lane = iota((1, 128), 1)
    return jnp.where((lane >= first) & (lane < first + CHUNK), row, 0.0)


def merge_stats(ref, parts):
    rows = [ref[i] for i in range(parts)]
    row_max = rows[0]
    for row in rows[1:]:
        row_max = jnp.maximum(row_max, row)
    row_sum = jnp.zeros((1, 128), F32)
    row_target = jnp.zeros((1, 128), F32)
    for row in rows:
        row_sum = row_sum + turn(row, CHUNK) * jnp.exp(row - row_max)
        row_target = row_target + row
    return row_max, row_sum, turn(row_target, 2 * CHUNK)


def pack_stats(row_max, row_sum, row_target):
    return (
        between(row_max, 0)
        + between(turn(row_sum, 128 - CHUNK), CHUNK)
        + between(turn(row_target, 128 - 2 * CHUNK), 2 * CHUNK)
    )


def fold_rows(rows):
    return (rows[0:16] + rows[16:32]) + (rows[32:48] + rows[48:64])


def unfold_rows(rows):
    return jnp.concatenate([rows, rows, rows, rows], axis=0)


def kernel(
    counts_hbm, cot_hbm, positions_hbm, targets_hbm, hidden_hbm, weight_hbm,
    head_hbm, grad_ref, losses_ref,
    counts_ref, cot_ref, positions_ref, targets_ref, hidden_ref,
    weight, pick_class, pick_own, pick_near, picked, picked_t, target_cols, target_out, target_in,
    core_out, core_in, part, y_fwd, y_sum, y_direct, y_acc, logits_ref,
    stat_seq, stat_rep, scales, exps, grads,
    row_sums, row_out, row_in, near_out, near_in, class_out, class_in, head_out,
    send_sem, recv_sem, load_sem, head_sem,
):
    z = lax.axis_index("seq")
    v = lax.axis_index("vocab")
    x = lax.axis_index("rep")
    y = lax.div(v, 2)
    c = lax.rem(v, 2)
    cls = lax.rem(z, 4)
    member = lax.div(z, 4)

    def at_z(shift):
        return {"seq": lax.rem(z + shift + SEQ, SEQ)}

    def at_x(shift):
        return {"rep": lax.rem(x + shift, REP)}

    def y_plus(shift):
        return lax.rem(y + shift, 4)

    def at_y(shift):
        return {"vocab": y_plus(shift) * 2 + c}

    def across_y(shift):
        return {"vocab": y_plus(shift) * 2 + 1 - c}

    def load(number, src, dst):
        copy = pltpu.make_async_copy(src, dst, load_sem.at[number])
        copy.start()
        return copy

    loads = [
        load(0, positions_hbm, positions_ref),
        load(1, counts_hbm, counts_ref),
        load(2, hidden_hbm, hidden_ref),
        load(3, cot_hbm, cot_ref),
        load(4, targets_hbm, targets_ref),
        load(5, weight_hbm, weight),
    ]

    sibling = {"vocab": y * 2 + 1 - c}

    started = []

    def send(number, src, dst, device):
        copy = pltpu.make_async_remote_copy(
            src_ref=src,
            dst_ref=dst,
            send_sem=send_sem.at[number],
            recv_sem=recv_sem.at[number],
            device_id=device,
            device_id_type=MESH,
        )
        copy.start()
        started.append(copy)
        return copy

    barrier = pltpu.get_barrier_semaphore()
    friends = [at_z(s) for s in range(1, SEQ)] + [at_x(s) for s in (1, 2, 3)]
    friends += [{"vocab": lax.rem(v + s, 8)} for s in range(1, 8)]
    for friend in friends:
        pl.semaphore_signal(barrier, inc=1, device_id=friend, device_id_type=MESH)

    loads[0].wait()
    loads[1].wait()
    all_positions = positions_ref[...].astype(F32)
    position_row = jnp.sum(
        jnp.where(iota((REP, SLOTS), 0) == x, all_positions, 0.0), axis=0, keepdims=True
    )
    count = counts_ref[x]
    position_col = to_column(position_row, SLOTS).astype(jnp.int32)
    live_col = iota((SLOTS, 1), 0) < count
    owner_col = jnp.where(live_col, lax.div(position_col, TOK), -1)
    pick_at = (iota((SLOTS, TOK), 1) + z * TOK == position_col) & (iota((SLOTS, TOK), 0) < count)
    put_at = (iota((TOK, SLOTS), 0) + z * TOK == position_row.astype(jnp.int32)) & (
        iota((TOK, SLOTS), 1) < count
    )

    loads[2].wait()
    own_rows = jnp.dot(
        jnp.where(pick_at, 1.0, 0.0).astype(BF16), hidden_ref[0], preferred_element_type=F32
    )
    folded = fold_rows(own_rows).astype(BF16)
    for h in range(2):
        pick_class[h, member] = folded[:, h * WIDE : (h + 1) * WIDE]

    pl.semaphore_wait(barrier, len(friends))

    class_copies = [
        [
            send(
                PICK_CLASS + 3 * h + d - 1, pick_class.at[h, member], pick_class.at[h, member],
                at_z(4 * d),
            )
            for d in (2, 1, 3)
        ]
        for h in range(2)
    ]

    def send_near(number, src, dst):
        low, high = pl.ds(0, 32), pl.ds(32, 32)
        return [
            send(number, src, dst.at[0], at_z(1)),
            send(number + 1, src, dst.at[1], at_z(-1)),
            send(number + 2, src.at[low], dst.at[2, low], at_z(2)),
            send(number + 3, src.at[high], dst.at[2, high], at_z(-2)),
        ]

    loads[4].wait()
    all_targets = targets_ref[...].astype(F32)
    column = iota((CHUNK, COLS), 1) + (z * REP + x) * COLS
    for i in range(8):
        target_cols[i] = to_column(
            all_targets[i // 2 : i // 2 + 1], CHUNK, CHUNK * (i % 2)
        ).astype(jnp.int32)

    def head_at_targets(h):
        hot = [jnp.where(column == target_cols[i], 1.0, 0.0).astype(BF16) for i in range(8)]
        there = lax.dot_general(
            jnp.concatenate(hot, axis=0), weight[h * WIDE : (h + 1) * WIDE],
            (((1,), (1,)), ((), ())), preferred_element_type=F32,
        ).reshape(REP, SLOTS, WIDE)
        for q in range(REP):
            target_out[q, h] = there[q].astype(BF16)

    loads[5].wait()
    head_at_targets(0)

    totals = []
    near_copies = []
    for h in range(2):
        for copy in class_copies[h]:
            copy.wait_recv()
        total = jnp.zeros((SLOTS, WIDE), F32)
        for j in range(4):
            block = unfold_rows(pick_class[h, j].astype(F32))
            total = total + jnp.where(owner_col == cls + 4 * j, block, 0.0)
        pick_own[h] = total.astype(BF16)
        near_copies.append(send_near(PICK_NEAR + 4 * h, pick_own.at[h], pick_near.at[h]))
        totals.append(total)
    head_at_targets(1)
    rep_copies = []
    for h in range(2):
        for copy in near_copies[h]:
            copy.wait_recv()
        total = totals[h]
        for i in range(3):
            total = total + pick_near[h, i].astype(F32)
        picked[h, x] = total.astype(BF16)
        rep_copies.append([
            send(PICK_REP + 3 * h + d - 1, picked.at[h, x], picked.at[h, x], at_x(d))
            for d in (1, 2, 3)
        ])

    def partial_logits(h, core, k):
        rows = picked[h, pl.ds(2 * core, 2)].reshape(2 * SLOTS, WIDE)
        return jnp.dot(
            rows, weight[h * WIDE : (h + 1) * WIDE, k * SPAN : (k + 1) * SPAN],
            preferred_element_type=F32,
        ).reshape(4, CHUNK, SPAN)

    for copy in rep_copies[0]:
        copy.wait_recv()
    for k in range(2):
        core_out[k] = partial_logits(0, 1 - c, k)
        part[k] = partial_logits(0, c, k)
    for copy in rep_copies[1]:
        copy.wait_recv()
    order = (2, 1, 3, 0)
    core_copies = []
    for k in range(2):
        core_out[k] = core_out[k] + partial_logits(1, 1 - c, k)
        core_copies.append({
            s: send(
                LOGIT_CORE + 4 * k + s, core_out.at[k, y_plus(s)], core_in.at[k, y_plus(s)], sibling
            )
            for s in order
        })
    for k in range(2):
        part[k] = part[k] + partial_logits(1, c, k)
    target_copies = [
        send(
            TARGET_REP + d - 1, target_out.at[lax.rem(x + d, REP)], target_in.at[d - 1], at_x(d)
        )
        for d in (1, 2, 3)
    ]

    low, high = pl.ds(0, HALF), pl.ds(HALF, HALF)
    fwd_copies = []
    last_copies = []
    for s in order:
        for k in range(2):
            core_copies[k][s].wait_recv()
            at = y_plus(s)
            part[k, at] = part[k, at] + core_in[k, at]
            number = LOGIT_Y + 6 * k
            if s == 2:
                fwd_copies.append((
                    send(number, part.at[k, at, low], y_fwd.at[k, 0], at_y(1)),
                    send(number + 1, part.at[k, at, high], y_fwd.at[k, 1], at_y(3)),
                ))
            if s == 1:
                last_copies.append(
                    send(number + 2, part.at[k, at, high], y_direct.at[k, 1], at_y(1))
                )
            if s == 3:
                last_copies.append(
                    send(number + 3, part.at[k, at, low], y_direct.at[k, 0], at_y(3))
                )
    for k in range(2):
        number = LOGIT_Y + 6 * k
        fwd_copies[k][0].wait_recv()
        y_sum[k, 0] = y_fwd[k, 0] + part[k, y_plus(1), 0:HALF]
        last_copies.append(send(number + 4, y_sum.at[k, 0], y_acc.at[k, 0], at_y(1)))
        fwd_copies[k][1].wait_recv()
        y_sum[k, 1] = y_fwd[k, 1] + part[k, y_plus(3), HALF:CHUNK]
        last_copies.append(send(number + 5, y_sum.at[k, 1], y_acc.at[k, 1], at_y(3)))
    for h in range(2):
        picked_t[h * WIDE : (h + 1) * WIDE] = picked[h].reshape(REP * SLOTS, WIDE).T
    for copy in last_copies:
        copy.wait_recv()
    for k in range(2):
        columns = pl.ds(k * SPAN, SPAN)
        logits_ref[0:HALF, columns] = part[k, y, 0:HALF] + (y_direct[k, 0] + y_acc[k, 0])
        logits_ref[HALF:CHUNK, columns] = part[k, y, HALF:CHUNK] + (y_direct[k, 1] + y_acc[k, 1])

    loads[3].wait()
    my_seq = 2 * c + lax.div(y, 2)
    first_slot = lax.rem(y, 2) * CHUNK
    my_count = counts_ref[my_seq]
    my_cot = cot_ref[my_seq]
    my_chunk = 4 * c + y
    is_target = column == target_cols[my_chunk]
    logits = logits_ref[...]
    local_max = jnp.max(logits, axis=1, keepdims=True)
    exponent = jnp.exp(logits - local_max)

    exps[my_chunk] = jnp.where(is_target, 0.0, exponent).astype(BF16)
    mine = exps.at[my_chunk]
    before = exps.at[4 * c + y_plus(3)]
    after = exps.at[4 * c + y_plus(1)]
    up_low = send(GRAD_Y, mine.at[low], mine.at[low], at_y(1))
    down_high = send(GRAD_Y + 1, mine.at[high], mine.at[high], at_y(3))
    up_high = send(GRAD_Y + 2, mine.at[high], mine.at[high], at_y(1))
    down_low = send(GRAD_Y + 3, mine.at[low], mine.at[low], at_y(3))
    core_copies = [send(GRAD_CORE, mine, mine, sibling)]

    local_sum = jnp.sum(exponent, axis=1, keepdims=True)
    local_target = jnp.sum(jnp.where(is_target, logits, 0.0), axis=1, keepdims=True)
    max_row = to_row(local_max, 0)
    stat_seq[z] = max_row + to_row(local_sum, CHUNK) + to_row(local_target, 2 * CHUNK)
    seq_copies = [
        send(STAT_SEQ + d - 1, stat_seq.at[z], stat_seq.at[z], at_z(d))
        for d in (8, 7, 9, 6, 10, 5, 11, 4, 12, 3, 13, 2, 14, 1, 15)
    ]

    up_low.wait_recv()
    relays = [
        send(GRAD_Y + 4, before.at[low], before.at[low], at_y(1)),
        send(GRAD_Y + 5, before.at[low], before.at[low], across_y(1)),
    ]
    down_high.wait_recv()
    relays.append(send(GRAD_Y + 6, after.at[high], after.at[high], at_y(3)))
    relays.append(send(GRAD_Y + 7, after.at[high], after.at[high], across_y(3)))
    up_high.wait_recv()
    core_copies.append(send(GRAD_CORE + 1, before, before, sibling))
    down_low.wait_recv()
    core_copies.append(send(GRAD_CORE + 2, after, after, sibling))

    def head_times(chunks):
        block = jnp.concatenate([exps[i] for i in chunks], axis=0)
        for h in range(2):
            rows = lax.dot_general(
                block, weight[h * WIDE : (h + 1) * WIDE], (((1,), (1,)), ((), ())),
                preferred_element_type=F32,
            )
            for n, i in enumerate(chunks):
                row_sums[h, i] = rows[n * CHUNK : (n + 1) * CHUNK]
                row_out[h, i] = rows[n * CHUNK : (n + 1) * CHUNK].astype(BF16)

    head_times([4 * c + y_plus(i) for i in (0, 1, 3)])
    for copy in seq_copies:
        copy.wait_recv()
    stat_rep[x] = pack_stats(*merge_stats(stat_seq, SEQ)) + to_row(local_max, 3 * CHUNK)
    stat_copies = [
        send(STAT_REP + d - 1, stat_rep.at[x], stat_rep.at[x], at_x(d)) for d in (1, 2, 3)
    ]
    for copy in core_copies:
        copy.wait_recv()
    head_times([4 * (1 - c) + y_plus(i) for i in (0, 1, 3)])
    for copy in relays:
        copy.wait_recv()
    head_times([4 * c + y_plus(2), 4 * (1 - c) + y_plus(2)])
    rep_copies = [
        [
            send(
                ROW_REP + 3 * h + d - 1, row_out.at[h, pl.ds(2 * lax.rem(x + d, REP), 2)],
                row_in.at[h, d - 1], at_x(d),
            )
            for d in (1, 2, 3)
        ]
        for h in range(2)
    ]

    for copy in stat_copies:
        copy.wait_recv()
    total_max, total_sum, target_logit = merge_stats(stat_rep, REP)
    lane = iota((1, 128), 1)
    live = (lane < CHUNK) & (lane + first_slot < my_count)
    count_row = jnp.full((1, 128), my_count.astype(F32), F32)
    weight_row = jnp.where(live, jnp.full((1, 128), my_cot, F32) / count_row, 0.0)
    factor_row = jnp.zeros((1, 128), F32)
    for i in range(REP):
        there = jnp.exp(turn(stat_rep[i], 3 * CHUNK) - total_max) / total_sum
        factor = jnp.where(live, weight_row * there, 0.0)
        factor_row = factor_row + (turn(factor, 128 - i * CHUNK) if i else factor)
    at_target = jnp.where(
        live, weight_row * (jnp.exp(target_logit - total_max) / total_sum - 1.0), 0.0
    )
    row_loss = jnp.where(live, (jnp.log(total_sum) + total_max - target_logit) / count_row, 0.0)
    scales[my_chunk, 0:1] = factor_row
    scales[my_chunk, 1:2] = at_target + turn(row_loss, 128 - CHUNK)
    scale_copies = [
        send(SCALE + d - 1, scales.at[my_chunk], scales.at[my_chunk], {"vocab": lax.rem(v + d, 8)})
        for d in range(1, 8)
    ]
    for copy in scale_copies:
        copy.wait_recv()

    def slots_of_mine(part_of, first):
        return jnp.concatenate(
            [to_column(scales[2 * x + i, part_of : part_of + 1], CHUNK, first) for i in range(2)],
            axis=0,
        )

    slot_factors = [
        slots_of_mine(0, CHUNK * lax.rem(x + REP - d, REP)) for d in range(REP)
    ]
    slot_target = slots_of_mine(1, 0).astype(BF16).astype(F32)
    for copy in target_copies:
        copy.wait_recv()
    owns = []
    for h in range(2):
        column_sum = target_out[x, h].astype(F32)
        for i in range(3):
            column_sum = column_sum + target_in[i, h].astype(F32)
        owns.append(slot_target * column_sum + slot_factors[0] * row_sums[h, pl.ds(2 * x, 2)].reshape(SLOTS, WIDE))

    def scale_grads():
        for i in range(8):
            factor = to_column(scales[i, 0:1], CHUNK, CHUNK * x)
            at_own = to_column(scales[i, 1:2], CHUNK)
            values = exps[i].astype(F32) * factor
            grads[i] = jnp.where(column == target_cols[i], at_own, values).astype(BF16)

    def head_part(i):
        columns = pl.ds(i * 256, 256)
        tile = jnp.dot(
            picked_t[...], grads[:, :, columns].reshape(REP * SLOTS, 256), preferred_element_type=F32
        )
        head_out[:, columns] = tile.astype(BF16)
        copy = pltpu.make_async_copy(
            head_out.at[:, columns], head_hbm.at[:, columns], head_sem.at[i]
        )
        copy.start()
        return copy

    near_copies = []
    for h in range(2):
        for copy in rep_copies[h]:
            copy.wait_recv()
        for i in range(3):
            owns[h] = owns[h] + slot_factors[i + 1] * row_in[h, i].reshape(SLOTS, WIDE).astype(F32)
        near_out[h] = owns[h].astype(BF16)
        near_copies.append(send_near(ROW_NEAR + 4 * h, near_out.at[h], near_in.at[h]))
    scale_grads()
    head_copies = [head_part(0), head_part(1)]
    mine_rows = []
    class_copies = []
    for h in range(2):
        for copy in near_copies[h]:
            copy.wait_recv()
        own = owns[h]
        for i in range(3):
            own = own + near_in[h, i].astype(F32)
        mine = jnp.zeros((FOLD, WIDE), F32)
        for j in range(4):
            block = fold_rows(jnp.where(owner_col == cls + 4 * j, own, 0.0))
            class_out[h, j] = block.astype(BF16)
            mine = jnp.where(member == j, block, mine)
        mine_rows.append(mine)
        class_copies.append([
            send(
                ROW_CLASS + 3 * h + d - 1, class_out.at[h, lax.rem(member + d, 4)],
                class_in.at[h, d - 1], at_z(4 * d),
            )
            for d in (2, 1, 3)
        ])
    head_copies += [head_part(2), head_part(3), head_part(4)]
    for copy in started[: -2 * 3]:
        copy.wait_send()
    for q in range(REP):
        losses_ref[q] = jnp.sum(between(scales[2 * q, 1:2] + scales[2 * q + 1, 1:2], CHUNK))
    for copy in head_copies:
        copy.wait()
    put = jnp.where(put_at, 1.0, 0.0).astype(BF16)
    for h in range(2):
        for copy in class_copies[h]:
            copy.wait_recv()
        mine = mine_rows[h]
        for i in range(3):
            mine = mine + class_in[h, i].astype(F32)
        final = unfold_rows(mine.astype(BF16).astype(F32))
        final = jnp.where(owner_col == z, final, 0.0).astype(BF16)
        grad_ref[0, :, h * WIDE : (h + 1) * WIDE] = jnp.dot(
            put, final, preferred_element_type=F32
        ).astype(BF16)

    for copies in class_copies:
        for copy in copies:
            copy.wait_send()


def hand_over(
    head_in, hidden_in, losses_in, head_ref, hidden_ref, losses_ref,
    head, hidden, losses, in_sem, out_sem,
):
    rows = FEAT // 4
    moves = [(hidden_in, hidden, hidden_ref), (losses_in, losses, losses_ref)]
    for i in range(4):
        at = pl.ds(i * rows, rows)
        moves.append((head_in.at[at], head.at[at], head_ref.at[at]))
    loads = [pltpu.make_async_copy(m[0], m[1], in_sem.at[i]) for i, m in enumerate(moves)]
    stores = [pltpu.make_async_copy(m[1], m[2], out_sem.at[i]) for i, m in enumerate(moves)]
    for load in loads:
        load.start()
    for load, store in zip(loads, stores):
        load.wait()
        store.start()
    for store in stores:
        store.wait()


def shards(hidden, head_weight, positions, counts, targets, seq_cotangent):
    vmem = pl.BlockSpec(memory_space=pltpu.VMEM)
    smem = pl.BlockSpec(memory_space=pltpu.SMEM)
    hbm = pl.BlockSpec(memory_space=pltpu.HBM)
    shapes = (
        jax.ShapeDtypeStruct((FEAT, COLS), BF16),
        jax.ShapeDtypeStruct((1, TOK, FEAT), BF16),
        jax.ShapeDtypeStruct((REP,), F32),
    )
    limit = 60 * 1024 * 1024
    results = pl.pallas_call(
        kernel,
        out_shape=shapes,
        in_specs=[hbm] * 6,
        out_specs=(hbm, vmem, smem),
        scratch_shapes=[
            pltpu.SMEM((REP,), jnp.int32),
            pltpu.SMEM((REP,), F32),
            pltpu.VMEM((REP, SLOTS), jnp.int32),
            pltpu.VMEM((REP, SLOTS), jnp.int32),
            pltpu.VMEM((1, TOK, FEAT), BF16),
            pltpu.VMEM((FEAT, COLS), BF16),
            pltpu.VMEM((2, 4, FOLD, WIDE), BF16),
            pltpu.VMEM((2, SLOTS, WIDE), BF16),
            pltpu.VMEM((2, 3, SLOTS, WIDE), BF16),
            pltpu.VMEM((2, REP, SLOTS, WIDE), BF16),
            pltpu.VMEM((FEAT, REP * SLOTS), BF16),
            pltpu.VMEM((8, CHUNK, 1), jnp.int32),
            pltpu.VMEM((REP, 2, SLOTS, WIDE), BF16),
            pltpu.VMEM((3, 2, SLOTS, WIDE), BF16),
            pltpu.VMEM((2, 4, CHUNK, SPAN), F32),
            pltpu.VMEM((2, 4, CHUNK, SPAN), F32),
            pltpu.VMEM((2, 4, CHUNK, SPAN), F32),
            pltpu.VMEM((2, 2, HALF, SPAN), F32),
            pltpu.VMEM((2, 2, HALF, SPAN), F32),
            pltpu.VMEM((2, 2, HALF, SPAN), F32),
            pltpu.VMEM((2, 2, HALF, SPAN), F32),
            pltpu.VMEM((CHUNK, COLS), F32),
            pltpu.VMEM((SEQ, 1, 128), F32),
            pltpu.VMEM((REP, 1, 128), F32),
            pltpu.VMEM((2 * REP, 2, 128), F32),
            pltpu.VMEM((2 * REP, CHUNK, COLS), BF16),
            pltpu.VMEM((2 * REP, CHUNK, COLS), BF16),
            pltpu.VMEM((2, 2 * REP, CHUNK, WIDE), F32),
            pltpu.VMEM((2, 2 * REP, CHUNK, WIDE), BF16),
            pltpu.VMEM((2, 3, 2, CHUNK, WIDE), BF16),
            pltpu.VMEM((2, SLOTS, WIDE), BF16),
            pltpu.VMEM((2, 3, SLOTS, WIDE), BF16),
            pltpu.VMEM((2, 4, FOLD, WIDE), BF16),
            pltpu.VMEM((2, 3, FOLD, WIDE), BF16),
            pltpu.VMEM((FEAT, COLS), BF16),
            pltpu.SemaphoreType.DMA((MESSAGES,)),
            pltpu.SemaphoreType.DMA((MESSAGES,)),
            pltpu.SemaphoreType.DMA((6,)),
            pltpu.SemaphoreType.DMA((5,)),
        ],
        compiler_params=pltpu.CompilerParams(
            collective_id=0, has_side_effects=True, vmem_limit_bytes=limit
        ),
        cost_estimate=pl.CostEstimate(
            flops=6 * 256 * FEAT * COLS, bytes_accessed=4 * FEAT * COLS, transcendentals=64 * COLS
        ),
    )(counts, seq_cotangent, positions, targets, hidden, head_weight)
    return pl.pallas_call(
        hand_over,
        out_shape=shapes,
        in_specs=[hbm] * 3,
        out_specs=(hbm,) * 3,
        scratch_shapes=[
            pltpu.VMEM((FEAT, COLS), BF16),
            pltpu.VMEM((1, TOK, FEAT), BF16),
            pltpu.SMEM((REP,), F32),
            pltpu.SemaphoreType.DMA((6,)),
            pltpu.SemaphoreType.DMA((6,)),
        ],
        compiler_params=pltpu.CompilerParams(vmem_limit_bytes=limit),
    )(*results)


def solution(mesh):
    return jax.shard_map(
        shards,
        mesh=mesh,
        in_specs=(P("rep", "seq", "vocab"), P("vocab", ("seq", "rep")), P(), P(), P(), P()),
        out_specs=(P("vocab", ("seq", "rep")), P("rep", "seq", "vocab"), P()),
        check_vma=False,
    )
```

```python
import jax
import jax.numpy as jnp
from jax import lax
from jax.experimental import pallas as pl
from jax.experimental.pallas import tpu as pltpu
from jax.sharding import PartitionSpec as P

MESH = pl.DeviceIdType.MESH
F32 = jnp.float32
BF16 = jnp.bfloat16

SEQ = 16
REP = 4
SLOTS = 64
TOK = 64
FEAT = 512
COLS = 1280
FOLD = 16
CHUNK = 32
HALF = 16
WIDE = FEAT // 2
SPAN = COLS // 2

PICK_CLASS = 0
PICK_NEAR = 6
PICK_REP = 14
LOGIT_CORE = 20
LOGIT_Y = 28
STAT_SEQ = 40
STAT_REP = 55
GRAD_Y = 58
GRAD_CORE = 66
SCALE = 69
ROW_REP = 76
ROW_NEAR = 82
ROW_CLASS = 90
TARGET_REP = 96
MESSAGES = 99


def iota(shape, dim):
    return lax.broadcasted_iota(jnp.int32, shape, dim)


def to_column(row, rows, shift=0):
    shape = (rows, row.shape[1])
    at = iota(shape, 1) == iota(shape, 0) + shift
    return jnp.sum(jnp.where(at, row, 0.0), axis=1, keepdims=True)


def to_row(column, shift):
    shape = (CHUNK, 128)
    at = iota(shape, 1) == iota(shape, 0) + shift
    return jnp.sum(jnp.where(at, column, 0.0), axis=0, keepdims=True)


def turn(row, shift):
    return pltpu.roll(row, 128 - shift, 1)


def between(row, first):
    lane = iota((1, 128), 1)
    return jnp.where((lane >= first) & (lane < first + CHUNK), row, 0.0)


def merge_stats(ref, parts):
    rows = [ref[i] for i in range(parts)]
    row_max = rows[0]
    for row in rows[1:]:
        row_max = jnp.maximum(row_max, row)
    row_sum = jnp.zeros((1, 128), F32)
    row_target = jnp.zeros((1, 128), F32)
    for row in rows:
        row_sum = row_sum + turn(row, CHUNK) * jnp.exp(row - row_max)
        row_target = row_target + row
    return row_max, row_sum, turn(row_target, 2 * CHUNK)


def pack_stats(row_max, row_sum, row_target):
    return (
        between(row_max, 0)
        + between(turn(row_sum, 128 - CHUNK), CHUNK)
        + between(turn(row_target, 128 - 2 * CHUNK), 2 * CHUNK)
    )


def fold_rows(rows):
    return (rows[0:16] + rows[16:32]) + (rows[32:48] + rows[48:64])


def unfold_rows(rows):
    return jnp.concatenate([rows, rows, rows, rows], axis=0)


def kernel(
    counts_hbm, cot_hbm, positions_hbm, targets_hbm, hidden_hbm, weight_hbm,
    head_hbm, grad_ref, losses_ref,
    counts_ref, cot_ref, positions_ref, targets_ref, hidden_ref,
    weight, pick_class, pick_own, pick_near, picked, picked_t, target_cols, target_out, target_in,
    core_out, core_in, part, y_fwd, y_sum, y_direct, y_acc, logits_ref,
    stat_seq, stat_rep, scales, exps, grads,
    row_sums, row_out, row_in, near_out, near_in, class_out, class_in, head_out,
    send_sem, recv_sem, load_sem, head_sem,
):
    z = lax.axis_index("seq")
    v = lax.axis_index("vocab")
    x = lax.axis_index("rep")
    y = lax.div(v, 2)
    c = lax.rem(v, 2)
    cls = lax.rem(z, 4)
    member = lax.div(z, 4)

    def at_z(shift):
        return {"seq": lax.rem(z + shift + SEQ, SEQ)}

    def at_x(shift):
        return {"rep": lax.rem(x + shift, REP)}

    def y_plus(shift):
        return lax.rem(y + shift, 4)

    def at_y(shift):
        return {"vocab": y_plus(shift) * 2 + c}

    def across_y(shift):
        return {"vocab": y_plus(shift) * 2 + 1 - c}

    def load(number, src, dst):
        copy = pltpu.make_async_copy(src, dst, load_sem.at[number])
        copy.start()
        return copy

    loads = [
        load(0, positions_hbm, positions_ref),
        load(1, counts_hbm, counts_ref),
        load(2, hidden_hbm, hidden_ref),
        load(3, cot_hbm, cot_ref),
        load(4, targets_hbm, targets_ref),
        load(5, weight_hbm, weight),
    ]

    sibling = {"vocab": y * 2 + 1 - c}

    started = []

    def send(number, src, dst, device):
        copy = pltpu.make_async_remote_copy(
            src_ref=src,
            dst_ref=dst,
            send_sem=send_sem.at[number],
            recv_sem=recv_sem.at[number],
            device_id=device,
            device_id_type=MESH,
        )
        copy.start()
        started.append(copy)
        return copy

    barrier = pltpu.get_barrier_semaphore()
    friends = [at_z(s) for s in range(1, SEQ)] + [at_x(s) for s in (1, 2, 3)]
    friends += [{"vocab": lax.rem(v + s, 8)} for s in range(1, 8)]
    for friend in friends:
        pl.semaphore_signal(barrier, inc=1, device_id=friend, device_id_type=MESH)

    loads[0].wait()
    loads[1].wait()
    all_positions = positions_ref[...].astype(F32)
    position_row = jnp.sum(
        jnp.where(iota((REP, SLOTS), 0) == x, all_positions, 0.0), axis=0, keepdims=True
    )
    count = counts_ref[x]
    position_col = to_column(position_row, SLOTS).astype(jnp.int32)
    live_col = iota((SLOTS, 1), 0) < count
    owner_col = jnp.where(live_col, lax.div(position_col, TOK), -1)
    pick_at = (iota((SLOTS, TOK), 1) + z * TOK == position_col) & (iota((SLOTS, TOK), 0) < count)
    put_at = (iota((TOK, SLOTS), 0) + z * TOK == position_row.astype(jnp.int32)) & (
        iota((TOK, SLOTS), 1) < count
    )

    loads[2].wait()
    own_rows = jnp.dot(
        jnp.where(pick_at, 1.0, 0.0).astype(BF16), hidden_ref[0], preferred_element_type=F32
    )
    folded = fold_rows(own_rows).astype(BF16)
    for h in range(2):
        pick_class[h, member] = folded[:, h * WIDE : (h + 1) * WIDE]

    pl.semaphore_wait(barrier, len(friends))

    class_copies = [
        [
            send(
                PICK_CLASS + 3 * h + d - 1, pick_class.at[h, member], pick_class.at[h, member],
                at_z(4 * d),
            )
            for d in (2, 1, 3)
        ]
        for h in range(2)
    ]

    def send_near(number, src, dst):
        low, high = pl.ds(0, 32), pl.ds(32, 32)
        return [
            send(number + 2, src.at[low], dst.at[2, low], at_z(2)),
            send(number + 3, src.at[high], dst.at[2, high], at_z(-2)),
            send(number, src, dst.at[0], at_z(1)),
            send(number + 1, src, dst.at[1], at_z(-1)),
        ]

    loads[4].wait()
    all_targets = targets_ref[...].astype(F32)
    column = iota((CHUNK, COLS), 1) + (z * REP + x) * COLS
    for i in range(8):
        target_cols[i] = to_column(
            all_targets[i // 2 : i // 2 + 1], CHUNK, CHUNK * (i % 2)
        ).astype(jnp.int32)

    def head_at_targets(h):
        hot = [jnp.where(column == target_cols[i], 1.0, 0.0).astype(BF16) for i in range(8)]
        there = lax.dot_general(
            jnp.concatenate(hot, axis=0), weight[h * WIDE : (h + 1) * WIDE],
            (((1,), (1,)), ((), ())), preferred_element_type=F32,
        ).reshape(REP, SLOTS, WIDE)
        for q in range(REP):
            target_out[q, h] = there[q].astype(BF16)

    loads[5].wait()
    head_at_targets(0)

    totals = []
    near_copies = []
    for h in range(2):
        for copy in class_copies[h]:
            copy.wait_recv()
        total = jnp.zeros((SLOTS, WIDE), F32)
        for j in range(4):
            block = unfold_rows(pick_class[h, j].astype(F32))
            total = total + jnp.where(owner_col == cls + 4 * j, block, 0.0)
        pick_own[h] = total.astype(BF16)
        near_copies.append(send_near(PICK_NEAR + 4 * h, pick_own.at[h], pick_near.at[h]))
        totals.append(total)
    head_at_targets(1)
    rep_copies = []
    for h in range(2):
        for copy in near_copies[h]:
            copy.wait_recv()
        total = totals[h]
        for i in range(3):
            total = total + pick_near[h, i].astype(F32)
        picked[h, x] = total.astype(BF16)
        rep_copies.append([
            send(PICK_REP + 3 * h + d - 1, picked.at[h, x], picked.at[h, x], at_x(d))
            for d in (2, 1, 3)
        ])

    def partial_logits(h, core, k):
        rows = picked[h, pl.ds(2 * core, 2)].reshape(2 * SLOTS, WIDE)
        return jnp.dot(
            rows, weight[h * WIDE : (h + 1) * WIDE, k * SPAN : (k + 1) * SPAN],
            preferred_element_type=F32,
        ).reshape(4, CHUNK, SPAN)

    for copy in rep_copies[0]:
        copy.wait_recv()
    for k in range(2):
        core_out[k] = partial_logits(0, 1 - c, k)
        part[k] = partial_logits(0, c, k)
    for copy in rep_copies[1]:
        copy.wait_recv()
    order = (2, 1, 3, 0)
    core_copies = []
    for k in range(2):
        core_out[k] = core_out[k] + partial_logits(1, 1 - c, k)
        core_copies.append({
            s: send(
                LOGIT_CORE + 4 * k + s, core_out.at[k, y_plus(s)], core_in.at[k, y_plus(s)], sibling
            )
            for s in order
        })
    for k in range(2):
        part[k] = part[k] + partial_logits(1, c, k)
    target_copies = [
        send(
            TARGET_REP + d - 1, target_out.at[lax.rem(x + d, REP)], target_in.at[d - 1], at_x(d)
        )
        for d in (1, 2, 3)
    ]

    low, high = pl.ds(0, HALF), pl.ds(HALF, HALF)
    fwd_copies = []
    last_copies = []
    for s in order:
        for k in range(2):
            core_copies[k][s].wait_recv()
            at = y_plus(s)
            part[k, at] = part[k, at] + core_in[k, at]
            number = LOGIT_Y + 6 * k
            if s == 2:
                fwd_copies.append((
                    send(number, part.at[k, at, low], y_fwd.at[k, 0], at_y(1)),
                    send(number + 1, part.at[k, at, high], y_fwd.at[k, 1], at_y(3)),
                ))
            if s == 1:
                last_copies.append(
                    send(number + 2, part.at[k, at, high], y_direct.at[k, 1], at_y(1))
                )
            if s == 3:
                last_copies.append(
                    send(number + 3, part.at[k, at, low], y_direct.at[k, 0], at_y(3))
                )
    for k in range(2):
        number = LOGIT_Y + 6 * k
        fwd_copies[k][0].wait_recv()
        y_sum[k, 0] = y_fwd[k, 0] + part[k, y_plus(1), 0:HALF]
        last_copies.append(send(number + 4, y_sum.at[k, 0], y_acc.at[k, 0], at_y(1)))
        fwd_copies[k][1].wait_recv()
        y_sum[k, 1] = y_fwd[k, 1] + part[k, y_plus(3), HALF:CHUNK]
        last_copies.append(send(number + 5, y_sum.at[k, 1], y_acc.at[k, 1], at_y(3)))
    for h in range(2):
        picked_t[h * WIDE : (h + 1) * WIDE] = picked[h].reshape(REP * SLOTS, WIDE).T
    for copy in last_copies:
        copy.wait_recv()
    for k in range(2):
        columns = pl.ds(k * SPAN, SPAN)
        logits_ref[0:HALF, columns] = part[k, y, 0:HALF] + (y_direct[k, 0] + y_acc[k, 0])
        logits_ref[HALF:CHUNK, columns] = part[k, y, HALF:CHUNK] + (y_direct[k, 1] + y_acc[k, 1])

    loads[3].wait()
    my_seq = 2 * c + lax.div(y, 2)
    first_slot = lax.rem(y, 2) * CHUNK
    my_count = counts_ref[my_seq]
    my_cot = cot_ref[my_seq]
    my_chunk = 4 * c + y
    is_target = column == target_cols[my_chunk]
    logits = logits_ref[...]
    local_max = jnp.max(logits, axis=1, keepdims=True)
    exponent = jnp.exp(logits - local_max)

    exps[my_chunk] = jnp.where(is_target, 0.0, exponent).astype(BF16)
    mine = exps.at[my_chunk]
    before = exps.at[4 * c + y_plus(3)]
    after = exps.at[4 * c + y_plus(1)]
    up_low = send(GRAD_Y, mine.at[low], mine.at[low], at_y(1))
    down_high = send(GRAD_Y + 1, mine.at[high], mine.at[high], at_y(3))
    up_high = send(GRAD_Y + 2, mine.at[high], mine.at[high], at_y(1))
    down_low = send(GRAD_Y + 3, mine.at[low], mine.at[low], at_y(3))
    core_copies = [send(GRAD_CORE, mine, mine, sibling)]

    local_sum = jnp.sum(exponent, axis=1, keepdims=True)
    local_target = jnp.sum(jnp.where(is_target, logits, 0.0), axis=1, keepdims=True)
    max_row = to_row(local_max, 0)
    stat_seq[z] = max_row + to_row(local_sum, CHUNK) + to_row(local_target, 2 * CHUNK)
    seq_copies = [
        send(STAT_SEQ + d - 1, stat_seq.at[z], stat_seq.at[z], at_z(d))
        for d in (8, 7, 9, 6, 10, 5, 11, 4, 12, 3, 13, 2, 14, 1, 15)
    ]

    up_low.wait_recv()
    relays = [
        send(GRAD_Y + 4, before.at[low], before.at[low], at_y(1)),
        send(GRAD_Y + 5, before.at[low], before.at[low], across_y(1)),
    ]
    down_high.wait_recv()
    relays.append(send(GRAD_Y + 6, after.at[high], after.at[high], at_y(3)))
    relays.append(send(GRAD_Y + 7, after.at[high], after.at[high], across_y(3)))
    up_high.wait_recv()
    core_copies.append(send(GRAD_CORE + 1, before, before, sibling))
    down_low.wait_recv()
    core_copies.append(send(GRAD_CORE + 2, after, after, sibling))

    def head_times(h, chunks):
        block = jnp.concatenate([exps[i] for i in chunks], axis=0)
        rows = lax.dot_general(
            block, weight[h * WIDE : (h + 1) * WIDE], (((1,), (1,)), ((), ())),
            preferred_element_type=F32,
        )
        for n, i in enumerate(chunks):
            row_sums[h, i] = rows[n * CHUNK : (n + 1) * CHUNK]
            row_out[h, i] = rows[n * CHUNK : (n + 1) * CHUNK].astype(BF16)

    for h in range(2):
        head_times(h, [4 * c + y_plus(i) for i in (0, 1, 3)])
    for copy in seq_copies:
        copy.wait_recv()
    stat_rep[x] = pack_stats(*merge_stats(stat_seq, SEQ)) + to_row(local_max, 3 * CHUNK)
    stat_copies = [
        send(STAT_REP + d - 1, stat_rep.at[x], stat_rep.at[x], at_x(d)) for d in (1, 2, 3)
    ]
    for copy in core_copies:
        copy.wait_recv()
    for h in range(2):
        head_times(h, [4 * (1 - c) + y_plus(i) for i in (0, 1, 3)])
    for copy in relays:
        copy.wait_recv()
    rep_copies = []
    for h in range(2):
        head_times(h, [4 * c + y_plus(2), 4 * (1 - c) + y_plus(2)])
        rep_copies.append([
            send(
                ROW_REP + 3 * h + d - 1, row_out.at[h, pl.ds(2 * lax.rem(x + d, REP), 2)],
                row_in.at[h, d - 1], at_x(d),
            )
            for d in (2, 1, 3)
        ])

    for copy in stat_copies:
        copy.wait_recv()
    total_max, total_sum, target_logit = merge_stats(stat_rep, REP)
    lane = iota((1, 128), 1)
    live = (lane < CHUNK) & (lane + first_slot < my_count)
    count_row = jnp.full((1, 128), my_count.astype(F32), F32)
    weight_row = jnp.where(live, jnp.full((1, 128), my_cot, F32) / count_row, 0.0)
    factor_row = jnp.zeros((1, 128), F32)
    for i in range(REP):
        there = jnp.exp(turn(stat_rep[i], 3 * CHUNK) - total_max) / total_sum
        factor = jnp.where(live, weight_row * there, 0.0)
        factor_row = factor_row + (turn(factor, 128 - i * CHUNK) if i else factor)
    at_target = jnp.where(
        live, weight_row * (jnp.exp(target_logit - total_max) / total_sum - 1.0), 0.0
    )
    row_loss = jnp.where(live, (jnp.log(total_sum) + total_max - target_logit) / count_row, 0.0)
    scales[my_chunk, 0:1] = factor_row
    scales[my_chunk, 1:2] = at_target + turn(row_loss, 128 - CHUNK)
    scale_copies = [
        send(SCALE + d - 1, scales.at[my_chunk], scales.at[my_chunk], {"vocab": lax.rem(v + d, 8)})
        for d in range(1, 8)
    ]
    for copy in scale_copies:
        copy.wait_recv()

    def slots_of_mine(part_of, first):
        return jnp.concatenate(
            [to_column(scales[2 * x + i, part_of : part_of + 1], CHUNK, first) for i in range(2)],
            axis=0,
        )

    slot_factors = [
        slots_of_mine(0, CHUNK * lax.rem(x + REP - d, REP)) for d in range(REP)
    ]
    slot_target = slots_of_mine(1, 0).astype(BF16).astype(F32)
    for copy in target_copies:
        copy.wait_recv()
    owns = []
    for h in range(2):
        column_sum = target_out[x, h].astype(F32)
        for i in range(3):
            column_sum = column_sum + target_in[i, h].astype(F32)
        owns.append(slot_target * column_sum + slot_factors[0] * row_sums[h, pl.ds(2 * x, 2)].reshape(SLOTS, WIDE))

    def scale_grads():
        for i in range(8):
            factor = to_column(scales[i, 0:1], CHUNK, CHUNK * x)
            at_own = to_column(scales[i, 1:2], CHUNK)
            values = exps[i].astype(F32) * factor
            grads[i] = jnp.where(column == target_cols[i], at_own, values).astype(BF16)

    def head_part(i):
        columns = pl.ds(i * 256, 256)
        tile = jnp.dot(
            picked_t[...], grads[:, :, columns].reshape(REP * SLOTS, 256), preferred_element_type=F32
        )
        head_out[:, columns] = tile.astype(BF16)
        copy = pltpu.make_async_copy(
            head_out.at[:, columns], head_hbm.at[:, columns], head_sem.at[i]
        )
        copy.start()
        return copy

    near_copies = []
    for h in range(2):
        for copy in rep_copies[h]:
            copy.wait_recv()
        for i in range(3):
            owns[h] = owns[h] + slot_factors[i + 1] * row_in[h, i].reshape(SLOTS, WIDE).astype(F32)
        near_out[h] = owns[h].astype(BF16)
        near_copies.append(send_near(ROW_NEAR + 4 * h, near_out.at[h], near_in.at[h]))
    scale_grads()
    head_copies = [head_part(0), head_part(1)]
    mine_rows = []
    class_copies = []
    for h in range(2):
        for copy in near_copies[h]:
            copy.wait_recv()
        own = owns[h]
        for i in range(3):
            own = own + near_in[h, i].astype(F32)
        mine = jnp.zeros((FOLD, WIDE), F32)
        for j in range(4):
            block = fold_rows(jnp.where(owner_col == cls + 4 * j, own, 0.0))
            class_out[h, j] = block.astype(BF16)
            mine = jnp.where(member == j, block, mine)
        mine_rows.append(mine)
        class_copies.append([
            send(
                ROW_CLASS + 3 * h + d - 1, class_out.at[h, lax.rem(member + d, 4)],
                class_in.at[h, d - 1], at_z(4 * d),
            )
            for d in (2, 1, 3)
        ])
    head_copies += [head_part(2), head_part(3), head_part(4)]
    for copy in started[: -2 * 3]:
        copy.wait_send()
    for q in range(REP):
        losses_ref[q] = jnp.sum(between(scales[2 * q, 1:2] + scales[2 * q + 1, 1:2], CHUNK))
    for copy in head_copies:
        copy.wait()
    put = jnp.where(put_at, 1.0, 0.0).astype(BF16)
    for h in range(2):
        for copy in class_copies[h]:
            copy.wait_recv()
        mine = mine_rows[h]
        for i in range(3):
            mine = mine + class_in[h, i].astype(F32)
        final = unfold_rows(mine.astype(BF16).astype(F32))
        final = jnp.where(owner_col == z, final, 0.0).astype(BF16)
        grad_ref[0, :, h * WIDE : (h + 1) * WIDE] = jnp.dot(
            put, final, preferred_element_type=F32
        ).astype(BF16)

    for copies in class_copies:
        for copy in copies:
            copy.wait_send()


def hand_over(
    head_in, hidden_in, losses_in, head_ref, hidden_ref, losses_ref,
    head, hidden, losses, in_sem, out_sem,
):
    rows = FEAT // 4
    moves = [(hidden_in, hidden, hidden_ref), (losses_in, losses, losses_ref)]
    for i in range(4):
        at = pl.ds(i * rows, rows)
        moves.append((head_in.at[at], head.at[at], head_ref.at[at]))
    loads = [pltpu.make_async_copy(m[0], m[1], in_sem.at[i]) for i, m in enumerate(moves)]
    stores = [pltpu.make_async_copy(m[1], m[2], out_sem.at[i]) for i, m in enumerate(moves)]
    for load in loads:
        load.start()
    for load, store in zip(loads, stores):
        load.wait()
        store.start()
    for store in stores:
        store.wait()


def shards(hidden, head_weight, positions, counts, targets, seq_cotangent):
    vmem = pl.BlockSpec(memory_space=pltpu.VMEM)
    smem = pl.BlockSpec(memory_space=pltpu.SMEM)
    hbm = pl.BlockSpec(memory_space=pltpu.HBM)
    shapes = (
        jax.ShapeDtypeStruct((FEAT, COLS), BF16),
        jax.ShapeDtypeStruct((1, TOK, FEAT), BF16),
        jax.ShapeDtypeStruct((REP,), F32),
    )
    limit = 60 * 1024 * 1024
    results = pl.pallas_call(
        kernel,
        out_shape=shapes,
        in_specs=[hbm] * 6,
        out_specs=(hbm, vmem, smem),
        scratch_shapes=[
            pltpu.SMEM((REP,), jnp.int32),
            pltpu.SMEM((REP,), F32),
            pltpu.VMEM((REP, SLOTS), jnp.int32),
            pltpu.VMEM((REP, SLOTS), jnp.int32),
            pltpu.VMEM((1, TOK, FEAT), BF16),
            pltpu.VMEM((FEAT, COLS), BF16),
            pltpu.VMEM((2, 4, FOLD, WIDE), BF16),
            pltpu.VMEM((2, SLOTS, WIDE), BF16),
            pltpu.VMEM((2, 3, SLOTS, WIDE), BF16),
            pltpu.VMEM((2, REP, SLOTS, WIDE), BF16),
            pltpu.VMEM((FEAT, REP * SLOTS), BF16),
            pltpu.VMEM((8, CHUNK, 1), jnp.int32),
            pltpu.VMEM((REP, 2, SLOTS, WIDE), BF16),
            pltpu.VMEM((3, 2, SLOTS, WIDE), BF16),
            pltpu.VMEM((2, 4, CHUNK, SPAN), F32),
            pltpu.VMEM((2, 4, CHUNK, SPAN), F32),
            pltpu.VMEM((2, 4, CHUNK, SPAN), F32),
            pltpu.VMEM((2, 2, HALF, SPAN), F32),
            pltpu.VMEM((2, 2, HALF, SPAN), F32),
            pltpu.VMEM((2, 2, HALF, SPAN), F32),
            pltpu.VMEM((2, 2, HALF, SPAN), F32),
            pltpu.VMEM((CHUNK, COLS), F32),
            pltpu.VMEM((SEQ, 1, 128), F32),
            pltpu.VMEM((REP, 1, 128), F32),
            pltpu.VMEM((2 * REP, 2, 128), F32),
            pltpu.VMEM((2 * REP, CHUNK, COLS), BF16),
            pltpu.VMEM((2 * REP, CHUNK, COLS), BF16),
            pltpu.VMEM((2, 2 * REP, CHUNK, WIDE), F32),
            pltpu.VMEM((2, 2 * REP, CHUNK, WIDE), BF16),
            pltpu.VMEM((2, 3, 2, CHUNK, WIDE), BF16),
            pltpu.VMEM((2, SLOTS, WIDE), BF16),
            pltpu.VMEM((2, 3, SLOTS, WIDE), BF16),
            pltpu.VMEM((2, 4, FOLD, WIDE), BF16),
            pltpu.VMEM((2, 3, FOLD, WIDE), BF16),
            pltpu.VMEM((FEAT, COLS), BF16),
            pltpu.SemaphoreType.DMA((MESSAGES,)),
            pltpu.SemaphoreType.DMA((MESSAGES,)),
            pltpu.SemaphoreType.DMA((6,)),
            pltpu.SemaphoreType.DMA((5,)),
        ],
        compiler_params=pltpu.CompilerParams(
            collective_id=0, has_side_effects=True, vmem_limit_bytes=limit
        ),
        cost_estimate=pl.CostEstimate(
            flops=6 * 256 * FEAT * COLS, bytes_accessed=4 * FEAT * COLS, transcendentals=64 * COLS
        ),
    )(counts, seq_cotangent, positions, targets, hidden, head_weight)
    return pl.pallas_call(
        hand_over,
        out_shape=shapes,
        in_specs=[hbm] * 3,
        out_specs=(hbm,) * 3,
        scratch_shapes=[
            pltpu.VMEM((FEAT, COLS), BF16),
            pltpu.VMEM((1, TOK, FEAT), BF16),
            pltpu.SMEM((REP,), F32),
            pltpu.SemaphoreType.DMA((6,)),
            pltpu.SemaphoreType.DMA((6,)),
        ],
        compiler_params=pltpu.CompilerParams(vmem_limit_bytes=limit),
    )(*results)


def solution(mesh):
    return jax.shard_map(
        shards,
        mesh=mesh,
        in_specs=(P("rep", "seq", "vocab"), P("vocab", ("seq", "rep")), P(), P(), P(), P()),
        out_specs=(P("vocab", ("seq", "rep")), P("rep", "seq", "vocab"), P()),
        check_vma=False,
    )
```

```python
import jax
import jax.numpy as jnp
from jax import lax
from jax.experimental import pallas as pl
from jax.experimental.pallas import tpu as pltpu
from jax.sharding import PartitionSpec as P

MESH = pl.DeviceIdType.MESH
F32 = jnp.float32
BF16 = jnp.bfloat16

SEQ = 16
REP = 4
SLOTS = 64
TOK = 64
FEAT = 512
COLS = 1280
FOLD = 16
CHUNK = 32
HALF = 16
WIDE = FEAT // 2
SPAN = COLS // 2

PICK_CLASS = 0
PICK_NEAR = 6
PICK_REP = 14
LOGIT_CORE = 20
LOGIT_Y = 28
STAT_SEQ = 40
STAT_REP = 55
GRAD_Y = 58
GRAD_CORE = 66
SCALE = 69
ROW_REP = 76
ROW_NEAR = 82
ROW_CLASS = 90
TARGET_REP = 96
MESSAGES = 99


def iota(shape, dim):
    return lax.broadcasted_iota(jnp.int32, shape, dim)


def to_column(row, rows, shift=0):
    shape = (rows, row.shape[1])
    at = iota(shape, 1) == iota(shape, 0) + shift
    return jnp.sum(jnp.where(at, row, 0.0), axis=1, keepdims=True)


def to_row(column, shift):
    shape = (CHUNK, 128)
    at = iota(shape, 1) == iota(shape, 0) + shift
    return jnp.sum(jnp.where(at, column, 0.0), axis=0, keepdims=True)


def turn(row, shift):
    return pltpu.roll(row, 128 - shift, 1)


def between(row, first):
    lane = iota((1, 128), 1)
    return jnp.where((lane >= first) & (lane < first + CHUNK), row, 0.0)


def merge_stats(ref, parts):
    rows = [ref[i] for i in range(parts)]
    row_max = rows[0]
    for row in rows[1:]:
        row_max = jnp.maximum(row_max, row)
    row_sum = jnp.zeros((1, 128), F32)
    row_target = jnp.zeros((1, 128), F32)
    for row in rows:
        row_sum = row_sum + turn(row, CHUNK) * jnp.exp(row - row_max)
        row_target = row_target + row
    return row_max, row_sum, turn(row_target, 2 * CHUNK)


def pack_stats(row_max, row_sum, row_target):
    return (
        between(row_max, 0)
        + between(turn(row_sum, 128 - CHUNK), CHUNK)
        + between(turn(row_target, 128 - 2 * CHUNK), 2 * CHUNK)
    )


def fold_rows(rows):
    return (rows[0:16] + rows[16:32]) + (rows[32:48] + rows[48:64])


def unfold_rows(rows):
    return jnp.concatenate([rows, rows, rows, rows], axis=0)


def kernel(
    counts_hbm, cot_hbm, positions_hbm, targets_hbm, hidden_hbm, weight_hbm,
    head_hbm, grad_ref, losses_ref,
    counts_ref, cot_ref, positions_ref, targets_ref, hidden_ref,
    weight, pick_class, pick_own, pick_near, picked, picked_t, target_cols, target_out, target_in,
    core_out, core_in, part, y_fwd, y_sum, y_direct, y_acc, logits_ref,
    stat_seq, stat_rep, scales, exps, grads,
    row_sums, row_out, row_in, near_out, near_in, class_out, class_in, head_out,
    send_sem, recv_sem, load_sem, head_sem,
):
    z = lax.axis_index("seq")
    v = lax.axis_index("vocab")
    x = lax.axis_index("rep")
    y = lax.div(v, 2)
    c = lax.rem(v, 2)
    cls = lax.rem(z, 4)
    member = lax.div(z, 4)

    def at_z(shift):
        return {"seq": lax.rem(z + shift + SEQ, SEQ)}

    def at_x(shift):
        return {"rep": lax.rem(x + shift, REP)}

    def y_plus(shift):
        return lax.rem(y + shift, 4)

    def at_y(shift):
        return {"vocab": y_plus(shift) * 2 + c}

    def across_y(shift):
        return {"vocab": y_plus(shift) * 2 + 1 - c}

    def load(number, src, dst):
        copy = pltpu.make_async_copy(src, dst, load_sem.at[number])
        copy.start()
        return copy

    loads = [
        load(0, positions_hbm, positions_ref),
        load(1, counts_hbm, counts_ref),
        load(2, hidden_hbm, hidden_ref),
        load(3, cot_hbm, cot_ref),
        load(4, targets_hbm, targets_ref),
        load(5, weight_hbm, weight),
    ]

    sibling = {"vocab": y * 2 + 1 - c}

    started = []

    def send(number, src, dst, device):
        copy = pltpu.make_async_remote_copy(
            src_ref=src,
            dst_ref=dst,
            send_sem=send_sem.at[number],
            recv_sem=recv_sem.at[number],
            device_id=device,
            device_id_type=MESH,
        )
        copy.start()
        started.append(copy)
        return copy

    barrier = pltpu.get_barrier_semaphore()
    friends = [at_z(s) for s in range(1, SEQ)] + [at_x(s) for s in (1, 2, 3)]
    friends += [{"vocab": lax.rem(v + s, 8)} for s in range(1, 8)]
    for friend in friends:
        pl.semaphore_signal(barrier, inc=1, device_id=friend, device_id_type=MESH)

    loads[0].wait()
    loads[1].wait()
    all_positions = positions_ref[...].astype(F32)
    position_row = jnp.sum(
        jnp.where(iota((REP, SLOTS), 0) == x, all_positions, 0.0), axis=0, keepdims=True
    )
    count = counts_ref[x]
    position_col = to_column(position_row, SLOTS).astype(jnp.int32)
    live_col = iota((SLOTS, 1), 0) < count
    owner_col = jnp.where(live_col, lax.div(position_col, TOK), -1)
    pick_at = (iota((SLOTS, TOK), 1) + z * TOK == position_col) & (iota((SLOTS, TOK), 0) < count)
    put_at = (iota((TOK, SLOTS), 0) + z * TOK == position_row.astype(jnp.int32)) & (
        iota((TOK, SLOTS), 1) < count
    )

    loads[2].wait()
    own_rows = jnp.dot(
        jnp.where(pick_at, 1.0, 0.0).astype(BF16), hidden_ref[0], preferred_element_type=F32
    )
    folded = fold_rows(own_rows).astype(BF16)
    for h in range(2):
        pick_class[h, member] = folded[:, h * WIDE : (h + 1) * WIDE]

    pl.semaphore_wait(barrier, len(friends))

    class_copies = [
        [
            send(
                PICK_CLASS + 3 * h + d - 1, pick_class.at[h, member], pick_class.at[h, member],
                at_z(4 * d),
            )
            for d in (2, 1, 3)
        ]
        for h in range(2)
    ]

    def send_near(number, src, dst):
        low, high = pl.ds(0, 32), pl.ds(32, 32)
        return [
            send(number + 2, src.at[low], dst.at[2, low], at_z(2)),
            send(number + 3, src.at[high], dst.at[2, high], at_z(-2)),
            send(number, src, dst.at[0], at_z(1)),
            send(number + 1, src, dst.at[1], at_z(-1)),
        ]

    loads[4].wait()
    all_targets = targets_ref[...].astype(F32)
    column = iota((CHUNK, COLS), 1) + (z * REP + x) * COLS
    for i in range(8):
        target_cols[i] = to_column(
            all_targets[i // 2 : i // 2 + 1], CHUNK, CHUNK * (i % 2)
        ).astype(jnp.int32)

    def head_at_targets(h):
        hot = [jnp.where(column == target_cols[i], 1.0, 0.0).astype(BF16) for i in range(8)]
        there = lax.dot_general(
            jnp.concatenate(hot, axis=0), weight[h * WIDE : (h + 1) * WIDE],
            (((1,), (1,)), ((), ())), preferred_element_type=F32,
        ).reshape(REP, SLOTS, WIDE)
        for q in range(REP):
            target_out[q, h] = there[q].astype(BF16)

    loads[5].wait()
    head_at_targets(0)

    totals = []
    near_copies = []
    for h in range(2):
        for copy in class_copies[h]:
            copy.wait_recv()
        total = jnp.zeros((SLOTS, WIDE), F32)
        for j in range(4):
            block = unfold_rows(pick_class[h, j].astype(F32))
            total = total + jnp.where(owner_col == cls + 4 * j, block, 0.0)
        pick_own[h] = total.astype(BF16)
        near_copies.append(send_near(PICK_NEAR + 4 * h, pick_own.at[h], pick_near.at[h]))
        totals.append(total)
    head_at_targets(1)
    rep_copies = []
    for h in range(2):
        for copy in near_copies[h]:
            copy.wait_recv()
        total = totals[h]
        for i in range(3):
            total = total + pick_near[h, i].astype(F32)
        picked[h, x] = total.astype(BF16)
        rep_copies.append([
            send(PICK_REP + 3 * h + d - 1, picked.at[h, x], picked.at[h, x], at_x(d))
            for d in (2, 1, 3)
        ])

    gathered = len(started)

    def partial_logits(h, core, k):
        rows = picked[h, pl.ds(2 * core, 2)].reshape(2 * SLOTS, WIDE)
        return jnp.dot(
            rows, weight[h * WIDE : (h + 1) * WIDE, k * SPAN : (k + 1) * SPAN],
            preferred_element_type=F32,
        ).reshape(4, CHUNK, SPAN)

    for copy in rep_copies[0]:
        copy.wait_recv()
    for k in range(2):
        core_out[k] = partial_logits(0, 1 - c, k)
        part[k] = partial_logits(0, c, k)
    for copy in rep_copies[1]:
        copy.wait_recv()
    order = (2, 1, 3, 0)
    core_copies = []
    for k in range(2):
        core_out[k] = core_out[k] + partial_logits(1, 1 - c, k)
        core_copies.append({
            s: send(
                LOGIT_CORE + 4 * k + s, core_out.at[k, y_plus(s)], core_in.at[k, y_plus(s)], sibling
            )
            for s in order
        })
    for k in range(2):
        part[k] = part[k] + partial_logits(1, c, k)
    target_copies = [
        send(
            TARGET_REP + d - 1, target_out.at[lax.rem(x + d, REP)], target_in.at[d - 1], at_x(d)
        )
        for d in (1, 2, 3)
    ]

    low, high = pl.ds(0, HALF), pl.ds(HALF, HALF)
    fwd_copies = []
    last_copies = []
    for s in order:
        for k in range(2):
            core_copies[k][s].wait_recv()
            at = y_plus(s)
            part[k, at] = part[k, at] + core_in[k, at]
            number = LOGIT_Y + 6 * k
            if s == 2:
                fwd_copies.append((
                    send(number, part.at[k, at, low], y_fwd.at[k, 0], at_y(1)),
                    send(number + 1, part.at[k, at, high], y_fwd.at[k, 1], at_y(3)),
                ))
            if s == 1:
                last_copies.append(
                    send(number + 2, part.at[k, at, high], y_direct.at[k, 1], at_y(1))
                )
            if s == 3:
                last_copies.append(
                    send(number + 3, part.at[k, at, low], y_direct.at[k, 0], at_y(3))
                )
    for k in range(2):
        number = LOGIT_Y + 6 * k
        fwd_copies[k][0].wait_recv()
        y_sum[k, 0] = y_fwd[k, 0] + part[k, y_plus(1), 0:HALF]
        last_copies.append(send(number + 4, y_sum.at[k, 0], y_acc.at[k, 0], at_y(1)))
        fwd_copies[k][1].wait_recv()
        y_sum[k, 1] = y_fwd[k, 1] + part[k, y_plus(3), HALF:CHUNK]
        last_copies.append(send(number + 5, y_sum.at[k, 1], y_acc.at[k, 1], at_y(3)))
    for h in range(2):
        picked_t[h * WIDE : (h + 1) * WIDE] = picked[h].reshape(REP * SLOTS, WIDE).T
    for copy in started[:gathered]:
        copy.wait_send()
    for copy in last_copies:
        copy.wait_recv()
    for k in range(2):
        columns = pl.ds(k * SPAN, SPAN)
        logits_ref[0:HALF, columns] = part[k, y, 0:HALF] + (y_direct[k, 0] + y_acc[k, 0])
        logits_ref[HALF:CHUNK, columns] = part[k, y, HALF:CHUNK] + (y_direct[k, 1] + y_acc[k, 1])

    loads[3].wait()
    my_seq = 2 * c + lax.div(y, 2)
    first_slot = lax.rem(y, 2) * CHUNK
    my_count = counts_ref[my_seq]
    my_cot = cot_ref[my_seq]
    my_chunk = 4 * c + y
    is_target = column == target_cols[my_chunk]
    logits = logits_ref[...]
    local_max = jnp.max(logits, axis=1, keepdims=True)
    exponent = jnp.exp(logits - local_max)

    exps[my_chunk] = jnp.where(is_target, 0.0, exponent).astype(BF16)
    mine = exps.at[my_chunk]
    before = exps.at[4 * c + y_plus(3)]
    after = exps.at[4 * c + y_plus(1)]
    up_low = send(GRAD_Y, mine.at[low], mine.at[low], at_y(1))
    down_high = send(GRAD_Y + 1, mine.at[high], mine.at[high], at_y(3))
    up_high = send(GRAD_Y + 2, mine.at[high], mine.at[high], at_y(1))
    down_low = send(GRAD_Y + 3, mine.at[low], mine.at[low], at_y(3))
    core_copies = [send(GRAD_CORE, mine, mine, sibling)]

    local_sum = jnp.sum(exponent, axis=1, keepdims=True)
    local_target = jnp.sum(jnp.where(is_target, logits, 0.0), axis=1, keepdims=True)
    max_row = to_row(local_max, 0)
    stat_seq[z] = max_row + to_row(local_sum, CHUNK) + to_row(local_target, 2 * CHUNK)
    seq_copies = [
        send(STAT_SEQ + d - 1, stat_seq.at[z], stat_seq.at[z], at_z(d))
        for d in (8, 7, 9, 6, 10, 5, 11, 4, 12, 3, 13, 2, 14, 1, 15)
    ]

    up_low.wait_recv()
    relays = [
        send(GRAD_Y + 4, before.at[low], before.at[low], at_y(1)),
        send(GRAD_Y + 5, before.at[low], before.at[low], across_y(1)),
    ]
    down_high.wait_recv()
    relays.append(send(GRAD_Y + 6, after.at[high], after.at[high], at_y(3)))
    relays.append(send(GRAD_Y + 7, after.at[high], after.at[high], across_y(3)))
    up_high.wait_recv()
    core_copies.append(send(GRAD_CORE + 1, before, before, sibling))
    down_low.wait_recv()
    core_copies.append(send(GRAD_CORE + 2, after, after, sibling))

    def head_times(h, chunks):
        block = jnp.concatenate([exps[i] for i in chunks], axis=0)
        rows = lax.dot_general(
            block, weight[h * WIDE : (h + 1) * WIDE], (((1,), (1,)), ((), ())),
            preferred_element_type=F32,
        )
        for n, i in enumerate(chunks):
            row_sums[h, i] = rows[n * CHUNK : (n + 1) * CHUNK]
            row_out[h, i] = rows[n * CHUNK : (n + 1) * CHUNK].astype(BF16)

    for h in range(2):
        head_times(h, [4 * c + y_plus(i) for i in (0, 1, 3)])
    for copy in seq_copies:
        copy.wait_recv()
    stat_rep[x] = pack_stats(*merge_stats(stat_seq, SEQ)) + to_row(local_max, 3 * CHUNK)
    stat_copies = [
        send(STAT_REP + d - 1, stat_rep.at[x], stat_rep.at[x], at_x(d)) for d in (2, 1, 3)
    ]
    for copy in core_copies:
        copy.wait_recv()
    for h in range(2):
        head_times(h, [4 * (1 - c) + y_plus(i) for i in (0, 1, 3)])
    for copy in relays:
        copy.wait_recv()
    rep_copies = []
    for h in range(2):
        head_times(h, [4 * c + y_plus(2), 4 * (1 - c) + y_plus(2)])
        rep_copies.append([
            send(
                ROW_REP + 3 * h + d - 1, row_out.at[h, pl.ds(2 * lax.rem(x + d, REP), 2)],
                row_in.at[h, d - 1], at_x(d),
            )
            for d in (2, 1, 3)
        ])

    for copy in stat_copies:
        copy.wait_recv()
    total_max, total_sum, target_logit = merge_stats(stat_rep, REP)
    lane = iota((1, 128), 1)
    live = (lane < CHUNK) & (lane + first_slot < my_count)
    count_row = jnp.full((1, 128), my_count.astype(F32), F32)
    weight_row = jnp.where(live, jnp.full((1, 128), my_cot, F32) / count_row, 0.0)
    factor_row = jnp.zeros((1, 128), F32)
    for i in range(REP):
        there = jnp.exp(turn(stat_rep[i], 3 * CHUNK) - total_max) / total_sum
        factor = jnp.where(live, weight_row * there, 0.0)
        factor_row = factor_row + (turn(factor, 128 - i * CHUNK) if i else factor)
    at_target = jnp.where(
        live, weight_row * (jnp.exp(target_logit - total_max) / total_sum - 1.0), 0.0
    )
    row_loss = jnp.where(live, (jnp.log(total_sum) + total_max - target_logit) / count_row, 0.0)
    scales[my_chunk, 0:1] = factor_row
    scales[my_chunk, 1:2] = at_target + turn(row_loss, 128 - CHUNK)
    scale_copies = [
        send(SCALE + d - 1, scales.at[my_chunk], scales.at[my_chunk], {"vocab": lax.rem(v + d, 8)})
        for d in range(1, 8)
    ]
    for copy in scale_copies:
        copy.wait_recv()

    def slots_of_mine(part_of, first):
        return jnp.concatenate(
            [to_column(scales[2 * x + i, part_of : part_of + 1], CHUNK, first) for i in range(2)],
            axis=0,
        )

    slot_factors = [
        slots_of_mine(0, CHUNK * lax.rem(x + REP - d, REP)) for d in range(REP)
    ]
    slot_target = slots_of_mine(1, 0).astype(BF16).astype(F32)
    for copy in target_copies:
        copy.wait_recv()
    owns = []
    for h in range(2):
        column_sum = target_out[x, h].astype(F32)
        for i in range(3):
            column_sum = column_sum + target_in[i, h].astype(F32)
        owns.append(slot_target * column_sum + slot_factors[0] * row_sums[h, pl.ds(2 * x, 2)].reshape(SLOTS, WIDE))

    def scale_grads():
        for i in range(8):
            factor = to_column(scales[i, 0:1], CHUNK, CHUNK * x)
            at_own = to_column(scales[i, 1:2], CHUNK)
            values = exps[i].astype(F32) * factor
            grads[i] = jnp.where(column == target_cols[i], at_own, values).astype(BF16)

    def head_part(i):
        columns = pl.ds(i * 256, 256)
        tile = jnp.dot(
            picked_t[...], grads[:, :, columns].reshape(REP * SLOTS, 256), preferred_element_type=F32
        )
        head_out[:, columns] = tile.astype(BF16)
        copy = pltpu.make_async_copy(
            head_out.at[:, columns], head_hbm.at[:, columns], head_sem.at[i]
        )
        copy.start()
        return copy

    near_copies = []
    for h in range(2):
        for copy in rep_copies[h]:
            copy.wait_recv()
        for i in range(3):
            owns[h] = owns[h] + slot_factors[i + 1] * row_in[h, i].reshape(SLOTS, WIDE).astype(F32)
        near_out[h] = owns[h].astype(BF16)
        near_copies.append(send_near(ROW_NEAR + 4 * h, near_out.at[h], near_in.at[h]))
    scale_grads()
    mine_rows = []
    class_copies = []
    for h in range(2):
        for copy in near_copies[h]:
            copy.wait_recv()
        own = owns[h]
        for i in range(3):
            own = own + near_in[h, i].astype(F32)
        mine = jnp.zeros((FOLD, WIDE), F32)
        for j in range(4):
            block = fold_rows(jnp.where(owner_col == cls + 4 * j, own, 0.0))
            class_out[h, j] = block.astype(BF16)
            mine = jnp.where(member == j, block, mine)
        mine_rows.append(mine)
        class_copies.append([
            send(
                ROW_CLASS + 3 * h + d - 1, class_out.at[h, lax.rem(member + d, 4)],
                class_in.at[h, d - 1], at_z(4 * d),
            )
            for d in (2, 1, 3)
        ])
    head_copies = [head_part(i) for i in range(5)]
    for copy in started[gathered : -2 * 3]:
        copy.wait_send()
    for q in range(REP):
        losses_ref[q] = jnp.sum(between(scales[2 * q, 1:2] + scales[2 * q + 1, 1:2], CHUNK))
    for copy in head_copies:
        copy.wait()
    put = jnp.where(put_at, 1.0, 0.0).astype(BF16)
    for h in range(2):
        for copy in class_copies[h]:
            copy.wait_recv()
        mine = mine_rows[h]
        for i in range(3):
            mine = mine + class_in[h, i].astype(F32)
        final = unfold_rows(mine.astype(BF16).astype(F32))
        final = jnp.where(owner_col == z, final, 0.0).astype(BF16)
        grad_ref[0, :, h * WIDE : (h + 1) * WIDE] = jnp.dot(
            put, final, preferred_element_type=F32
        ).astype(BF16)

    for copies in class_copies:
        for copy in copies:
            copy.wait_send()


def hand_over(
    head_in, hidden_in, losses_in, head_ref, hidden_ref, losses_ref,
    head, hidden, losses, in_sem, out_sem,
):
    rows = FEAT // 8
    moves = [(hidden_in, hidden, hidden_ref), (losses_in, losses, losses_ref)]
    for i in range(8):
        at = pl.ds(i * rows, rows)
        moves.append((head_in.at[at], head.at[at], head_ref.at[at]))
    loads = [pltpu.make_async_copy(m[0], m[1], in_sem.at[i]) for i, m in enumerate(moves)]
    stores = [pltpu.make_async_copy(m[1], m[2], out_sem.at[i]) for i, m in enumerate(moves)]
    for load in loads:
        load.start()
    for load, store in zip(loads, stores):
        load.wait()
        store.start()
    for store in stores:
        store.wait()


def shards(hidden, head_weight, positions, counts, targets, seq_cotangent):
    vmem = pl.BlockSpec(memory_space=pltpu.VMEM)
    smem = pl.BlockSpec(memory_space=pltpu.SMEM)
    hbm = pl.BlockSpec(memory_space=pltpu.HBM)
    shapes = (
        jax.ShapeDtypeStruct((FEAT, COLS), BF16),
        jax.ShapeDtypeStruct((1, TOK, FEAT), BF16),
        jax.ShapeDtypeStruct((REP,), F32),
    )
    limit = 60 * 1024 * 1024
    results = pl.pallas_call(
        kernel,
        out_shape=shapes,
        in_specs=[hbm] * 6,
        out_specs=(hbm, vmem, smem),
        scratch_shapes=[
            pltpu.SMEM((REP,), jnp.int32),
            pltpu.SMEM((REP,), F32),
            pltpu.VMEM((REP, SLOTS), jnp.int32),
            pltpu.VMEM((REP, SLOTS), jnp.int32),
            pltpu.VMEM((1, TOK, FEAT), BF16),
            pltpu.VMEM((FEAT, COLS), BF16),
            pltpu.VMEM((2, 4, FOLD, WIDE), BF16),
            pltpu.VMEM((2, SLOTS, WIDE), BF16),
            pltpu.VMEM((2, 3, SLOTS, WIDE), BF16),
            pltpu.VMEM((2, REP, SLOTS, WIDE), BF16),
            pltpu.VMEM((FEAT, REP * SLOTS), BF16),
            pltpu.VMEM((8, CHUNK, 1), jnp.int32),
            pltpu.VMEM((REP, 2, SLOTS, WIDE), BF16),
            pltpu.VMEM((3, 2, SLOTS, WIDE), BF16),
            pltpu.VMEM((2, 4, CHUNK, SPAN), F32),
            pltpu.VMEM((2, 4, CHUNK, SPAN), F32),
            pltpu.VMEM((2, 4, CHUNK, SPAN), F32),
            pltpu.VMEM((2, 2, HALF, SPAN), F32),
            pltpu.VMEM((2, 2, HALF, SPAN), F32),
            pltpu.VMEM((2, 2, HALF, SPAN), F32),
            pltpu.VMEM((2, 2, HALF, SPAN), F32),
            pltpu.VMEM((CHUNK, COLS), F32),
            pltpu.VMEM((SEQ, 1, 128), F32),
            pltpu.VMEM((REP, 1, 128), F32),
            pltpu.VMEM((2 * REP, 2, 128), F32),
            pltpu.VMEM((2 * REP, CHUNK, COLS), BF16),
            pltpu.VMEM((2 * REP, CHUNK, COLS), BF16),
            pltpu.VMEM((2, 2 * REP, CHUNK, WIDE), F32),
            pltpu.VMEM((2, 2 * REP, CHUNK, WIDE), BF16),
            pltpu.VMEM((2, 3, 2, CHUNK, WIDE), BF16),
            pltpu.VMEM((2, SLOTS, WIDE), BF16),
            pltpu.VMEM((2, 3, SLOTS, WIDE), BF16),
            pltpu.VMEM((2, 4, FOLD, WIDE), BF16),
            pltpu.VMEM((2, 3, FOLD, WIDE), BF16),
            pltpu.VMEM((FEAT, COLS), BF16),
            pltpu.SemaphoreType.DMA((MESSAGES,)),
            pltpu.SemaphoreType.DMA((MESSAGES,)),
            pltpu.SemaphoreType.DMA((6,)),
            pltpu.SemaphoreType.DMA((5,)),
        ],
        compiler_params=pltpu.CompilerParams(
            collective_id=0, has_side_effects=True, vmem_limit_bytes=limit
        ),
        cost_estimate=pl.CostEstimate(
            flops=6 * 256 * FEAT * COLS, bytes_accessed=4 * FEAT * COLS, transcendentals=64 * COLS
        ),
    )(counts, seq_cotangent, positions, targets, hidden, head_weight)
    return pl.pallas_call(
        hand_over,
        out_shape=shapes,
        in_specs=[hbm] * 3,
        out_specs=(hbm,) * 3,
        scratch_shapes=[
            pltpu.VMEM((FEAT, COLS), BF16),
            pltpu.VMEM((1, TOK, FEAT), BF16),
            pltpu.SMEM((REP,), F32),
            pltpu.SemaphoreType.DMA((10,)),
            pltpu.SemaphoreType.DMA((10,)),
        ],
        compiler_params=pltpu.CompilerParams(vmem_limit_bytes=limit),
    )(*results)


def solution(mesh):
    return jax.shard_map(
        shards,
        mesh=mesh,
        in_specs=(P("rep", "seq", "vocab"), P("vocab", ("seq", "rep")), P(), P(), P(), P()),
        out_specs=(P("vocab", ("seq", "rep")), P("rep", "seq", "vocab"), P()),
        check_vma=False,
    )
```

```python
import jax
import jax.numpy as jnp
from jax import lax
from jax.experimental import pallas as pl
from jax.experimental.pallas import tpu as pltpu
from jax.sharding import PartitionSpec as P

MESH = pl.DeviceIdType.MESH
F32 = jnp.float32
BF16 = jnp.bfloat16

SEQ = 16
REP = 4
SLOTS = 64
TOK = 64
FEAT = 512
COLS = 1280
FOLD = 16
CHUNK = 32
HALF = 16
WIDE = FEAT // 2
THIN = FEAT // 4
SPAN = COLS // 2

PICK_CLASS = 0
PICK_NEAR = 12
PICK_REP = 28
LOGIT_CORE = 40
LOGIT_Y = 48
STAT_SEQ = 60
STAT_REP = 75
GRAD_Y = 78
GRAD_CORE = 86
SCALE = 89
ROW_REP = 96
ROW_NEAR = 108
ROW_CLASS = 124
TARGET_REP = 136
MESSAGES = 139


def iota(shape, dim):
    return lax.broadcasted_iota(jnp.int32, shape, dim)


def to_column(row, rows, shift=0):
    shape = (rows, row.shape[1])
    at = iota(shape, 1) == iota(shape, 0) + shift
    return jnp.sum(jnp.where(at, row, 0.0), axis=1, keepdims=True)


def to_row(column, shift):
    shape = (CHUNK, 128)
    at = iota(shape, 1) == iota(shape, 0) + shift
    return jnp.sum(jnp.where(at, column, 0.0), axis=0, keepdims=True)


def turn(row, shift):
    return pltpu.roll(row, 128 - shift, 1)


def between(row, first):
    lane = iota((1, 128), 1)
    return jnp.where((lane >= first) & (lane < first + CHUNK), row, 0.0)


def merge_stats(ref, parts):
    rows = [ref[i] for i in range(parts)]
    row_max = rows[0]
    for row in rows[1:]:
        row_max = jnp.maximum(row_max, row)
    row_sum = jnp.zeros((1, 128), F32)
    row_target = jnp.zeros((1, 128), F32)
    for row in rows:
        row_sum = row_sum + turn(row, CHUNK) * jnp.exp(row - row_max)
        row_target = row_target + row
    return row_max, row_sum, turn(row_target, 2 * CHUNK)


def pack_stats(row_max, row_sum, row_target):
    return (
        between(row_max, 0)
        + between(turn(row_sum, 128 - CHUNK), CHUNK)
        + between(turn(row_target, 128 - 2 * CHUNK), 2 * CHUNK)
    )


def fold_rows(rows):
    return (rows[0:16] + rows[16:32]) + (rows[32:48] + rows[48:64])


def unfold_rows(rows):
    return jnp.concatenate([rows, rows, rows, rows], axis=0)


def kernel(
    counts_hbm, cot_hbm, positions_hbm, targets_hbm, hidden_hbm, weight_hbm,
    head_hbm, grad_ref, losses_ref,
    counts_ref, cot_ref, positions_ref, targets_ref, hidden_ref,
    weight, pick_class, pick_own, pick_near, picked, picked_t, target_cols, target_out, target_in,
    core_out, core_in, part, y_fwd, y_sum, y_direct, y_acc, logits_ref,
    stat_seq, stat_rep, scales, exps, grads,
    row_sums, row_out, row_in, near_out, near_in, class_out, class_in, head_out,
    send_sem, recv_sem, load_sem, head_sem,
):
    z = lax.axis_index("seq")
    v = lax.axis_index("vocab")
    x = lax.axis_index("rep")
    y = lax.div(v, 2)
    c = lax.rem(v, 2)
    cls = lax.rem(z, 4)
    member = lax.div(z, 4)

    def at_z(shift):
        return {"seq": lax.rem(z + shift + SEQ, SEQ)}

    def at_x(shift):
        return {"rep": lax.rem(x + shift, REP)}

    def y_plus(shift):
        return lax.rem(y + shift, 4)

    def at_y(shift):
        return {"vocab": y_plus(shift) * 2 + c}

    def across_y(shift):
        return {"vocab": y_plus(shift) * 2 + 1 - c}

    def load(number, src, dst):
        copy = pltpu.make_async_copy(src, dst, load_sem.at[number])
        copy.start()
        return copy

    loads = [
        load(0, positions_hbm, positions_ref),
        load(1, counts_hbm, counts_ref),
        load(2, hidden_hbm, hidden_ref),
        load(3, cot_hbm, cot_ref),
        load(4, targets_hbm, targets_ref),
        load(5, weight_hbm, weight),
    ]

    sibling = {"vocab": y * 2 + 1 - c}

    started = []

    def send(number, src, dst, device):
        copy = pltpu.make_async_remote_copy(
            src_ref=src,
            dst_ref=dst,
            send_sem=send_sem.at[number],
            recv_sem=recv_sem.at[number],
            device_id=device,
            device_id_type=MESH,
        )
        copy.start()
        started.append(copy)
        return copy

    barrier = pltpu.get_barrier_semaphore()
    friends = [at_z(s) for s in range(1, SEQ)] + [at_x(s) for s in (1, 2, 3)]
    friends += [{"vocab": lax.rem(v + s, 8)} for s in range(1, 8)]
    for friend in friends:
        pl.semaphore_signal(barrier, inc=1, device_id=friend, device_id_type=MESH)

    loads[0].wait()
    loads[1].wait()
    all_positions = positions_ref[...].astype(F32)
    position_row = jnp.sum(
        jnp.where(iota((REP, SLOTS), 0) == x, all_positions, 0.0), axis=0, keepdims=True
    )
    count = counts_ref[x]
    position_col = to_column(position_row, SLOTS).astype(jnp.int32)
    live_col = iota((SLOTS, 1), 0) < count
    owner_col = jnp.where(live_col, lax.div(position_col, TOK), -1)
    pick_at = (iota((SLOTS, TOK), 1) + z * TOK == position_col) & (iota((SLOTS, TOK), 0) < count)
    put_at = (iota((TOK, SLOTS), 0) + z * TOK == position_row.astype(jnp.int32)) & (
        iota((TOK, SLOTS), 1) < count
    )

    loads[2].wait()
    own_rows = jnp.dot(
        jnp.where(pick_at, 1.0, 0.0).astype(BF16), hidden_ref[0], preferred_element_type=F32
    )
    folded = fold_rows(own_rows).astype(BF16)
    for h in range(4):
        pick_class[h, member] = folded[:, h * THIN : (h + 1) * THIN]

    pl.semaphore_wait(barrier, len(friends))

    class_copies = [
        [
            send(
                PICK_CLASS + 3 * h + d - 1, pick_class.at[h, member], pick_class.at[h, member],
                at_z(4 * d),
            )
            for d in (2, 1, 3)
        ]
        for h in range(4)
    ]

    def send_near(number, src, dst):
        low, high = pl.ds(0, 32), pl.ds(32, 32)
        return [
            send(number + 2, src.at[low], dst.at[2, low], at_z(2)),
            send(number + 3, src.at[high], dst.at[2, high], at_z(-2)),
            send(number, src, dst.at[0], at_z(1)),
            send(number + 1, src, dst.at[1], at_z(-1)),
        ]

    loads[4].wait()
    all_targets = targets_ref[...].astype(F32)
    column = iota((CHUNK, COLS), 1) + (z * REP + x) * COLS
    for i in range(8):
        target_cols[i] = to_column(
            all_targets[i // 2 : i // 2 + 1], CHUNK, CHUNK * (i % 2)
        ).astype(jnp.int32)

    def head_at_targets(h):
        hot = [jnp.where(column == target_cols[i], 1.0, 0.0).astype(BF16) for i in range(8)]
        there = lax.dot_general(
            jnp.concatenate(hot, axis=0), weight[h * WIDE : (h + 1) * WIDE],
            (((1,), (1,)), ((), ())), preferred_element_type=F32,
        ).reshape(REP, SLOTS, WIDE)
        for q in range(REP):
            target_out[q, h] = there[q].astype(BF16)

    loads[5].wait()
    head_at_targets(0)

    totals = []
    near_copies = []
    for h in range(4):
        for copy in class_copies[h]:
            copy.wait_recv()
        total = jnp.zeros((SLOTS, THIN), F32)
        for j in range(4):
            block = unfold_rows(pick_class[h, j].astype(F32))
            total = total + jnp.where(owner_col == cls + 4 * j, block, 0.0)
        pick_own[h] = total.astype(BF16)
        near_copies.append(send_near(PICK_NEAR + 4 * h, pick_own.at[h], pick_near.at[h]))
        totals.append(total)
    head_at_targets(1)
    rep_copies = []
    for h in range(4):
        for copy in near_copies[h]:
            copy.wait_recv()
        total = totals[h]
        for i in range(3):
            total = total + pick_near[h, i].astype(F32)
        picked[h, x] = total.astype(BF16)
        rep_copies.append([
            send(PICK_REP + 3 * h + d - 1, picked.at[h, x], picked.at[h, x], at_x(d))
            for d in (2, 1, 3)
        ])

    def partial_logits(h, core, k):
        rows = jnp.concatenate(
            [picked[2 * h + i, pl.ds(2 * core, 2)].reshape(2 * SLOTS, THIN) for i in range(2)], axis=1
        )
        return jnp.dot(
            rows, weight[h * WIDE : (h + 1) * WIDE, k * SPAN : (k + 1) * SPAN],
            preferred_element_type=F32,
        ).reshape(4, CHUNK, SPAN)

    for copy in rep_copies[0] + rep_copies[1]:
        copy.wait_recv()
    for k in range(2):
        core_out[k] = partial_logits(0, 1 - c, k)
        part[k] = partial_logits(0, c, k)
    for copy in rep_copies[2] + rep_copies[3]:
        copy.wait_recv()
    order = (2, 1, 3, 0)
    core_copies = []
    for k in range(2):
        core_out[k] = core_out[k] + partial_logits(1, 1 - c, k)
        core_copies.append({
            s: send(
                LOGIT_CORE + 4 * k + s, core_out.at[k, y_plus(s)], core_in.at[k, y_plus(s)], sibling
            )
            for s in order
        })
    for k in range(2):
        part[k] = part[k] + partial_logits(1, c, k)
    target_copies = [
        send(
            TARGET_REP + d - 1, target_out.at[lax.rem(x + d, REP)], target_in.at[d - 1], at_x(d)
        )
        for d in (1, 2, 3)
    ]

    low, high = pl.ds(0, HALF), pl.ds(HALF, HALF)
    fwd_copies = []
    last_copies = []
    for s in order:
        for k in range(2):
            core_copies[k][s].wait_recv()
            at = y_plus(s)
            part[k, at] = part[k, at] + core_in[k, at]
            number = LOGIT_Y + 6 * k
            if s == 2:
                fwd_copies.append((
                    send(number, part.at[k, at, low], y_fwd.at[k, 0], at_y(1)),
                    send(number + 1, part.at[k, at, high], y_fwd.at[k, 1], at_y(3)),
                ))
            if s == 1:
                last_copies.append(
                    send(number + 2, part.at[k, at, high], y_direct.at[k, 1], at_y(1))
                )
            if s == 3:
                last_copies.append(
                    send(number + 3, part.at[k, at, low], y_direct.at[k, 0], at_y(3))
                )
    for k in range(2):
        number = LOGIT_Y + 6 * k
        fwd_copies[k][0].wait_recv()
        y_sum[k, 0] = y_fwd[k, 0] + part[k, y_plus(1), 0:HALF]
        last_copies.append(send(number + 4, y_sum.at[k, 0], y_acc.at[k, 0], at_y(1)))
        fwd_copies[k][1].wait_recv()
        y_sum[k, 1] = y_fwd[k, 1] + part[k, y_plus(3), HALF:CHUNK]
        last_copies.append(send(number + 5, y_sum.at[k, 1], y_acc.at[k, 1], at_y(3)))
    for h in range(4):
        picked_t[h * THIN : (h + 1) * THIN] = picked[h].reshape(REP * SLOTS, THIN).T
    for copy in last_copies:
        copy.wait_recv()
    for k in range(2):
        columns = pl.ds(k * SPAN, SPAN)
        logits_ref[0:HALF, columns] = part[k, y, 0:HALF] + (y_direct[k, 0] + y_acc[k, 0])
        logits_ref[HALF:CHUNK, columns] = part[k, y, HALF:CHUNK] + (y_direct[k, 1] + y_acc[k, 1])

    loads[3].wait()
    my_seq = 2 * c + lax.div(y, 2)
    first_slot = lax.rem(y, 2) * CHUNK
    my_count = counts_ref[my_seq]
    my_cot = cot_ref[my_seq]
    my_chunk = 4 * c + y
    is_target = column == target_cols[my_chunk]
    logits = logits_ref[...]
    local_max = jnp.max(logits, axis=1, keepdims=True)
    exponent = jnp.exp(logits - local_max)

    exps[my_chunk] = jnp.where(is_target, 0.0, exponent).astype(BF16)
    mine = exps.at[my_chunk]
    before = exps.at[4 * c + y_plus(3)]
    after = exps.at[4 * c + y_plus(1)]
    up_low = send(GRAD_Y, mine.at[low], mine.at[low], at_y(1))
    down_high = send(GRAD_Y + 1, mine.at[high], mine.at[high], at_y(3))
    up_high = send(GRAD_Y + 2, mine.at[high], mine.at[high], at_y(1))
    down_low = send(GRAD_Y + 3, mine.at[low], mine.at[low], at_y(3))
    core_copies = [send(GRAD_CORE, mine, mine, sibling)]

    local_sum = jnp.sum(exponent, axis=1, keepdims=True)
    local_target = jnp.sum(jnp.where(is_target, logits, 0.0), axis=1, keepdims=True)
    max_row = to_row(local_max, 0)
    stat_seq[z] = max_row + to_row(local_sum, CHUNK) + to_row(local_target, 2 * CHUNK)
    seq_copies = [
        send(STAT_SEQ + d - 1, stat_seq.at[z], stat_seq.at[z], at_z(d))
        for d in (8, 7, 9, 6, 10, 5, 11, 4, 12, 3, 13, 2, 14, 1, 15)
    ]

    up_low.wait_recv()
    relays = [
        send(GRAD_Y + 4, before.at[low], before.at[low], at_y(1)),
        send(GRAD_Y + 5, before.at[low], before.at[low], across_y(1)),
    ]
    down_high.wait_recv()
    relays.append(send(GRAD_Y + 6, after.at[high], after.at[high], at_y(3)))
    relays.append(send(GRAD_Y + 7, after.at[high], after.at[high], across_y(3)))
    up_high.wait_recv()
    core_copies.append(send(GRAD_CORE + 1, before, before, sibling))
    down_low.wait_recv()
    core_copies.append(send(GRAD_CORE + 2, after, after, sibling))

    def head_times(h, chunks):
        block = jnp.concatenate([exps[i] for i in chunks], axis=0)
        rows = lax.dot_general(
            block, weight[h * WIDE : (h + 1) * WIDE], (((1,), (1,)), ((), ())),
            preferred_element_type=F32,
        )
        for n, i in enumerate(chunks):
            row_sums[h, i] = rows[n * CHUNK : (n + 1) * CHUNK]
            for p in range(2):
                row_out[2 * h + p, i] = rows[
                    n * CHUNK : (n + 1) * CHUNK, p * THIN : (p + 1) * THIN
                ].astype(BF16)

    for h in range(2):
        head_times(h, [4 * c + y_plus(i) for i in (0, 1, 3)])
    for copy in seq_copies:
        copy.wait_recv()
    stat_rep[x] = pack_stats(*merge_stats(stat_seq, SEQ)) + to_row(local_max, 3 * CHUNK)
    stat_copies = [
        send(STAT_REP + d - 1, stat_rep.at[x], stat_rep.at[x], at_x(d)) for d in (1, 2, 3)
    ]
    for copy in core_copies:
        copy.wait_recv()
    for h in range(2):
        head_times(h, [4 * (1 - c) + y_plus(i) for i in (0, 1, 3)])
    for copy in relays:
        copy.wait_recv()
    rep_copies = []
    for h in range(2):
        head_times(h, [4 * c + y_plus(2), 4 * (1 - c) + y_plus(2)])
        for p in (2 * h, 2 * h + 1):
            rep_copies.append([
                send(
                    ROW_REP + 3 * p + d - 1, row_out.at[p, pl.ds(2 * lax.rem(x + d, REP), 2)],
                    row_in.at[p, d - 1], at_x(d),
                )
                for d in (2, 1, 3)
            ])

    for copy in stat_copies:
        copy.wait_recv()
    total_max, total_sum, target_logit = merge_stats(stat_rep, REP)
    lane = iota((1, 128), 1)
    live = (lane < CHUNK) & (lane + first_slot < my_count)
    count_row = jnp.full((1, 128), my_count.astype(F32), F32)
    weight_row = jnp.where(live, jnp.full((1, 128), my_cot, F32) / count_row, 0.0)
    factor_row = jnp.zeros((1, 128), F32)
    for i in range(REP):
        there = jnp.exp(turn(stat_rep[i], 3 * CHUNK) - total_max) / total_sum
        factor = jnp.where(live, weight_row * there, 0.0)
        factor_row = factor_row + (turn(factor, 128 - i * CHUNK) if i else factor)
    at_target = jnp.where(
        live, weight_row * (jnp.exp(target_logit - total_max) / total_sum - 1.0), 0.0
    )
    row_loss = jnp.where(live, (jnp.log(total_sum) + total_max - target_logit) / count_row, 0.0)
    scales[my_chunk, 0:1] = factor_row
    scales[my_chunk, 1:2] = at_target + turn(row_loss, 128 - CHUNK)
    scale_copies = [
        send(SCALE + d - 1, scales.at[my_chunk], scales.at[my_chunk], {"vocab": lax.rem(v + d, 8)})
        for d in range(1, 8)
    ]
    for copy in scale_copies:
        copy.wait_recv()

    def slots_of_mine(part_of, first):
        return jnp.concatenate(
            [to_column(scales[2 * x + i, part_of : part_of + 1], CHUNK, first) for i in range(2)],
            axis=0,
        )

    slot_factors = [
        slots_of_mine(0, CHUNK * lax.rem(x + REP - d, REP)) for d in range(REP)
    ]
    slot_target = slots_of_mine(1, 0).astype(BF16).astype(F32)
    for copy in target_copies:
        copy.wait_recv()
    owns = []
    for h in range(2):
        column_sum = target_out[x, h].astype(F32)
        for i in range(3):
            column_sum = column_sum + target_in[i, h].astype(F32)
        rows = row_sums[h, pl.ds(2 * x, 2)].reshape(SLOTS, WIDE)
        own = slot_target * column_sum + slot_factors[0] * rows
        owns += [own[:, 0:THIN], own[:, THIN:WIDE]]

    def scale_grads():
        for i in range(8):
            factor = to_column(scales[i, 0:1], CHUNK, CHUNK * x)
            at_own = to_column(scales[i, 1:2], CHUNK)
            values = exps[i].astype(F32) * factor
            grads[i] = jnp.where(column == target_cols[i], at_own, values).astype(BF16)

    def head_part(i):
        columns = pl.ds(i * 256, 256)
        tile = jnp.dot(
            picked_t[...], grads[:, :, columns].reshape(REP * SLOTS, 256), preferred_element_type=F32
        )
        head_out[:, columns] = tile.astype(BF16)
        copy = pltpu.make_async_copy(
            head_out.at[:, columns], head_hbm.at[:, columns], head_sem.at[i]
        )
        copy.start()
        return copy

    near_copies = []
    for h in range(4):
        for copy in rep_copies[h]:
            copy.wait_recv()
        for i in range(3):
            owns[h] = owns[h] + slot_factors[i + 1] * row_in[h, i].reshape(SLOTS, THIN).astype(F32)
        near_out[h] = owns[h].astype(BF16)
        near_copies.append(send_near(ROW_NEAR + 4 * h, near_out.at[h], near_in.at[h]))
    scale_grads()
    head_copies = [head_part(0), head_part(1)]
    mine_rows = []
    class_copies = []
    for h in range(4):
        for copy in near_copies[h]:
            copy.wait_recv()
        own = owns[h]
        for i in range(3):
            own = own + near_in[h, i].astype(F32)
        mine = jnp.zeros((FOLD, THIN), F32)
        for j in range(4):
            block = fold_rows(jnp.where(owner_col == cls + 4 * j, own, 0.0))
            class_out[h, j] = block.astype(BF16)
            mine = jnp.where(member == j, block, mine)
        mine_rows.append(mine)
        class_copies.append([
            send(
                ROW_CLASS + 3 * h + d - 1, class_out.at[h, lax.rem(member + d, 4)],
                class_in.at[h, d - 1], at_z(4 * d),
            )
            for d in (2, 1, 3)
        ])
    head_copies += [head_part(2), head_part(3), head_part(4)]
    for copy in started[: -4 * 3]:
        copy.wait_send()
    for q in range(REP):
        losses_ref[q] = jnp.sum(between(scales[2 * q, 1:2] + scales[2 * q + 1, 1:2], CHUNK))
    for copy in head_copies:
        copy.wait()
    put = jnp.where(put_at, 1.0, 0.0).astype(BF16)
    for h in range(4):
        for copy in class_copies[h]:
            copy.wait_recv()
        mine = mine_rows[h]
        for i in range(3):
            mine = mine + class_in[h, i].astype(F32)
        final = unfold_rows(mine.astype(BF16).astype(F32))
        final = jnp.where(owner_col == z, final, 0.0).astype(BF16)
        grad_ref[0, :, h * THIN : (h + 1) * THIN] = jnp.dot(
            put, final, preferred_element_type=F32
        ).astype(BF16)

    for copies in class_copies:
        for copy in copies:
            copy.wait_send()


def hand_over(
    head_in, hidden_in, losses_in, head_ref, hidden_ref, losses_ref,
    head, hidden, losses, in_sem, out_sem,
):
    rows = FEAT // 4
    moves = [(hidden_in, hidden, hidden_ref), (losses_in, losses, losses_ref)]
    for i in range(4):
        at = pl.ds(i * rows, rows)
        moves.append((head_in.at[at], head.at[at], head_ref.at[at]))
    loads = [pltpu.make_async_copy(m[0], m[1], in_sem.at[i]) for i, m in enumerate(moves)]
    stores = [pltpu.make_async_copy(m[1], m[2], out_sem.at[i]) for i, m in enumerate(moves)]
    for load in loads:
        load.start()
    for load, store in zip(loads, stores):
        load.wait()
        store.start()
    for store in stores:
        store.wait()


def shards(hidden, head_weight, positions, counts, targets, seq_cotangent):
    vmem = pl.BlockSpec(memory_space=pltpu.VMEM)
    smem = pl.BlockSpec(memory_space=pltpu.SMEM)
    hbm = pl.BlockSpec(memory_space=pltpu.HBM)
    shapes = (
        jax.ShapeDtypeStruct((FEAT, COLS), BF16),
        jax.ShapeDtypeStruct((1, TOK, FEAT), BF16),
        jax.ShapeDtypeStruct((REP,), F32),
    )
    limit = 60 * 1024 * 1024
    results = pl.pallas_call(
        kernel,
        out_shape=shapes,
        in_specs=[hbm] * 6,
        out_specs=(hbm, vmem, smem),
        scratch_shapes=[
            pltpu.SMEM((REP,), jnp.int32),
            pltpu.SMEM((REP,), F32),
            pltpu.VMEM((REP, SLOTS), jnp.int32),
            pltpu.VMEM((REP, SLOTS), jnp.int32),
            pltpu.VMEM((1, TOK, FEAT), BF16),
            pltpu.VMEM((FEAT, COLS), BF16),
            pltpu.VMEM((4, 4, FOLD, THIN), BF16),
            pltpu.VMEM((4, SLOTS, THIN), BF16),
            pltpu.VMEM((4, 3, SLOTS, THIN), BF16),
            pltpu.VMEM((4, REP, SLOTS, THIN), BF16),
            pltpu.VMEM((FEAT, REP * SLOTS), BF16),
            pltpu.VMEM((8, CHUNK, 1), jnp.int32),
            pltpu.VMEM((REP, 2, SLOTS, WIDE), BF16),
            pltpu.VMEM((3, 2, SLOTS, WIDE), BF16),
            pltpu.VMEM((2, 4, CHUNK, SPAN), F32),
            pltpu.VMEM((2, 4, CHUNK, SPAN), F32),
            pltpu.VMEM((2, 4, CHUNK, SPAN), F32),
            pltpu.VMEM((2, 2, HALF, SPAN), F32),
            pltpu.VMEM((2, 2, HALF, SPAN), F32),
            pltpu.VMEM((2, 2, HALF, SPAN), F32),
            pltpu.VMEM((2, 2, HALF, SPAN), F32),
            pltpu.VMEM((CHUNK, COLS), F32),
            pltpu.VMEM((SEQ, 1, 128), F32),
            pltpu.VMEM((REP, 1, 128), F32),
            pltpu.VMEM((2 * REP, 2, 128), F32),
            pltpu.VMEM((2 * REP, CHUNK, COLS), BF16),
            pltpu.VMEM((2 * REP, CHUNK, COLS), BF16),
            pltpu.VMEM((2, 2 * REP, CHUNK, WIDE), F32),
            pltpu.VMEM((4, 2 * REP, CHUNK, THIN), BF16),
            pltpu.VMEM((4, 3, 2, CHUNK, THIN), BF16),
            pltpu.VMEM((4, SLOTS, THIN), BF16),
            pltpu.VMEM((4, 3, SLOTS, THIN), BF16),
            pltpu.VMEM((4, 4, FOLD, THIN), BF16),
            pltpu.VMEM((4, 3, FOLD, THIN), BF16),
            pltpu.VMEM((FEAT, COLS), BF16),
            pltpu.SemaphoreType.DMA((MESSAGES,)),
            pltpu.SemaphoreType.DMA((MESSAGES,)),
            pltpu.SemaphoreType.DMA((6,)),
            pltpu.SemaphoreType.DMA((5,)),
        ],
        compiler_params=pltpu.CompilerParams(
            collective_id=0, has_side_effects=True, vmem_limit_bytes=limit
        ),
        cost_estimate=pl.CostEstimate(
            flops=6 * 256 * FEAT * COLS, bytes_accessed=4 * FEAT * COLS, transcendentals=64 * COLS
        ),
    )(counts, seq_cotangent, positions, targets, hidden, head_weight)
    return pl.pallas_call(
        hand_over,
        out_shape=shapes,
        in_specs=[hbm] * 3,
        out_specs=(hbm,) * 3,
        scratch_shapes=[
            pltpu.VMEM((FEAT, COLS), BF16),
            pltpu.VMEM((1, TOK, FEAT), BF16),
            pltpu.SMEM((REP,), F32),
            pltpu.SemaphoreType.DMA((6,)),
            pltpu.SemaphoreType.DMA((6,)),
        ],
        compiler_params=pltpu.CompilerParams(vmem_limit_bytes=limit),
    )(*results)


def solution(mesh):
    return jax.shard_map(
        shards,
        mesh=mesh,
        in_specs=(P("rep", "seq", "vocab"), P("vocab", ("seq", "rep")), P(), P(), P(), P()),
        out_specs=(P("vocab", ("seq", "rep")), P("rep", "seq", "vocab"), P()),
        check_vma=False,
    )
```

```python
import jax
import jax.numpy as jnp
from jax import lax
from jax.experimental import pallas as pl
from jax.experimental.pallas import tpu as pltpu
from jax.sharding import PartitionSpec as P

MESH = pl.DeviceIdType.MESH
F32 = jnp.float32
BF16 = jnp.bfloat16

SEQ = 16
REP = 4
SLOTS = 64
TOK = 64
FEAT = 512
COLS = 1280
FOLD = 16
CHUNK = 32
HALF = 16
WIDE = FEAT // 2
SPAN = COLS // 2

PICK_CLASS = 0
PICK_NEAR = 6
PICK_REP = 14
LOGIT_CORE = 20
LOGIT_Y = 28
STAT_SEQ = 40
STAT_REP = 55
GRAD_Y = 58
GRAD_CORE = 66
SCALE = 69
ROW_REP = 76
ROW_NEAR = 82
ROW_CLASS = 90
TARGET_REP = 96
MESSAGES = 99


def iota(shape, dim):
    return lax.broadcasted_iota(jnp.int32, shape, dim)


def to_column(row, rows, shift=0):
    shape = (rows, row.shape[1])
    at = iota(shape, 1) == iota(shape, 0) + shift
    return jnp.sum(jnp.where(at, row, 0.0), axis=1, keepdims=True)


def to_row(column, shift):
    shape = (CHUNK, 128)
    at = iota(shape, 1) == iota(shape, 0) + shift
    return jnp.sum(jnp.where(at, column, 0.0), axis=0, keepdims=True)


def turn(row, shift):
    return pltpu.roll(row, 128 - shift, 1)


def between(row, first):
    lane = iota((1, 128), 1)
    return jnp.where((lane >= first) & (lane < first + CHUNK), row, 0.0)


def merge_stats(ref, parts):
    rows = [ref[i] for i in range(parts)]
    row_max = rows[0]
    for row in rows[1:]:
        row_max = jnp.maximum(row_max, row)
    row_sum = jnp.zeros((1, 128), F32)
    row_target = jnp.zeros((1, 128), F32)
    for row in rows:
        row_sum = row_sum + turn(row, CHUNK) * jnp.exp(row - row_max)
        row_target = row_target + row
    return row_max, row_sum, turn(row_target, 2 * CHUNK)


def pack_stats(row_max, row_sum, row_target):
    return (
        between(row_max, 0)
        + between(turn(row_sum, 128 - CHUNK), CHUNK)
        + between(turn(row_target, 128 - 2 * CHUNK), 2 * CHUNK)
    )


def fold_rows(rows):
    return (rows[0:16] + rows[16:32]) + (rows[32:48] + rows[48:64])


def unfold_rows(rows):
    return jnp.concatenate([rows, rows, rows, rows], axis=0)


def kernel(
    counts_hbm, cot_hbm, positions_hbm, targets_hbm, hidden_hbm, weight_hbm,
    head_hbm, grad_ref, losses_ref,
    counts_ref, cot_ref, positions_ref, targets_ref, hidden_ref,
    weight, pick_class, pick_own, pick_near, picked, picked_t, target_cols, target_out, target_in,
    core_out, core_in, part, y_fwd, y_sum, y_direct, y_acc, logits_ref,
    stat_seq, stat_rep, scales, exps, grads,
    row_sums, row_out, row_in, near_out, near_in, class_out, class_in, head_out,
    send_sem, recv_sem, load_sem, head_sem,
):
    z = lax.axis_index("seq")
    v = lax.axis_index("vocab")
    x = lax.axis_index("rep")
    y = lax.div(v, 2)
    c = lax.rem(v, 2)
    cls = lax.rem(z, 4)
    member = lax.div(z, 4)

    def at_z(shift):
        return {"seq": lax.rem(z + shift + SEQ, SEQ)}

    def at_x(shift):
        return {"rep": lax.rem(x + shift, REP)}

    def y_plus(shift):
        return lax.rem(y + shift, 4)

    def at_y(shift):
        return {"vocab": y_plus(shift) * 2 + c}

    def across_y(shift):
        return {"vocab": y_plus(shift) * 2 + 1 - c}

    def load(number, src, dst):
        copy = pltpu.make_async_copy(src, dst, load_sem.at[number])
        copy.start()
        return copy

    loads = [
        load(0, positions_hbm, positions_ref),
        load(1, counts_hbm, counts_ref),
        load(2, hidden_hbm, hidden_ref),
        load(3, cot_hbm, cot_ref),
        load(4, targets_hbm, targets_ref),
        load(5, weight_hbm, weight),
    ]

    sibling = {"vocab": y * 2 + 1 - c}

    started = []

    def send(number, src, dst, device):
        copy = pltpu.make_async_remote_copy(
            src_ref=src,
            dst_ref=dst,
            send_sem=send_sem.at[number],
            recv_sem=recv_sem.at[number],
            device_id=device,
            device_id_type=MESH,
        )
        copy.start()
        started.append(copy)
        return copy

    barrier = pltpu.get_barrier_semaphore()
    friends = [at_z(s) for s in range(1, SEQ)] + [at_x(s) for s in (1, 2, 3)]
    friends += [{"vocab": lax.rem(v + s, 8)} for s in range(1, 8)]
    for friend in friends:
        pl.semaphore_signal(barrier, inc=1, device_id=friend, device_id_type=MESH)

    loads[0].wait()
    loads[1].wait()
    all_positions = positions_ref[...].astype(F32)
    position_row = jnp.sum(
        jnp.where(iota((REP, SLOTS), 0) == x, all_positions, 0.0), axis=0, keepdims=True
    )
    count = counts_ref[x]
    position_col = to_column(position_row, SLOTS).astype(jnp.int32)
    live_col = iota((SLOTS, 1), 0) < count
    owner_col = jnp.where(live_col, lax.div(position_col, TOK), -1)
    pick_at = (iota((SLOTS, TOK), 1) + z * TOK == position_col) & (iota((SLOTS, TOK), 0) < count)
    put_at = (iota((TOK, SLOTS), 0) + z * TOK == position_row.astype(jnp.int32)) & (
        iota((TOK, SLOTS), 1) < count
    )

    loads[2].wait()
    own_rows = jnp.dot(
        jnp.where(pick_at, 1.0, 0.0).astype(BF16), hidden_ref[0], preferred_element_type=F32
    )
    folded = fold_rows(own_rows).astype(BF16)
    for h in range(2):
        pick_class[h, member] = folded[:, h * WIDE : (h + 1) * WIDE]

    pl.semaphore_wait(barrier, len(friends))

    class_copies = [
        [
            send(
                PICK_CLASS + 3 * h + d - 1, pick_class.at[h, member], pick_class.at[h, member],
                at_z(4 * d),
            )
            for d in (2, 1, 3)
        ]
        for h in range(2)
    ]

    def send_near(number, src, dst):
        low, high = pl.ds(0, 32), pl.ds(32, 32)
        return [
            send(number + 2, src.at[low], dst.at[2, low], at_z(2)),
            send(number + 3, src.at[high], dst.at[2, high], at_z(-2)),
            send(number, src, dst.at[0], at_z(1)),
            send(number + 1, src, dst.at[1], at_z(-1)),
        ]

    loads[4].wait()
    all_targets = targets_ref[...].astype(F32)
    column = iota((CHUNK, COLS), 1) + (z * REP + x) * COLS
    for i in range(8):
        target_cols[i] = to_column(
            all_targets[i // 2 : i // 2 + 1], CHUNK, CHUNK * (i % 2)
        ).astype(jnp.int32)

    def head_at_targets(h):
        hot = [jnp.where(column == target_cols[i], 1.0, 0.0).astype(BF16) for i in range(8)]
        there = lax.dot_general(
            jnp.concatenate(hot, axis=0), weight[h * WIDE : (h + 1) * WIDE],
            (((1,), (1,)), ((), ())), preferred_element_type=F32,
        ).reshape(REP, SLOTS, WIDE)
        for q in range(REP):
            target_out[q, h] = there[q].astype(BF16)

    loads[5].wait()
    head_at_targets(0)

    totals = []
    near_copies = []
    for h in range(2):
        for copy in class_copies[h]:
            copy.wait_recv()
        total = jnp.zeros((SLOTS, WIDE), F32)
        for j in range(4):
            block = unfold_rows(pick_class[h, j].astype(F32))
            total = total + jnp.where(owner_col == cls + 4 * j, block, 0.0)
        pick_own[h] = total.astype(BF16)
        near_copies.append(send_near(PICK_NEAR + 4 * h, pick_own.at[h], pick_near.at[h]))
        totals.append(total)
    head_at_targets(1)
    rep_copies = []
    for h in range(2):
        for copy in near_copies[h]:
            copy.wait_recv()
        total = totals[h]
        for i in range(3):
            total = total + pick_near[h, i].astype(F32)
        picked[h, x] = total.astype(BF16)
        rep_copies.append([
            send(PICK_REP + 3 * h + d - 1, picked.at[h, x], picked.at[h, x], at_x(d))
            for d in (2, 1, 3)
        ])

    def partial_logits(h, core, k):
        rows = picked[h, pl.ds(2 * core, 2)].reshape(2 * SLOTS, WIDE)
        return jnp.dot(
            rows, weight[h * WIDE : (h + 1) * WIDE, k * SPAN : (k + 1) * SPAN],
            preferred_element_type=F32,
        ).reshape(4, CHUNK, SPAN)

    for copy in rep_copies[0]:
        copy.wait_recv()
    for k in range(2):
        core_out[k] = partial_logits(0, 1 - c, k)
        part[k] = partial_logits(0, c, k)
    for copy in rep_copies[1]:
        copy.wait_recv()
    order = (2, 1, 3, 0)
    core_copies = []
    for k in range(2):
        core_out[k] = core_out[k] + partial_logits(1, 1 - c, k)
        core_copies.append({
            s: send(
                LOGIT_CORE + 4 * k + s, core_out.at[k, y_plus(s)], core_in.at[k, y_plus(s)], sibling
            )
            for s in order
        })
    for k in range(2):
        part[k] = part[k] + partial_logits(1, c, k)
    target_copies = [
        send(
            TARGET_REP + d - 1, target_out.at[lax.rem(x + d, REP)], target_in.at[d - 1], at_x(d)
        )
        for d in (1, 2, 3)
    ]

    low, high = pl.ds(0, HALF), pl.ds(HALF, HALF)
    fwd_copies = []
    last_copies = []
    for s in order:
        for k in range(2):
            core_copies[k][s].wait_recv()
            at = y_plus(s)
            part[k, at] = part[k, at] + core_in[k, at]
            number = LOGIT_Y + 6 * k
            if s == 2:
                fwd_copies.append((
                    send(number, part.at[k, at, low], y_fwd.at[k, 0], at_y(1)),
                    send(number + 1, part.at[k, at, high], y_fwd.at[k, 1], at_y(3)),
                ))
            if s == 1:
                last_copies.append(
                    send(number + 2, part.at[k, at, high], y_direct.at[k, 1], at_y(1))
                )
            if s == 3:
                last_copies.append(
                    send(number + 3, part.at[k, at, low], y_direct.at[k, 0], at_y(3))
                )
    for k in range(2):
        number = LOGIT_Y + 6 * k
        fwd_copies[k][0].wait_recv()
        y_sum[k, 0] = y_fwd[k, 0] + part[k, y_plus(1), 0:HALF]
        last_copies.append(send(number + 4, y_sum.at[k, 0], y_acc.at[k, 0], at_y(1)))
        fwd_copies[k][1].wait_recv()
        y_sum[k, 1] = y_fwd[k, 1] + part[k, y_plus(3), HALF:CHUNK]
        last_copies.append(send(number + 5, y_sum.at[k, 1], y_acc.at[k, 1], at_y(3)))
    for h in range(2):
        picked_t[h * WIDE : (h + 1) * WIDE] = picked[h].reshape(REP * SLOTS, WIDE).T
    for copy in last_copies:
        copy.wait_recv()
    for k in range(2):
        columns = pl.ds(k * SPAN, SPAN)
        logits_ref[0:HALF, columns] = part[k, y, 0:HALF] + (y_direct[k, 0] + y_acc[k, 0])
        logits_ref[HALF:CHUNK, columns] = part[k, y, HALF:CHUNK] + (y_direct[k, 1] + y_acc[k, 1])

    loads[3].wait()
    my_seq = 2 * c + lax.div(y, 2)
    first_slot = lax.rem(y, 2) * CHUNK
    my_count = counts_ref[my_seq]
    my_cot = cot_ref[my_seq]
    my_chunk = 4 * c + y
    is_target = column == target_cols[my_chunk]
    logits = logits_ref[...]
    local_max = jnp.max(logits, axis=1, keepdims=True)
    exponent = jnp.exp(logits - local_max)

    exps[my_chunk] = jnp.where(is_target, 0.0, exponent).astype(BF16)
    mine = exps.at[my_chunk]
    before = exps.at[4 * c + y_plus(3)]
    after = exps.at[4 * c + y_plus(1)]
    up_low = send(GRAD_Y, mine.at[low], mine.at[low], at_y(1))
    down_high = send(GRAD_Y + 1, mine.at[high], mine.at[high], at_y(3))
    up_high = send(GRAD_Y + 2, mine.at[high], mine.at[high], at_y(1))
    down_low = send(GRAD_Y + 3, mine.at[low], mine.at[low], at_y(3))
    core_copies = [send(GRAD_CORE, mine, mine, sibling)]

    local_sum = jnp.sum(exponent, axis=1, keepdims=True)
    local_target = jnp.sum(jnp.where(is_target, logits, 0.0), axis=1, keepdims=True)
    max_row = to_row(local_max, 0)
    stat_seq[z] = max_row + to_row(local_sum, CHUNK) + to_row(local_target, 2 * CHUNK)
    seq_copies = [
        send(STAT_SEQ + d - 1, stat_seq.at[z], stat_seq.at[z], at_z(d))
        for d in (8, 7, 9, 6, 10, 5, 11, 4, 12, 3, 13, 2, 14, 1, 15)
    ]

    up_low.wait_recv()
    relays = [
        send(GRAD_Y + 4, before.at[low], before.at[low], at_y(1)),
        send(GRAD_Y + 5, before.at[low], before.at[low], across_y(1)),
    ]
    down_high.wait_recv()
    relays.append(send(GRAD_Y + 6, after.at[high], after.at[high], at_y(3)))
    relays.append(send(GRAD_Y + 7, after.at[high], after.at[high], across_y(3)))
    up_high.wait_recv()
    core_copies.append(send(GRAD_CORE + 1, before, before, sibling))
    down_low.wait_recv()
    core_copies.append(send(GRAD_CORE + 2, after, after, sibling))

    def head_times(h, chunks):
        block = jnp.concatenate([exps[i] for i in chunks], axis=0)
        rows = lax.dot_general(
            block, weight[h * WIDE : (h + 1) * WIDE], (((1,), (1,)), ((), ())),
            preferred_element_type=F32,
        )
        for n, i in enumerate(chunks):
            row_sums[h, i] = rows[n * CHUNK : (n + 1) * CHUNK]
            row_out[h, i] = rows[n * CHUNK : (n + 1) * CHUNK].astype(BF16)

    for h in range(2):
        head_times(h, [4 * c + y_plus(i) for i in (0, 1, 3)])
    for copy in seq_copies:
        copy.wait_recv()
    stat_rep[x] = pack_stats(*merge_stats(stat_seq, SEQ)) + to_row(local_max, 3 * CHUNK)
    stat_copies = [
        send(STAT_REP + d - 1, stat_rep.at[x], stat_rep.at[x], at_x(d)) for d in (1, 2, 3)
    ]
    for copy in core_copies:
        copy.wait_recv()
    for h in range(2):
        head_times(h, [4 * (1 - c) + y_plus(i) for i in (0, 1, 3)])
    for copy in relays:
        copy.wait_recv()
    def send_scales():
        for copy in stat_copies:
            copy.wait_recv()
        total_max, total_sum, target_logit = merge_stats(stat_rep, REP)
        lane = iota((1, 128), 1)
        live = (lane < CHUNK) & (lane + first_slot < my_count)
        count_row = jnp.full((1, 128), my_count.astype(F32), F32)
        weight_row = jnp.where(live, jnp.full((1, 128), my_cot, F32) / count_row, 0.0)
        factor_row = jnp.zeros((1, 128), F32)
        for i in range(REP):
            there = jnp.exp(turn(stat_rep[i], 3 * CHUNK) - total_max) / total_sum
            factor = jnp.where(live, weight_row * there, 0.0)
            factor_row = factor_row + (turn(factor, 128 - i * CHUNK) if i else factor)
        at_target = jnp.where(
            live, weight_row * (jnp.exp(target_logit - total_max) / total_sum - 1.0), 0.0
        )
        row_loss = jnp.where(live, (jnp.log(total_sum) + total_max - target_logit) / count_row, 0.0)
        scales[my_chunk, 0:1] = factor_row
        scales[my_chunk, 1:2] = at_target + turn(row_loss, 128 - CHUNK)
        return [
            send(SCALE + d - 1, scales.at[my_chunk], scales.at[my_chunk], {"vocab": lax.rem(v + d, 8)})
            for d in range(1, 8)
        ]

    rep_copies = []
    for h in range(2):
        head_times(h, [4 * c + y_plus(2), 4 * (1 - c) + y_plus(2)])
        rep_copies.append([
            send(
                ROW_REP + 3 * h + d - 1, row_out.at[h, pl.ds(2 * lax.rem(x + d, REP), 2)],
                row_in.at[h, d - 1], at_x(d),
            )
            for d in (2, 1, 3)
        ])
        if h == 0:
            scale_copies = send_scales()

    for copy in scale_copies:
        copy.wait_recv()

    def slots_of_mine(part_of, first):
        return jnp.concatenate(
            [to_column(scales[2 * x + i, part_of : part_of + 1], CHUNK, first) for i in range(2)],
            axis=0,
        )

    slot_factors = [
        slots_of_mine(0, CHUNK * lax.rem(x + REP - d, REP)) for d in range(REP)
    ]
    slot_target = slots_of_mine(1, 0).astype(BF16).astype(F32)
    for copy in target_copies:
        copy.wait_recv()
    owns = []
    for h in range(2):
        column_sum = target_out[x, h].astype(F32)
        for i in range(3):
            column_sum = column_sum + target_in[i, h].astype(F32)
        owns.append(slot_target * column_sum + slot_factors[0] * row_sums[h, pl.ds(2 * x, 2)].reshape(SLOTS, WIDE))

    def scale_grads():
        for i in range(8):
            factor = to_column(scales[i, 0:1], CHUNK, CHUNK * x)
            at_own = to_column(scales[i, 1:2], CHUNK)
            values = exps[i].astype(F32) * factor
            grads[i] = jnp.where(column == target_cols[i], at_own, values).astype(BF16)

    def head_part(i):
        columns = pl.ds(i * 256, 256)
        tile = jnp.dot(
            picked_t[...], grads[:, :, columns].reshape(REP * SLOTS, 256), preferred_element_type=F32
        )
        head_out[:, columns] = tile.astype(BF16)
        copy = pltpu.make_async_copy(
            head_out.at[:, columns], head_hbm.at[:, columns], head_sem.at[i]
        )
        copy.start()
        return copy

    near_copies = []
    for h in range(2):
        for copy in rep_copies[h]:
            copy.wait_recv()
        for i in range(3):
            owns[h] = owns[h] + slot_factors[i + 1] * row_in[h, i].reshape(SLOTS, WIDE).astype(F32)
        near_out[h] = owns[h].astype(BF16)
        near_copies.append(send_near(ROW_NEAR + 4 * h, near_out.at[h], near_in.at[h]))
    scale_grads()
    head_copies = [head_part(0), head_part(1)]
    mine_rows = []
    class_copies = []
    for h in range(2):
        for copy in near_copies[h]:
            copy.wait_recv()
        own = owns[h]
        for i in range(3):
            own = own + near_in[h, i].astype(F32)
        mine = jnp.zeros((FOLD, WIDE), F32)
        for j in range(4):
            block = fold_rows(jnp.where(owner_col == cls + 4 * j, own, 0.0))
            class_out[h, j] = block.astype(BF16)
            mine = jnp.where(member == j, block, mine)
        mine_rows.append(mine)
        class_copies.append([
            send(
                ROW_CLASS + 3 * h + d - 1, class_out.at[h, lax.rem(member + d, 4)],
                class_in.at[h, d - 1], at_z(4 * d),
            )
            for d in (2, 1, 3)
        ])
    head_copies += [head_part(2), head_part(3), head_part(4)]
    for copy in started[: -2 * 3]:
        copy.wait_send()
    for q in range(REP):
        losses_ref[q] = jnp.sum(between(scales[2 * q, 1:2] + scales[2 * q + 1, 1:2], CHUNK))
    for copy in head_copies:
        copy.wait()
    put = jnp.where(put_at, 1.0, 0.0).astype(BF16)
    for h in range(2):
        for copy in class_copies[h]:
            copy.wait_recv()
        mine = mine_rows[h]
        for i in range(3):
            mine = mine + class_in[h, i].astype(F32)
        final = unfold_rows(mine.astype(BF16).astype(F32))
        final = jnp.where(owner_col == z, final, 0.0).astype(BF16)
        grad_ref[0, :, h * WIDE : (h + 1) * WIDE] = jnp.dot(
            put, final, preferred_element_type=F32
        ).astype(BF16)

    for copies in class_copies:
        for copy in copies:
            copy.wait_send()


def hand_over(
    head_in, hidden_in, losses_in, head_ref, hidden_ref, losses_ref,
    head, hidden, losses, in_sem, out_sem,
):
    rows = FEAT // 4
    moves = [(hidden_in, hidden, hidden_ref), (losses_in, losses, losses_ref)]
    for i in range(4):
        at = pl.ds(i * rows, rows)
        moves.append((head_in.at[at], head.at[at], head_ref.at[at]))
    loads = [pltpu.make_async_copy(m[0], m[1], in_sem.at[i]) for i, m in enumerate(moves)]
    stores = [pltpu.make_async_copy(m[1], m[2], out_sem.at[i]) for i, m in enumerate(moves)]
    for load in loads:
        load.start()
    for load, store in zip(loads, stores):
        load.wait()
        store.start()
    for store in stores:
        store.wait()


def shards(hidden, head_weight, positions, counts, targets, seq_cotangent):
    vmem = pl.BlockSpec(memory_space=pltpu.VMEM)
    smem = pl.BlockSpec(memory_space=pltpu.SMEM)
    hbm = pl.BlockSpec(memory_space=pltpu.HBM)
    shapes = (
        jax.ShapeDtypeStruct((FEAT, COLS), BF16),
        jax.ShapeDtypeStruct((1, TOK, FEAT), BF16),
        jax.ShapeDtypeStruct((REP,), F32),
    )
    limit = 60 * 1024 * 1024
    results = pl.pallas_call(
        kernel,
        out_shape=shapes,
        in_specs=[hbm] * 6,
        out_specs=(hbm, vmem, smem),
        scratch_shapes=[
            pltpu.SMEM((REP,), jnp.int32),
            pltpu.SMEM((REP,), F32),
            pltpu.VMEM((REP, SLOTS), jnp.int32),
            pltpu.VMEM((REP, SLOTS), jnp.int32),
            pltpu.VMEM((1, TOK, FEAT), BF16),
            pltpu.VMEM((FEAT, COLS), BF16),
            pltpu.VMEM((2, 4, FOLD, WIDE), BF16),
            pltpu.VMEM((2, SLOTS, WIDE), BF16),
            pltpu.VMEM((2, 3, SLOTS, WIDE), BF16),
            pltpu.VMEM((2, REP, SLOTS, WIDE), BF16),
            pltpu.VMEM((FEAT, REP * SLOTS), BF16),
            pltpu.VMEM((8, CHUNK, 1), jnp.int32),
            pltpu.VMEM((REP, 2, SLOTS, WIDE), BF16),
            pltpu.VMEM((3, 2, SLOTS, WIDE), BF16),
            pltpu.VMEM((2, 4, CHUNK, SPAN), F32),
            pltpu.VMEM((2, 4, CHUNK, SPAN), F32),
            pltpu.VMEM((2, 4, CHUNK, SPAN), F32),
            pltpu.VMEM((2, 2, HALF, SPAN), F32),
            pltpu.VMEM((2, 2, HALF, SPAN), F32),
            pltpu.VMEM((2, 2, HALF, SPAN), F32),
            pltpu.VMEM((2, 2, HALF, SPAN), F32),
            pltpu.VMEM((CHUNK, COLS), F32),
            pltpu.VMEM((SEQ, 1, 128), F32),
            pltpu.VMEM((REP, 1, 128), F32),
            pltpu.VMEM((2 * REP, 2, 128), F32),
            pltpu.VMEM((2 * REP, CHUNK, COLS), BF16),
            pltpu.VMEM((2 * REP, CHUNK, COLS), BF16),
            pltpu.VMEM((2, 2 * REP, CHUNK, WIDE), F32),
            pltpu.VMEM((2, 2 * REP, CHUNK, WIDE), BF16),
            pltpu.VMEM((2, 3, 2, CHUNK, WIDE), BF16),
            pltpu.VMEM((2, SLOTS, WIDE), BF16),
            pltpu.VMEM((2, 3, SLOTS, WIDE), BF16),
            pltpu.VMEM((2, 4, FOLD, WIDE), BF16),
            pltpu.VMEM((2, 3, FOLD, WIDE), BF16),
            pltpu.VMEM((FEAT, COLS), BF16),
            pltpu.SemaphoreType.DMA((MESSAGES,)),
            pltpu.SemaphoreType.DMA((MESSAGES,)),
            pltpu.SemaphoreType.DMA((6,)),
            pltpu.SemaphoreType.DMA((5,)),
        ],
        compiler_params=pltpu.CompilerParams(
            collective_id=0, has_side_effects=True, vmem_limit_bytes=limit
        ),
        cost_estimate=pl.CostEstimate(
            flops=6 * 256 * FEAT * COLS, bytes_accessed=4 * FEAT * COLS, transcendentals=64 * COLS
        ),
    )(counts, seq_cotangent, positions, targets, hidden, head_weight)
    return pl.pallas_call(
        hand_over,
        out_shape=shapes,
        in_specs=[hbm] * 3,
        out_specs=(hbm,) * 3,
        scratch_shapes=[
            pltpu.VMEM((FEAT, COLS), BF16),
            pltpu.VMEM((1, TOK, FEAT), BF16),
            pltpu.SMEM((REP,), F32),
            pltpu.SemaphoreType.DMA((6,)),
            pltpu.SemaphoreType.DMA((6,)),
        ],
        compiler_params=pltpu.CompilerParams(vmem_limit_bytes=limit),
    )(*results)


def solution(mesh):
    return jax.shard_map(
        shards,
        mesh=mesh,
        in_specs=(P("rep", "seq", "vocab"), P("vocab", ("seq", "rep")), P(), P(), P(), P()),
        out_specs=(P("vocab", ("seq", "rep")), P("rep", "seq", "vocab"), P()),
        check_vma=False,
    )
```
